1024 devices in a mesh: gx: 4 (over x), gy: 8 (over y, core), gz: 32 (over z).
Axes of the slice: x: 4, y: 4, z: 32, core: 2. Of those that a mesh axis runs over, the one named last changes fastest.
Arguments:
- right_side: float32 [3, 16, 64, 4096], P(None, 'gx', 'gy', 'gz'), may hold values from -8 to 8
- block_diag: float32 [3, 16, 64, 4096], P(None, 'gx', 'gy', 'gz'), may hold values from 2 to 4
- block_off: float32 [3, 16, 64, 4096], P(None, 'gx', 'gy', 'gz'), may hold values from -0.6 to 0.6
- mobility: float32 [3, 16, 64, 4096], P(None, 'gx', 'gy', 'gz'), may hold values from 0.1 to 10
- perf_cell: int32 [4, 8, 16384], P('gx', 'gy', 'gz'), may hold values from 0 to 4095
- perf_well: int32 [4, 8, 16384], P('gx', 'gy', 'gz'), may hold values from 0 to 639
- perf_factor: float32 [4, 8, 16384], P('gx', 'gy', 'gz'), may hold values from 0.5 to 8
Outputs:
- solution_field: float32 [3, 16, 64, 4096], P(None, 'gx', 'gy', 'gz')
- residual: float32 [3, 16, 64, 4096], P(None, 'gx', 'gy', 'gz')
The draws below stay inside these ranges and needn't reach their ends.
All inputs are finite; a program needn't handle non-finite values.
Results may differ from the reference program's by a relative error of at most 0.00012.
Values sent between devices are 32-bit elements; how exact they have to be, the bound alone decides.
No kernel may reach another device: no remote copies, remote signals or barrier semaphores. Data moves between devices by JAX's collectives and lax.ppermute only.
A program may use at most 32 MiB of HBM per device.

```python
import math
import jax
import jax.numpy as jnp
import numpy as np

CX = 4
CY = 8
CZ = 128
P_DEV = 512
W_COL = 640
ITERS = 3
NX = 16
NY = 64
NZ = 4096
PERFS = 16384
N_GX = 4
N_GY = 8
N_GZ = 32


def set_ends(array, rng, least, largest):
    longest = array.shape.index(max(array.shape))
    spots = []
    for shift in (0, 1):
        where = [jax.random.randint(jax.random.fold_in(rng, axis), (), 0, length) for axis, length in enumerate(array.shape)]
        where[longest] = (where[longest] + shift) % array.shape[longest]
        spots.append(tuple(where))
    return array.at[spots[0]].set(least).at[spots[1]].set(largest)


def shard_levels(own_key, shape, split, least, largest):
    factor_of = 1.0
    for position, shards_of in split:
        steps = jax.random.uniform(jax.random.fold_in(jax.random.fold_in(own_key, 6), position), (shards_of,), jnp.float32, least / len(split), largest / len(split))
        factor_of = factor_of * jnp.repeat(jnp.exp(steps), shape[position] // shards_of).reshape((-1,) + (1,) * (len(shape) - 1 - position))
    return factor_of


def rank_table(count, slope):
    weights = [(1 << 20) // math.isqrt(rank ** slope) + 1 for rank in range(1, count + 1)]
    width = 1 + sum(weights) // (1 << 30)
    return np.cumsum(np.array([max(1, weight // width) for weight in weights]))


def skewed_ids(rng, shape, amount, slope):
    grid = rank_table(amount, slope)
    ticket = jax.random.randint(jax.random.fold_in(rng, 1), shape, 0, int(grid[amount - 1]))
    standing = jnp.searchsorted(jnp.asarray(grid, jnp.int32), ticket, side="right")
    return jax.random.permutation(jax.random.fold_in(rng, 2), amount)[standing].astype(jnp.int32)


def bell_draw(rng, dims, width, limit, cuts=(), kind=jnp.bfloat16):
    factor_of = shard_levels(rng, dims, cuts, -0.22, 0.18) if cuts else 1.0
    values = jax.random.normal(rng, dims, jnp.float32) * width * factor_of
    return jnp.minimum(jnp.maximum(values, -limit), limit).astype(kind)


def setup_inputs(seed: int = 0) -> dict:
    arg_keys = jax.random.split(jax.random.key(seed), 8)
    right_side = bell_draw(arg_keys[0], (3, NX, NY, NZ), 1.0, 8.0, ((1, 4), (2, 8), (3, 32)), jnp.float32)
    block_diag = jnp.clip(2.0 + 2.0 * jax.random.uniform(arg_keys[1], (3, NX, NY, NZ), jnp.float32) ** shard_levels(arg_keys[1], (3, NX, NY, NZ), ((1, 4), (2, 8), (3, 32)), -0.2, 0.2), 2.0, 4.0)
    block_off = jnp.clip(jax.random.uniform(arg_keys[2], (3, NX, NY, NZ), jnp.float32, -0.6, 0.6) * shard_levels(arg_keys[2], (3, NX, NY, NZ), ((1, 4), (2, 8), (3, 32)), -0.4, 0.0), -0.6, 0.6)
    mobility = jnp.clip(jnp.exp(math.log(10.0) - 4.6051702 * jax.random.uniform(arg_keys[3], (3, NX, NY, NZ), jnp.float32) ** shard_levels(arg_keys[3], (3, NX, NY, NZ), ((1, 4), (2, 8), (3, 32)), -0.2, 0.2)), 0.1, 10.0)
    perf_cell = set_ends(jax.random.randint(arg_keys[4], (N_GX, N_GY, PERFS), 0, CX * CY * CZ), jax.random.fold_in(arg_keys[4], 1), 0, (CX * CY * CZ) - 1).astype(jnp.int32)
    perf_well = set_ends(skewed_ids(arg_keys[5], (N_GX, N_GY, PERFS), W_COL, 2), jax.random.fold_in(arg_keys[5], 3), 0, W_COL - 1).astype(jnp.int32)
    perf_factor = jnp.clip(jnp.exp(math.log(8.0) - 2.7725887 * jax.random.uniform(arg_keys[6], (N_GX, N_GY, PERFS), jnp.float32) ** shard_levels(arg_keys[6], (N_GX, N_GY, PERFS), ((0, 4), (1, 8), (2, 32)), -0.2, 0.2)), 0.5, 8.0)
    return dict(right_side=right_side, block_diag=block_diag, block_off=block_off, mobility=mobility, perf_cell=perf_cell, perf_well=perf_well, perf_factor=perf_factor)


def to_blocks(field):
    shaped = field.reshape(3, N_GX, CX, N_GY, CY, N_GZ, CZ)
    return shaped.transpose(1, 3, 5, 0, 2, 4, 6).reshape(N_GX, N_GY, N_GZ, 3, CX * CY * CZ)


def from_blocks(blocks):
    shaped = blocks.reshape(N_GX, N_GY, N_GZ, 3, CX, CY, CZ)
    return shaped.transpose(3, 0, 4, 1, 5, 2, 6).reshape(3, CX * N_GX, CY * N_GY, CZ * N_GZ)


def side_views(padded):
    return [padded[:, 2:, 1:-1, 1:-1], padded[:, :-2, 1:-1, 1:-1],
            padded[:, 1:-1, 2:, 1:-1], padded[:, 1:-1, :-2, 1:-1],
            padded[:, 1:-1, 1:-1, 2:], padded[:, 1:-1, 1:-1, :-2]]


def well_term(field, perf_cell, perf_well, perf_factor):
    cells = CX * CY * CZ
    blocks = to_blocks(field)
    cell_index = perf_cell.reshape(N_GX, N_GY, N_GZ, P_DEV)
    wells = perf_well.reshape(N_GX, N_GY, N_GZ, P_DEV)
    factor = perf_factor.reshape(N_GX, N_GY, N_GZ, P_DEV)
    values = jnp.take_along_axis(blocks, cell_index[:, :, :, None, :], axis=4)
    values = values.transpose(0, 1, 2, 4, 3).reshape(-1, 3)
    column = (jnp.arange(N_GX)[:, None] * N_GY + jnp.arange(N_GY)[None, :]).astype(jnp.int32)
    ids = (column[:, :, None, None] * W_COL + wells).reshape(-1).astype(jnp.int32)
    flat_factor = factor.reshape(-1)
    segments = N_GX * N_GY * W_COL
    num = jax.ops.segment_sum(flat_factor[:, None] * values, ids, num_segments=segments)
    den = jax.ops.segment_sum(flat_factor, ids, num_segments=segments)
    mean = num / (1.0 + den)[:, None]
    delta = flat_factor[:, None] * (values - mean[ids])
    device = ((jnp.arange(N_GX)[:, None, None] * N_GY + jnp.arange(N_GY)[None, :, None]) * N_GZ
              + jnp.arange(N_GZ)[None, None, :]).astype(jnp.int32)
    target = (device[:, :, :, None] * cells + cell_index).reshape(-1).astype(jnp.int32)
    total = jnp.zeros((N_GX * N_GY * N_GZ * cells, 3), jnp.float32).at[target].add(delta)
    total = total.reshape(N_GX, N_GY, N_GZ, cells, 3).transpose(0, 1, 2, 4, 3)
    return from_blocks(total)


def operate(field, block_diag, block_off, mobility, perf_cell, perf_well, perf_factor):
    widths = ((0, 0), (1, 1), (1, 1), (1, 1))
    padded = jnp.pad(field, widths)
    padded_mob = jnp.pad(mobility, widths)
    flow = jnp.zeros_like(field)
    for near_field, near_mob in zip(side_views(padded), side_views(padded_mob)):
        cond = 2.0 * mobility * near_mob / (mobility + near_mob)
        flow = flow + cond * (field - near_field)
    first = block_diag[0] * field[0] + block_off[0] * field[1] + block_off[1] * field[2]
    second = block_off[0] * field[0] + block_diag[1] * field[1] + block_off[2] * field[2]
    third = block_off[1] * field[0] + block_off[2] * field[1] + block_diag[2] * field[2]
    local = jnp.stack([first, second, third])
    return local + flow + well_term(field, perf_cell, perf_well, perf_factor)


def reference(right_side, block_diag, block_off, mobility, perf_cell, perf_well, perf_factor):
    solution_field = jnp.zeros_like(right_side)
    residual = right_side
    direction = right_side
    norm_now = jnp.sum(residual * residual)
    for index in range(ITERS):
        image = operate(direction, block_diag, block_off, mobility, perf_cell, perf_well, perf_factor)
        alpha = norm_now / jnp.sum(direction * image)
        solution_field = solution_field + alpha * direction
        residual = residual - alpha * image
        norm_next = jnp.sum(residual * residual)
        direction = residual + (norm_next / norm_now) * direction
        norm_now = norm_next
    return solution_field, residual
```

```python
import jax
import jax.numpy as jnp
from jax import lax
from jax.experimental import pallas as pl
from jax.experimental.pallas import tpu as pltpu
from jax.sharding import PartitionSpec as P

W_COL = 640
WELL_ROWS = W_COL // 128
SHIFT = 8.0
F32 = jnp.float32
BF16 = jnp.bfloat16


def split3(a):
    first = a.astype(BF16)
    rest = a - first.astype(F32)
    second = rest.astype(BF16)
    third = (rest - second.astype(F32)).astype(BF16)
    return [first, second, third]


def sum3(a, rows):
    return a[:rows] + a[rows : 2 * rows] + a[2 * rows : 3 * rows]


def one_hot(index, rows):
    ids = lax.broadcasted_iota(jnp.int32, (rows, index.shape[1]), 0)
    return ids == index


def cell_masks(cell):
    row = one_hot(lax.shift_right_logical(cell, 7), 32).astype(F32)
    lane = one_hot(lax.bitwise_and(cell, 127), 128).astype(F32).astype(BF16)
    return row, lane


def well_mask(well):
    return one_hot(well, W_COL).astype(F32).astype(BF16)


def gather_cells(fields, row, lane):
    parts = [part for field in fields for part in split3(field)]
    picked = jnp.dot(jnp.concatenate(parts, 0), lane, preferred_element_type=F32)
    out = []
    for u in range(len(fields)):
        block = sum3(picked[96 * u : 96 * (u + 1)], 32)
        out.append(jnp.sum(block * row, axis=0, keepdims=True))
    return out


def scatter_cells(values, row, lane):
    parts = [part for value in values for part in split3(row * value)]
    placed = lax.dot_general(
        jnp.concatenate(parts, 0), lane, (((1,), (1,)), ((), ())), preferred_element_type=F32
    )
    return [sum3(placed[96 * u : 96 * (u + 1)], 32) for u in range(len(values))]


def scatter_wells(values, wells):
    count = len(values)
    stacked = jnp.concatenate(values + [jnp.zeros_like(values[0])] * (8 - count), 0)
    sums = lax.dot_general(
        jnp.concatenate(split3(stacked), 0), wells, (((1,), (1,)), ((), ())),
        preferred_element_type=F32,
    )
    sums = sum3(sums, 8)
    return [sums[u : u + 1] for u in range(count)]


def gather_wells(rows, wells):
    count = len(rows)
    stacked = jnp.concatenate(rows + [jnp.zeros_like(rows[0])] * (8 - count), 0)
    picked = sum3(jnp.dot(jnp.concatenate(split3(stacked), 0), wells, preferred_element_type=F32), 8)
    return [picked[u : u + 1] for u in range(count)]


def put_well_rows(ref, rows):
    for u, row in enumerate(rows):
        for j in range(WELL_ROWS):
            ref[u * WELL_ROWS + j : u * WELL_ROWS + j + 1, :] = row[:, 128 * j : 128 * (j + 1)]


def get_well_rows(table, count):
    out = []
    for u in range(count):
        pieces = [table[u * WELL_ROWS + j : u * WELL_ROWS + j + 1] for j in range(WELL_ROWS)]
        out.append(jnp.concatenate(pieces, 1))
    return out


def lanes():
    return lax.broadcasted_iota(jnp.int32, (8, 128), 1)


def put_faces(refs, fields):
    gx_high, gx_low, gy_high, gy_low, gz_both = refs
    lane = lanes()
    both = jnp.zeros((8, 128), F32)
    for k, field in enumerate(fields):
        for u in range(3):
            gx_high[3 * k + u] = field[u, 24:32]
            gx_low[3 * k + u] = field[u, 0:8]
            for x in range(4):
                at = 12 * k + 4 * u + x
                gy_high[at : at + 1] = field[u, 8 * x + 7 : 8 * x + 8]
                gy_low[at : at + 1] = field[u, 8 * x : 8 * x + 1]
                value = field[u, 8 * x : 8 * x + 8]
                at = 32 * k + 4 * u + x
                both = jnp.where(lane == at, pltpu.roll(value, (at + 1) % 128, 1), both)
                both = jnp.where(lane == at + 16, pltpu.roll(value, at + 16, 1), both)
    gz_both[...] = both


def low_views(field, k, u, x, halo, lane, sub):
    gx_low, gy_low, gz_low = halo
    value = field[u, 8 * x : 8 * x + 8]
    view_x = field[u, 8 * x - 8 : 8 * x] if x else gx_low[3 * k + u]
    at = 12 * k + 4 * u + x
    edge = jnp.broadcast_to(gy_low[at : at + 1], (8, 128))
    view_y = jnp.where(sub == 0, edge, pltpu.roll(value, 1, 0))
    at = 32 * k + 4 * u + x
    edge = pltpu.roll(gz_low[...], (128 - at) % 128, 1)
    view_z = jnp.where(lane == 0, edge, pltpu.roll(value, 1, 1))
    return [view_x, view_y, view_z]


def high_views(field, k, u, x, halo, lane, sub):
    gx_high, gy_high, gz_high = halo
    value = field[u, 8 * x : 8 * x + 8]
    view_x = field[u, 8 * x + 8 : 8 * x + 16] if x < 3 else gx_high[3 * k + u]
    at = 12 * k + 4 * u + x
    edge = jnp.broadcast_to(gy_high[at : at + 1], (8, 128))
    view_y = jnp.where(sub == 7, edge, pltpu.roll(value, 7, 0))
    at = 32 * k + 4 * u + x + 16
    edge = pltpu.roll(gz_high[...], 127 - at, 1)
    view_z = jnp.where(lane == 127, edge, pltpu.roll(value, 127, 1))
    return [view_x, view_y, view_z]


def block_row(field, diag, off, u, rows):
    pick = ((None, 0, 1), (0, None, 2), (1, 2, None))[u]
    total = (diag[u, rows] - SHIFT) * field[u, rows]
    for t in range(3):
        if pick[t] is not None:
            total = total + off[pick[t], rows] * field[t, rows]
    return total


def first_kernel(right, mobility, cell, well, factor, table, *faces):
    row, lane = cell_masks(cell[0])
    values = gather_cells([right[u] for u in range(3)], row, lane)
    weight = factor[0]
    put_well_rows(table, scatter_wells([weight * v for v in values] + [weight], well_mask(well[0])))
    table[4 * WELL_ROWS : 24] = jnp.zeros((24 - 4 * WELL_ROWS, 128), F32)
    put_faces(faces, [right, mobility])


def first_flow_kernel(
    right, mobility, diag, off, xl, yl, zl, xh, yh, zh, flow, cond_low, cond_high
):
    lane, sub = lanes(), lax.broadcasted_iota(jnp.int32, (8, 128), 0)
    for u in range(3):
        for x in range(4):
            rows = slice(8 * x, 8 * x + 8)
            total = block_row(right, diag, off, u, rows)
            value, own = right[u, rows], mobility[u, rows]
            for views, halo, cond in (
                (low_views, (xl, yl, zl), cond_low),
                (high_views, (xh, yh, zh), cond_high),
            ):
                near = views(right, 0, u, x, halo, lane, sub)
                near_mob = views(mobility, 1, u, x, halo, lane, sub)
                for d in range(3):
                    weight = 2.0 * own * near_mob[d] / (own + near_mob[d])
                    cond[d, u, rows] = weight
                    total = total + weight * (value - near[d])
            flow[u, rows] = total


def flow_kernel(field, diag, off, cond_low, cond_high, xl, yl, zl, xh, yh, zh, flow):
    lane, sub = lanes(), lax.broadcasted_iota(jnp.int32, (8, 128), 0)
    for u in range(3):
        for x in range(4):
            rows = slice(8 * x, 8 * x + 8)
            total = block_row(field, diag, off, u, rows)
            value = field[u, rows]
            low = low_views(field, 0, u, x, (xl, yl, zl), lane, sub)
            high = high_views(field, 0, u, x, (xh, yh, zh), lane, sub)
            for d in range(3):
                total = total + cond_low[d, u, rows] * (value - low[d])
                total = total + cond_high[d, u, rows] * (value - high[d])
            flow[u, rows] = total


def advance(means, flow, field, extra, weight, row, lane, wells):
    picked = gather_wells(means, wells)
    pulled = scatter_cells([weight * m for m in picked], row, lane)
    return [flow[u] + extra * field[u] - pulled[u] for u in range(3)]


def second_kernel(slots, flow, right, cell, well, factor, field, table, inverse, extra, *faces):
    total = jnp.sum(slots[...], axis=0)
    scale = 1.0 / (1.0 + total[3 * WELL_ROWS : 4 * WELL_ROWS])
    inverse[...] = jnp.zeros((8, 128), F32)
    inverse[0:WELL_ROWS] = scale
    rows = get_well_rows(total[: 3 * WELL_ROWS], 3)
    scale_row = get_well_rows(scale, 1)[0]
    row, lane = cell_masks(cell[0])
    wells = well_mask(well[0])
    weight = factor[0]
    own = scatter_cells([weight], row, lane)[0]
    extra[...] = own
    fresh = advance([r * scale_row for r in rows], flow, right, own, weight, row, lane, wells)
    for u in range(3):
        field[u] = fresh[u]
    values = gather_cells(fresh, row, lane)
    put_well_rows(table, scatter_wells([weight * v for v in values], wells))
    table[15:16] = jnp.zeros((1, 128), F32)
    put_faces(faces, [field])


def third_kernel(slots, flow, before, extra, inverse, cell, well, factor, field, table, *faces):
    total = jnp.sum(slots[...], axis=0)
    scale_row = get_well_rows(inverse[...], 1)[0]
    rows = get_well_rows(total, 3)
    row, lane = cell_masks(cell[0])
    wells = well_mask(well[0])
    weight = factor[0]
    fresh = advance([r * scale_row for r in rows], flow, before, extra[...], weight, row, lane, wells)
    for u in range(3):
        field[u] = fresh[u]
    values = gather_cells(fresh, row, lane)
    put_well_rows(table, scatter_wells([weight * v for v in values], wells))
    table[15:16] = jnp.zeros((1, 128), F32)
    put_faces(faces, [field])


def tree(terms):
    while len(terms) > 1:
        pairs = [a + b for a, b in zip(terms[::2], terms[1::2])]
        terms = pairs + ([terms[-1]] if len(terms) % 2 else [])
    return terms[0]


def moment_kernel(wells_table, w0, w1, w2, extra, diag, off, cond_low, xl, yl, zl, table):
    lane, sub = lanes(), lax.broadcasted_iota(jnp.int32, (8, 128), 0)
    sums = [[] for _ in range(6)]
    for u in range(3):
        for x in range(4):
            rows = slice(8 * x, 8 * x + 8)
            a, b, c = w0[u, rows], w1[u, rows], w2[u, rows]
            for k, (p, q) in enumerate(((a, a), (a, b), (b, b), (b, c), (c, c))):
                sums[k].append(p * q)
            energy = c * (block_row(w2, diag, off, u, rows) + extra[rows] * c)
            for d, near in enumerate(low_views(w2, 0, u, x, (xl, yl, zl), lane, sub)):
                energy = energy + cond_low[d, u, rows] * (c - near) * (c - near)
            sums[5].append(energy)
    line = jnp.zeros((1, 128), F32)
    first_lane = lane[0:1]
    for k in range(6):
        both = jnp.sum(tree(sums[k]), axis=0, keepdims=True)
        line = jnp.where(first_lane == k, jnp.sum(both, axis=1, keepdims=True), line)
    table[...] = wells_table[...]
    table[15:16] = line


def scalar_kernel(slots, inverse, moments):
    total = jnp.sum(slots[...], axis=0)
    pull = jnp.zeros((WELL_ROWS, 128), F32)
    scale = inverse[0:WELL_ROWS]
    for u in range(3):
        part = total[u * WELL_ROWS : (u + 1) * WELL_ROWS]
        pull = pull + part * part * scale
    pull = jnp.sum(jnp.sum(pull, axis=0, keepdims=True), axis=1, keepdims=True)
    line = total[15:16]
    lane = lanes()[0:1]
    out = []
    for k in range(6):
        value = jnp.sum(jnp.where(lane == k, line, 0.0), axis=1, keepdims=True)
        if k == 5:
            value = value - pull
        moments[k : k + 1] = jnp.broadcast_to(value, (1, 128))
    moments[6:8] = jnp.zeros((2, 128), F32)


def last_vector_kernel(slots, flow, before, extra, inverse, cell, well, factor, field):
    total = jnp.sum(slots[...], axis=0)
    scale_row = get_well_rows(inverse[...], 1)[0]
    rows = get_well_rows(total, 3)
    row, lane = cell_masks(cell[0])
    fresh = advance(
        [r * scale_row for r in rows], flow, before, extra[...], factor[0], row, lane,
        well_mask(well[0]),
    )
    for u in range(3):
        field[u] = fresh[u]


def plus(a, b, scale):
    size = max(len(a), len(b))
    out = []
    for k in range(size):
        p = a[k] if k < len(a) else None
        q = scale * b[k] if k < len(b) else None
        out.append(q if p is None else p if q is None else p + q)
    return out


def image_of(a):
    raised = [None] + list(a)
    return [
        SHIFT * a[0] if k == 0 else raised[k] + SHIFT * a[k] if k < len(a) else raised[k]
        for k in range(len(a) + 1)
    ]


def inner(a, b, moment):
    by_degree = {}
    for i, p in enumerate(a):
        for j, q in enumerate(b):
            by_degree[i + j] = by_degree.get(i + j, 0.0) + p * q
    return tree([by_degree[k] * moment[k] for k in sorted(by_degree)])


def combine_kernel(slots, w0, w1, w2, w3, solved, rest):
    terms = [slots[k] for k in range(slots.shape[0])]
    total = tree(terms)
    moment = [total[k : k + 1] for k in range(6)]
    one = jnp.ones((1, 128), F32)
    residual, direction, solution_field = [one], [one], []
    norm = moment[0]
    for step in range(3):
        image = image_of(direction)
        alpha = norm / inner(direction, image, moment)
        solution_field = plus(solution_field, direction, alpha)
        residual = plus(residual, image, -alpha)
        if step < 2:
            fresh = inner(residual, residual, moment)
            direction = plus(residual, direction, fresh / norm)
            norm = fresh
    solution_field = [jnp.broadcast_to(c, (8, 128)) for c in solution_field]
    residual = [jnp.broadcast_to(c, (8, 128)) for c in residual]
    for u in range(3):
        for x in range(4):
            rows = slice(8 * x, 8 * x + 8)
            basis = [w0[u, rows], w1[u, rows], w2[u, rows], w3[u, rows]]
            solved[u, rows] = tree([c * w for c, w in zip(solution_field, basis)])
            rest[u, rows] = tree([c * w for c, w in zip(residual, basis)])


def call(kernel, shapes, *args):
    return pl.pallas_call(
        kernel,
        out_shape=[jax.ShapeDtypeStruct(shape, F32) for shape in shapes],
        in_specs=[pl.BlockSpec(memory_space=pltpu.VMEM)] * len(args),
        out_specs=[pl.BlockSpec(memory_space=pltpu.VMEM)] * len(shapes),
        compiler_params=pltpu.CompilerParams(vmem_limit_bytes=32 * 1024 * 1024),
    )(*args)


NEAR = 4


def near_sum(table):
    count = lax.axis_size("gz")
    groups = [[NEAR * g + k for k in range(NEAR)] for g in range(count // NEAR)]
    sent = jnp.broadcast_to(table[None], (NEAR,) + table.shape)
    return jnp.sum(lax.all_to_all(sent, "gz", 0, 0, axis_index_groups=groups), axis=0)


def far_slots(table):
    count = lax.axis_size("gz")
    groups = [[g + NEAR * k for k in range(count // NEAR)] for g in range(NEAR)]
    sent = jnp.broadcast_to(table[None], (count // NEAR,) + table.shape)
    return lax.all_to_all(sent, "gz", 0, 0, axis_index_groups=groups)


def forward(piece, axis):
    count = lax.axis_size(axis)
    return lax.ppermute(piece, axis, [(i, i + 1) for i in range(count - 1)])


def backward(piece, axis):
    count = lax.axis_size(axis)
    return lax.ppermute(piece, axis, [(i + 1, i) for i in range(count - 1)])


def low_halos(faces):
    gx_high, _, gy_high, _, gz_both = faces
    return [forward(gx_high, "gx"), forward(gy_high, "gy"), forward(gz_both, "gz")]


def high_halos(faces):
    _, gx_low, _, gy_low, gz_both = faces
    return [backward(gx_low, "gx"), backward(gy_low, "gy"), backward(gz_both, "gz")]


def after(first, *later):
    return lax.optimization_barrier((first, *later))


def face_shapes(fields):
    return [(3 * fields, 8, 128)] * 2 + [(12 * fields, 128)] * 2 + [(8, 128)]


def body(right_side, block_diag, block_off, mobility, perf_cell, perf_well, perf_factor):
    block = (3, 32, 128)
    right, diag, off, mob = (
        a.reshape(block) for a in (right_side, block_diag, block_off, mobility)
    )
    perfs = (perf_cell, perf_well, perf_factor)

    table, *faces = call(first_kernel, [(24, 128)] + face_shapes(2), right, mob, *perfs)
    table, *faces = after(near_sum(table), *faces)
    slots = far_slots(table)
    flow, cond_low, cond_high = call(
        first_flow_kernel, [block, (3,) + block, (3,) + block],
        right, mob, diag, off, *low_halos(faces), *high_halos(faces),
    )

    w1, table, inverse, extra, *faces = call(
        second_kernel, [block, (16, 128), (8, 128), (32, 128)] + face_shapes(1),
        slots, flow, right, *perfs,
    )
    table, *faces = after(near_sum(table), *faces)
    slots = far_slots(table)
    flow = call(
        flow_kernel, [block],
        w1, diag, off, cond_low, cond_high, *low_halos(faces), *high_halos(faces),
    )[0]

    w2, table, *faces = call(
        third_kernel, [block, (16, 128)] + face_shapes(1), slots, flow, w1, extra, inverse, *perfs
    )
    low = low_halos(faces)
    table = call(
        moment_kernel, [(16, 128)], table, right, w1, w2, extra, diag, off, cond_low, *low
    )[0]
    table, *faces = after(near_sum(table), *faces)
    slots = far_slots(table)
    flow = call(
        flow_kernel, [block], w2, diag, off, cond_low, cond_high, *low, *high_halos(faces)
    )[0]

    moments = call(scalar_kernel, [(8, 128)], slots, inverse)[0]
    count = lax.axis_size("gx") * lax.axis_size("gy")
    sent = jnp.broadcast_to(moments[None], (count, 8, 128))
    moment_slots = lax.all_to_all(sent, ("gx", "gy"), 0, 0)
    w3 = call(last_vector_kernel, [block], slots, flow, w2, extra, inverse, *perfs)[0]
    solved, rest = call(combine_kernel, [block, block], moment_slots, right, w1, w2, w3)
    return solved.reshape(right_side.shape), rest.reshape(right_side.shape)


def solution(mesh):
    field = P(None, "gx", "gy", "gz")
    perf = P("gx", "gy", "gz")
    return jax.shard_map(
        body,
        mesh=mesh,
        in_specs=(field, field, field, field, perf, perf, perf),
        out_specs=(field, field),
        check_vma=False,
    )
```

```python
import jax
import jax.numpy as jnp
from jax import lax
from jax.experimental import pallas as pl
from jax.experimental.pallas import tpu as pltpu
from jax.sharding import PartitionSpec as P

W_COL = 640
WELL_ROWS = W_COL // 128
SHIFT = 8.0
F32 = jnp.float32
BF16 = jnp.bfloat16


def split3(a):
    first = a.astype(BF16)
    rest = a - first.astype(F32)
    second = rest.astype(BF16)
    third = (rest - second.astype(F32)).astype(BF16)
    return [first, second, third]


def sum3(a, rows):
    return a[:rows] + a[rows : 2 * rows] + a[2 * rows : 3 * rows]


def one_hot(index, rows):
    ids = lax.broadcasted_iota(jnp.int32, (rows, index.shape[1]), 0)
    return ids == index


def cell_masks(cell):
    row = one_hot(lax.shift_right_logical(cell, 7), 32).astype(F32)
    lane = one_hot(lax.bitwise_and(cell, 127), 128).astype(F32).astype(BF16)
    return row, lane


def well_mask(well):
    return one_hot(well, W_COL).astype(F32).astype(BF16)


def gather_cells(fields, row, lane):
    parts = [part for field in fields for part in split3(field)]
    picked = jnp.dot(jnp.concatenate(parts, 0), lane, preferred_element_type=F32)
    out = []
    for u in range(len(fields)):
        block = sum3(picked[96 * u : 96 * (u + 1)], 32)
        out.append(jnp.sum(block * row, axis=0, keepdims=True))
    return out


def scatter_cells(values, row, lane):
    parts = [part for value in values for part in split3(row * value)]
    placed = lax.dot_general(
        jnp.concatenate(parts, 0), lane, (((1,), (1,)), ((), ())), preferred_element_type=F32
    )
    return [sum3(placed[96 * u : 96 * (u + 1)], 32) for u in range(len(values))]


def scatter_wells(values, wells):
    count = len(values)
    stacked = jnp.concatenate(values + [jnp.zeros_like(values[0])] * (8 - count), 0)
    sums = lax.dot_general(
        jnp.concatenate(split3(stacked), 0), wells, (((1,), (1,)), ((), ())),
        preferred_element_type=F32,
    )
    sums = sum3(sums, 8)
    return [sums[u : u + 1] for u in range(count)]


def gather_wells(rows, wells):
    count = len(rows)
    stacked = jnp.concatenate(rows + [jnp.zeros_like(rows[0])] * (8 - count), 0)
    picked = sum3(jnp.dot(jnp.concatenate(split3(stacked), 0), wells, preferred_element_type=F32), 8)
    return [picked[u : u + 1] for u in range(count)]


def put_well_rows(ref, rows):
    for u, row in enumerate(rows):
        for j in range(WELL_ROWS):
            ref[u * WELL_ROWS + j : u * WELL_ROWS + j + 1, :] = row[:, 128 * j : 128 * (j + 1)]


def get_well_rows(table, count):
    out = []
    for u in range(count):
        pieces = [table[u * WELL_ROWS + j : u * WELL_ROWS + j + 1] for j in range(WELL_ROWS)]
        out.append(jnp.concatenate(pieces, 1))
    return out


def lanes():
    return lax.broadcasted_iota(jnp.int32, (8, 128), 1)


def put_faces(refs, fields):
    gx_high, gx_low, gy_high, gy_low = refs
    for k, field in enumerate(fields):
        for u in range(3):
            gx_high[3 * k + u] = field[u, 24:32]
            gx_low[3 * k + u] = field[u, 0:8]
            for x in range(4):
                at = 12 * k + 4 * u + x
                gy_high[at : at + 1] = field[u, 8 * x + 7 : 8 * x + 8]
                gy_low[at : at + 1] = field[u, 8 * x : 8 * x + 1]


def end_tile(highs, lows):
    lane = lanes()
    tile = jnp.zeros((8, 128), F32)
    for fields, turn in ((highs, 1), (lows, 0)):
        for field, start in fields:
            for u in range(3):
                for x in range(4):
                    at = start + 4 * u + x
                    value = pltpu.roll(field[u, 8 * x : 8 * x + 8], at + turn, 1)
                    tile = jnp.where(lane == at, value, tile)
    return tile


def fold(tile):
    return jnp.where(lanes()[0:4] < 64, tile[0:4], pltpu.roll(tile, 64, 1)[4:8])


def unfold(rows):
    return jnp.concatenate([rows, pltpu.roll(jnp.concatenate([rows, rows], 0), 64, 1)[0:4]], 0)


def low_views(field, k, u, x, halo, sub):
    gx_low, gy_low = halo
    value = field[u, 8 * x : 8 * x + 8]
    view_x = field[u, 8 * x - 8 : 8 * x] if x else gx_low[3 * k + u]
    at = 12 * k + 4 * u + x
    edge = jnp.broadcast_to(gy_low[at : at + 1], (8, 128))
    return [view_x, jnp.where(sub == 0, edge, pltpu.roll(value, 1, 0))]


def high_views(field, k, u, x, halo, sub):
    gx_high, gy_high = halo
    value = field[u, 8 * x : 8 * x + 8]
    view_x = field[u, 8 * x + 8 : 8 * x + 16] if x < 3 else gx_high[3 * k + u]
    at = 12 * k + 4 * u + x
    edge = jnp.broadcast_to(gy_high[at : at + 1], (8, 128))
    return [view_x, jnp.where(sub == 7, edge, pltpu.roll(value, 7, 0))]


def low_along(value, tile, at, lane):
    return jnp.where(lane == 0, pltpu.roll(tile, (128 - at) % 128, 1), pltpu.roll(value, 1, 1))


def high_along(value, tile, at, lane):
    return jnp.where(lane == 127, pltpu.roll(tile, 127 - at, 1), pltpu.roll(value, 127, 1))


def place():
    at = lax.axis_index("gz")
    return lax.div(at, NEAR), lax.rem(at, NEAR)


def near_tiles(tiles):
    _, member = place()
    low, high = tiles[0], tiles[-1]
    for k in range(1, NEAR - 1):
        low = jnp.where(member == k + 1, tiles[k], low)
        high = jnp.where(member == k - 1, tiles[k], high)
    return low, high


def halo_tiles(near, slots, read):
    group, member = place()
    last = slots.shape[0] - 1
    below = jnp.where(group == 0, 0.0, read(slots[jnp.maximum(group - 1, 0)]))
    above = jnp.where(group == last, 0.0, read(slots[jnp.minimum(group + 1, last)]))
    return jnp.where(member == 0, below, near[0]), jnp.where(member == NEAR - 1, above, near[1])


def block_row(field, diag, off, u, rows):
    pick = ((None, 0, 1), (0, None, 2), (1, 2, None))[u]
    total = (diag[u, rows] - SHIFT) * field[u, rows]
    for t in range(3):
        if pick[t] is not None:
            total = total + off[pick[t], rows] * field[t, rows]
    return total


def first_kernel(right_any, mobility_any, cell_any, well_any, factor_any, table, *rest):
    faces, (right, mobility, cell, well, factor, sems) = rest[:4], rest[4:]
    copies = [
        pltpu.make_async_copy(source, target, sems.at[k])
        for k, (source, target) in enumerate(
            (
                (cell_any, cell),
                (right_any, right),
                (factor_any, factor),
                (well_any, well),
                (mobility_any, mobility),
            )
        )
    ]
    for copy in copies:
        copy.start()
    for copy in copies:
        copy.wait()
    row, lane = cell_masks(cell[0])
    values = gather_cells([right[u] for u in range(3)], row, lane)
    weight = factor[0]
    put_well_rows(table, scatter_wells([weight * v for v in values] + [weight], well_mask(well[0])))
    ends = [(right, 0), (mobility, 32)], [(right, 16), (mobility, 48)]
    table[4 * WELL_ROWS : 24] = fold(end_tile(*ends))
    put_faces(faces, [right, mobility])


def first_near_kernel(slots, sent, near):
    rows = 4 * WELL_ROWS
    total = jnp.sum(slots[...], axis=0)
    tiles = [unfold(slots[k, rows:24]) for k in range(NEAR)]
    low, high = near_tiles(tiles)
    near[0], near[1] = low, high
    lane = lanes()
    ends = fold(jnp.where(lax.bitwise_and(lane, 31) < 16, tiles[-1], tiles[0]))
    for k in range(sent.shape[0]):
        sent[k, 0:rows] = total[0:rows]
        sent[k, rows:24] = ends


def near_kernel(slots, sent, near):
    total = jnp.sum(slots[...], axis=0)
    tiles = [slots[k, 16:24] for k in range(NEAR)]
    low, high = near_tiles(tiles)
    near[0], near[1] = low, high
    ends = jnp.where(lanes() < 16, tiles[-1], tiles[0])
    for k in range(sent.shape[0]):
        sent[k, 0:16] = total[0:16]
        sent[k, 16:24] = ends


def face_energy(below, above):
    step = pltpu.roll(above, 112, 1) - below
    return jnp.where(lanes() < 12, pltpu.roll(above, 96, 1) * step * step, 0.0)


def whole_sum(a):
    return jnp.sum(jnp.sum(a, axis=0, keepdims=True), axis=1, keepdims=True)


def last_near_kernel(slots, sent, near):
    total = jnp.sum(slots[...], axis=0)
    tiles = [slots[k, 16:24] for k in range(NEAR)]
    low, high = near_tiles(tiles)
    near[0], near[1] = low, high
    between = whole_sum(tree([face_energy(a, b) for a, b in zip(tiles, tiles[1:])]))
    line = total[15:16] + jnp.where(lanes()[0:1] == 5, between, 0.0)
    ends = jnp.where(lanes() < 16, tiles[-1], tiles[0])
    for k in range(sent.shape[0]):
        sent[k, 0:15] = total[0:15]
        sent[k, 15:16] = line
        sent[k, 16:24] = ends


def first_flow_kernel(right, mobility, diag, off, xl, yl, xh, yh, flow, cond):
    sub = lax.broadcasted_iota(jnp.int32, (8, 128), 0)
    for u in range(3):
        for x in range(4):
            rows = slice(8 * x, 8 * x + 8)
            total = block_row(right, diag, off, u, rows)
            value, own = right[u, rows], mobility[u, rows]
            near = low_views(right, 0, u, x, (xl, yl), sub)
            near += high_views(right, 0, u, x, (xh, yh), sub)
            near_mob = low_views(mobility, 1, u, x, (xl, yl), sub)
            near_mob += high_views(mobility, 1, u, x, (xh, yh), sub)
            for d in range(4):
                weight = 2.0 * own * near_mob[d] / (own + near_mob[d])
                cond[d, u, rows] = weight
                total = total + weight * (value - near[d])
            flow[u, rows] = total


def flow_kernel(field, diag, off, cond, xl, yl, xh, yh, flow):
    sub = lax.broadcasted_iota(jnp.int32, (8, 128), 0)
    for u in range(3):
        for x in range(4):
            rows = slice(8 * x, 8 * x + 8)
            total = block_row(field, diag, off, u, rows)
            value = field[u, rows]
            near = low_views(field, 0, u, x, (xl, yl), sub)
            near += high_views(field, 0, u, x, (xh, yh), sub)
            for d in range(4):
                total = total + cond[d, u, rows] * (value - near[d])
            flow[u, rows] = total


def flow_along(field, flow, cond, low, high):
    lane = lanes()
    out = []
    for u in range(3):
        blocks = []
        for x in range(4):
            rows = slice(8 * x, 8 * x + 8)
            value = field[u, rows]
            step_low = value - low_along(value, low, 4 * u + x, lane)
            step_high = value - high_along(value, high, 16 + 4 * u + x, lane)
            total = flow[u, rows] + cond[0, u, rows] * step_low
            blocks.append(total + cond[1, u, rows] * step_high)
        out.append(jnp.concatenate(blocks, 0))
    return out


def put_cond_along(cond, mobility, low, high):
    lane = lanes()
    for u in range(3):
        for x in range(4):
            rows = slice(8 * x, 8 * x + 8)
            own = mobility[u, rows]
            near = low_along(own, low, 32 + 4 * u + x, lane)
            cond[0, u, rows] = 2.0 * own * near / (own + near)
            near = high_along(own, high, 48 + 4 * u + x, lane)
            cond[1, u, rows] = 2.0 * own * near / (own + near)


def advance(means, flow, field, extra, weight, row, lane, wells):
    picked = gather_wells(means, wells)
    pulled = scatter_cells([weight * m for m in picked], row, lane)
    return [flow[u] + extra * field[u] - pulled[u] for u in range(3)]


def second_kernel(
    slots, near, flow, right, mobility, cell, well, factor,
    field, table, inverse, extra, cond, *faces
):
    total = jnp.sum(slots[...], axis=0)
    low, high = halo_tiles(near, slots, lambda a: unfold(a[4 * WELL_ROWS : 24]))
    put_cond_along(cond, mobility, low, high)
    whole = flow_along(right, flow, cond, low, high)
    scale = 1.0 / (1.0 + total[3 * WELL_ROWS : 4 * WELL_ROWS])
    inverse[...] = jnp.zeros((8, 128), F32)
    inverse[0:WELL_ROWS] = scale
    rows = get_well_rows(total[: 3 * WELL_ROWS], 3)
    scale_row = get_well_rows(scale, 1)[0]
    row, lane = cell_masks(cell[0])
    wells = well_mask(well[0])
    weight = factor[0]
    own = scatter_cells([weight], row, lane)[0]
    extra[...] = own
    fresh = advance([r * scale_row for r in rows], whole, right, own, weight, row, lane, wells)
    for u in range(3):
        field[u] = fresh[u]
    values = gather_cells(fresh, row, lane)
    put_well_rows(table, scatter_wells([weight * v for v in values], wells))
    table[15:16] = jnp.zeros((1, 128), F32)
    table[16:24] = end_tile([(field, 0)], [(field, 16)])
    put_faces(faces, [field])


def third_kernel(
    slots, near, flow, before, extra, inverse, cond, cell, well, factor, field, table, *faces
):
    total = jnp.sum(slots[...], axis=0)
    low, high = halo_tiles(near, slots, lambda a: a[16:24])
    whole = flow_along(before, flow, cond, low, high)
    scale_row = get_well_rows(inverse[...], 1)[0]
    rows = get_well_rows(total, 3)
    row, lane = cell_masks(cell[0])
    wells = well_mask(well[0])
    weight = factor[0]
    fresh = advance([r * scale_row for r in rows], whole, before, extra[...], weight, row, lane, wells)
    for u in range(3):
        field[u] = fresh[u]
    values = gather_cells(fresh, row, lane)
    put_well_rows(table, scatter_wells([weight * v for v in values], wells))
    table[15:16] = jnp.zeros((1, 128), F32)
    table[16:24] = end_tile([(field, 0)], [(field, 16), (cond.at[0], 32)])
    put_faces(faces, [field])


def tree(terms):
    while len(terms) > 1:
        pairs = [a + b for a, b in zip(terms[::2], terms[1::2])]
        terms = pairs + ([terms[-1]] if len(terms) % 2 else [])
    return terms[0]


def moment_kernel(wells_table, w0, w1, w2, extra, diag, off, cond, cond_along, xl, yl, table):
    lane, sub = lanes(), lax.broadcasted_iota(jnp.int32, (8, 128), 0)
    sums = [[] for _ in range(6)]
    for u in range(3):
        for x in range(4):
            rows = slice(8 * x, 8 * x + 8)
            a, b, c = w0[u, rows], w1[u, rows], w2[u, rows]
            for k, (p, q) in enumerate(((a, a), (a, b), (b, b), (b, c), (c, c))):
                sums[k].append(p * q)
            energy = c * (block_row(w2, diag, off, u, rows) + extra[rows] * c)
            for d, near in enumerate(low_views(w2, 0, u, x, (xl, yl), sub)):
                energy = energy + cond[d, u, rows] * (c - near) * (c - near)
            step = jnp.where(lane == 0, 0.0, c - pltpu.roll(c, 1, 1))
            sums[5].append(energy + cond_along[0, u, rows] * step * step)
    line = jnp.zeros((1, 128), F32)
    for k in range(6):
        line = jnp.where(lane[0:1] == k, whole_sum(tree(sums[k])), line)
    table[...] = wells_table[...]
    table[15:16] = line


def scalar_kernel(slots, inverse, moments):
    total = jnp.sum(slots[...], axis=0)
    pull = jnp.zeros((WELL_ROWS, 128), F32)
    scale = inverse[0:WELL_ROWS]
    for u in range(3):
        part = total[u * WELL_ROWS : (u + 1) * WELL_ROWS]
        pull = pull + part * part * scale
    tiles = [slots[k, 16:24] for k in range(slots.shape[0])]
    between = tree([face_energy(a, b) for a, b in zip(tiles, tiles[1:])])
    line = total[15:16]
    lane = lanes()[0:1]
    for k in range(6):
        value = jnp.sum(jnp.where(lane == k, line, 0.0), axis=1, keepdims=True)
        if k == 5:
            value = value + (whole_sum(between) - whole_sum(pull))
        moments[k : k + 1] = jnp.broadcast_to(value, (1, 128))
    moments[6:8] = jnp.zeros((2, 128), F32)


def last_vector_kernel(
    slots, near, flow, before, extra, inverse, cond, cell, well, factor, field
):
    total = jnp.sum(slots[...], axis=0)
    low, high = halo_tiles(near, slots, lambda a: a[16:24])
    whole = flow_along(before, flow, cond, low, high)
    scale_row = get_well_rows(inverse[...], 1)[0]
    rows = get_well_rows(total, 3)
    row, lane = cell_masks(cell[0])
    fresh = advance(
        [r * scale_row for r in rows], whole, before, extra[...], factor[0], row, lane,
        well_mask(well[0]),
    )
    for u in range(3):
        field[u] = fresh[u]


def plus(a, b, scale):
    size = max(len(a), len(b))
    out = []
    for k in range(size):
        p = a[k] if k < len(a) else None
        q = scale * b[k] if k < len(b) else None
        out.append(q if p is None else p if q is None else p + q)
    return out


def image_of(a):
    raised = [None] + list(a)
    return [
        SHIFT * a[0] if k == 0 else raised[k] + SHIFT * a[k] if k < len(a) else raised[k]
        for k in range(len(a) + 1)
    ]


def inner(a, b, moment):
    by_degree = {}
    for i, p in enumerate(a):
        for j, q in enumerate(b):
            by_degree[i + j] = by_degree.get(i + j, 0.0) + p * q
    return tree([by_degree[k] * moment[k] for k in sorted(by_degree)])


def combine_kernel(slots, w0, w1, w2, w3, solved, rest):
    terms = [slots[k] for k in range(slots.shape[0])]
    total = tree(terms)
    moment = [total[k : k + 1] for k in range(6)]
    one = jnp.ones((1, 128), F32)
    residual, direction, solution_field = [one], [one], []
    norm = moment[0]
    for step in range(3):
        image = image_of(direction)
        alpha = norm / inner(direction, image, moment)
        solution_field = plus(solution_field, direction, alpha)
        residual = plus(residual, image, -alpha)
        if step < 2:
            fresh = inner(residual, residual, moment)
            direction = plus(residual, direction, fresh / norm)
            norm = fresh
    solution_field = [jnp.broadcast_to(c, (8, 128)) for c in solution_field]
    residual = [jnp.broadcast_to(c, (8, 128)) for c in residual]
    for u in range(3):
        for x in range(4):
            rows = slice(8 * x, 8 * x + 8)
            basis = [w0[u, rows], w1[u, rows], w2[u, rows], w3[u, rows]]
            solved[u, rows] = tree([c * w for c, w in zip(solution_field, basis)])
            rest[u, rows] = tree([c * w for c, w in zip(residual, basis)])


def call(kernel, shapes, *args, space=pltpu.VMEM, scratch=(), mib=32):
    return pl.pallas_call(
        kernel,
        out_shape=[jax.ShapeDtypeStruct(shape, F32) for shape in shapes],
        in_specs=[pl.BlockSpec(memory_space=space)] * len(args),
        out_specs=[pl.BlockSpec(memory_space=pltpu.VMEM)] * len(shapes),
        scratch_shapes=list(scratch),
        compiler_params=pltpu.CompilerParams(vmem_limit_bytes=mib * 1024 * 1024),
    )(*args)


NEAR = 4


def near_slots(table):
    count = lax.axis_size("gz")
    groups = [[NEAR * g + k for k in range(NEAR)] for g in range(count // NEAR)]
    sent = jnp.broadcast_to(table[None], (NEAR,) + table.shape)
    return lax.all_to_all(sent, "gz", 0, 0, axis_index_groups=groups)


def far_slots(sent):
    count = lax.axis_size("gz")
    groups = [[g + NEAR * k for k in range(count // NEAR)] for g in range(NEAR)]
    return lax.all_to_all(sent, "gz", 0, 0, axis_index_groups=groups)


def forward(piece, axis):
    count = lax.axis_size(axis)
    return lax.ppermute(piece, axis, [(i, i + 1) for i in range(count - 1)])


def backward(piece, axis):
    count = lax.axis_size(axis)
    return lax.ppermute(piece, axis, [(i + 1, i) for i in range(count - 1)])


def low_halos(faces):
    return [forward(faces[0], "gx"), forward(faces[2], "gy")]


def high_halos(faces):
    return [backward(faces[1], "gx"), backward(faces[3], "gy")]


def after(first, *later):
    return lax.optimization_barrier((first, *later))


def face_shapes(fields):
    return [(3 * fields, 8, 128)] * 2 + [(12 * fields, 128)] * 2


def body(right_side, block_diag, block_off, mobility, perf_cell, perf_well, perf_factor):
    block = (3, 32, 128)
    right, diag, off, mob = (
        a.reshape(block) for a in (right_side, block_diag, block_off, mobility)
    )
    perfs = (perf_cell, perf_well, perf_factor)
    sent_shapes = [(lax.axis_size("gz") // NEAR, 24, 128), (2, 8, 128)]

    table, *faces = call(
        first_kernel, [(24, 128)] + face_shapes(2), right, mob, *perfs,
        space=pltpu.HBM, mib=60,
        scratch=[pltpu.VMEM(block, F32)] * 2
        + [pltpu.VMEM(a.shape, a.dtype) for a in perfs]
        + [pltpu.SemaphoreType.DMA((5,))],
    )
    sent, near = call(first_near_kernel, sent_shapes, near_slots(table))
    sent, *faces = after(sent, *faces)
    slots = far_slots(sent)
    flow, cond = call(
        first_flow_kernel, [block, (4,) + block],
        right, mob, diag, off, *low_halos(faces), *high_halos(faces),
    )
    w1, table, inverse, extra, cond_along, *faces = call(
        second_kernel,
        [block, (24, 128), (8, 128), (32, 128), (2,) + block] + face_shapes(1),
        slots, near, flow, right, mob, *perfs,
    )

    sent, near = call(near_kernel, sent_shapes, near_slots(table))
    sent, *faces = after(sent, *faces)
    slots = far_slots(sent)
    flow = call(
        flow_kernel, [block], w1, diag, off, cond, *low_halos(faces), *high_halos(faces)
    )[0]
    w2, table, *faces = call(
        third_kernel, [block, (24, 128)] + face_shapes(1),
        slots, near, flow, w1, extra, inverse, cond_along, *perfs,
    )

    low = low_halos(faces)
    table = call(
        moment_kernel, [(24, 128)],
        table, right, w1, w2, extra, diag, off, cond, cond_along, *low,
    )[0]
    sent, near = call(last_near_kernel, sent_shapes, near_slots(table))
    sent, *faces = after(sent, *faces)
    slots, *high = after(far_slots(sent), *high_halos(faces))
    flow = call(flow_kernel, [block], w2, diag, off, cond, *low, *high)[0]

    moments = call(scalar_kernel, [(8, 128)], slots, inverse)[0]
    count = lax.axis_size("gx") * lax.axis_size("gy")
    sent = jnp.broadcast_to(moments[None], (count, 8, 128))
    moment_slots = lax.all_to_all(sent, ("gx", "gy"), 0, 0)
    w3 = call(
        last_vector_kernel, [block],
        slots, near, flow, w2, extra, inverse, cond_along, *perfs,
    )[0]
    solved, rest = call(combine_kernel, [block, block], moment_slots, right, w1, w2, w3)
    return solved.reshape(right_side.shape), rest.reshape(right_side.shape)


def solution(mesh):
    field = P(None, "gx", "gy", "gz")
    perf = P("gx", "gy", "gz")
    return jax.shard_map(
        body,
        mesh=mesh,
        in_specs=(field, field, field, field, perf, perf, perf),
        out_specs=(field, field),
        check_vma=False,
    )
```

```python
import jax
import jax.numpy as jnp
from jax import lax
from jax.experimental import pallas as pl
from jax.experimental.pallas import tpu as pltpu
from jax.sharding import PartitionSpec as P

W_COL = 640
WELL_ROWS = W_COL // 128
SHIFT = 8.0
F32 = jnp.float32
BF16 = jnp.bfloat16


def split3(a):
    first = a.astype(BF16)
    rest = a - first.astype(F32)
    second = rest.astype(BF16)
    third = (rest - second.astype(F32)).astype(BF16)
    return [first, second, third]


def sum3(a, rows):
    return a[:rows] + a[rows : 2 * rows] + a[2 * rows : 3 * rows]


def one_hot(index, rows):
    ids = lax.broadcasted_iota(jnp.int32, (rows, index.shape[1]), 0)
    return ids == index


def cell_masks(cell):
    row = one_hot(lax.shift_right_logical(cell, 7), 32).astype(F32)
    lane = one_hot(lax.bitwise_and(cell, 127), 128).astype(F32).astype(BF16)
    return row, lane


def well_mask(well):
    return one_hot(well, W_COL).astype(F32).astype(BF16)


def gather_cells(fields, row, lane):
    parts = [part for field in fields for part in split3(field)]
    picked = jnp.dot(jnp.concatenate(parts, 0), lane, preferred_element_type=F32)
    out = []
    for u in range(len(fields)):
        block = sum3(picked[96 * u : 96 * (u + 1)], 32)
        out.append(jnp.sum(block * row, axis=0, keepdims=True))
    return out


def scatter_cells(values, row, lane):
    parts = [part for value in values for part in split3(row * value)]
    placed = lax.dot_general(
        jnp.concatenate(parts, 0), lane, (((1,), (1,)), ((), ())), preferred_element_type=F32
    )
    return [sum3(placed[96 * u : 96 * (u + 1)], 32) for u in range(len(values))]


def scatter_wells(values, wells):
    count = len(values)
    stacked = jnp.concatenate(values + [jnp.zeros_like(values[0])] * (8 - count), 0)
    sums = lax.dot_general(
        jnp.concatenate(split3(stacked), 0), wells, (((1,), (1,)), ((), ())),
        preferred_element_type=F32,
    )
    sums = sum3(sums, 8)
    return [sums[u : u + 1] for u in range(count)]


def gather_wells(rows, wells):
    count = len(rows)
    stacked = jnp.concatenate(rows + [jnp.zeros_like(rows[0])] * (8 - count), 0)
    picked = sum3(jnp.dot(jnp.concatenate(split3(stacked), 0), wells, preferred_element_type=F32), 8)
    return [picked[u : u + 1] for u in range(count)]


def put_well_rows(ref, rows):
    for u, row in enumerate(rows):
        for j in range(WELL_ROWS):
            ref[u * WELL_ROWS + j : u * WELL_ROWS + j + 1, :] = row[:, 128 * j : 128 * (j + 1)]


def get_well_rows(table, count):
    out = []
    for u in range(count):
        pieces = [table[u * WELL_ROWS + j : u * WELL_ROWS + j + 1] for j in range(WELL_ROWS)]
        out.append(jnp.concatenate(pieces, 1))
    return out


def lanes():
    return lax.broadcasted_iota(jnp.int32, (8, 128), 1)


def put_faces(refs, fields):
    gx_high, gx_low, gy_high, gy_low = refs
    for k, field in enumerate(fields):
        for u in range(3):
            gx_high[3 * k + u] = field[u, 24:32]
            gx_low[3 * k + u] = field[u, 0:8]
            for x in range(4):
                at = 12 * k + 4 * u + x
                gy_high[at : at + 1] = field[u, 8 * x + 7 : 8 * x + 8]
                gy_low[at : at + 1] = field[u, 8 * x : 8 * x + 1]


def end_tile(highs, lows):
    lane = lanes()
    tile = jnp.zeros((8, 128), F32)
    for fields, turn in ((highs, 1), (lows, 0)):
        for field, start in fields:
            for u in range(3):
                for x in range(4):
                    at = start + 4 * u + x
                    value = pltpu.roll(field[u, 8 * x : 8 * x + 8], at + turn, 1)
                    tile = jnp.where(lane == at, value, tile)
    return tile


def fold(tile):
    return jnp.where(lanes()[0:4] < 64, tile[0:4], pltpu.roll(tile, 64, 1)[4:8])


def unfold(rows):
    return jnp.concatenate([rows, pltpu.roll(jnp.concatenate([rows, rows], 0), 64, 1)[0:4]], 0)


def low_views(field, k, u, x, halo, sub):
    gx_low, gy_low = halo
    value = field[u, 8 * x : 8 * x + 8]
    view_x = field[u, 8 * x - 8 : 8 * x] if x else gx_low[3 * k + u]
    at = 12 * k + 4 * u + x
    edge = jnp.broadcast_to(gy_low[at : at + 1], (8, 128))
    return [view_x, jnp.where(sub == 0, edge, pltpu.roll(value, 1, 0))]


def high_views(field, k, u, x, halo, sub):
    gx_high, gy_high = halo
    value = field[u, 8 * x : 8 * x + 8]
    view_x = field[u, 8 * x + 8 : 8 * x + 16] if x < 3 else gx_high[3 * k + u]
    at = 12 * k + 4 * u + x
    edge = jnp.broadcast_to(gy_high[at : at + 1], (8, 128))
    return [view_x, jnp.where(sub == 7, edge, pltpu.roll(value, 7, 0))]


def low_along(value, tile, at, lane):
    return jnp.where(lane == 0, pltpu.roll(tile, (128 - at) % 128, 1), pltpu.roll(value, 1, 1))


def high_along(value, tile, at, lane):
    return jnp.where(lane == 127, pltpu.roll(tile, 127 - at, 1), pltpu.roll(value, 127, 1))


def place():
    at = lax.axis_index("gz")
    return lax.div(at, NEAR), lax.rem(at, NEAR)


def near_tiles(tiles):
    _, member = place()
    low, high = tiles[0], tiles[-1]
    for k in range(1, NEAR - 1):
        low = jnp.where(member == k + 1, tiles[k], low)
        high = jnp.where(member == k - 1, tiles[k], high)
    return low, high


def halo_tiles(near, slots, read):
    group, member = place()
    last = slots.shape[0] - 1
    below = jnp.where(group == 0, 0.0, read(slots[jnp.maximum(group - 1, 0)]))
    above = jnp.where(group == last, 0.0, read(slots[jnp.minimum(group + 1, last)]))
    return jnp.where(member == 0, below, near[0]), jnp.where(member == NEAR - 1, above, near[1])


def block_row(field, diag, off, u, rows):
    pick = ((None, 0, 1), (0, None, 2), (1, 2, None))[u]
    total = (diag[u, rows] - SHIFT) * field[u, rows]
    for t in range(3):
        if pick[t] is not None:
            total = total + off[pick[t], rows] * field[t, rows]
    return total


def first_kernel(right_any, mobility_any, cell_any, well_any, factor_any, table, *rest):
    faces, (right, mobility, cell, well, factor, sems) = rest[:4], rest[4:]
    copies = [
        pltpu.make_async_copy(source, target, sems.at[k])
        for k, (source, target) in enumerate(
            (
                (cell_any, cell),
                (right_any, right),
                (factor_any, factor),
                (well_any, well),
                (mobility_any, mobility),
            )
        )
    ]
    for copy in copies:
        copy.start()
    for copy in copies:
        copy.wait()
    row, lane = cell_masks(cell[0])
    values = gather_cells([right[u] for u in range(3)], row, lane)
    weight = factor[0]
    put_well_rows(table, scatter_wells([weight * v for v in values] + [weight], well_mask(well[0])))
    ends = [(right, 0), (mobility, 32)], [(right, 16), (mobility, 48)]
    table[4 * WELL_ROWS : 24] = fold(end_tile(*ends))
    put_faces(faces, [right, mobility])


def first_near_kernel(slots, sent, near):
    rows = 4 * WELL_ROWS
    total = jnp.sum(slots[...], axis=0)
    tiles = [unfold(slots[k, rows:24]) for k in range(NEAR)]
    low, high = near_tiles(tiles)
    near[0], near[1] = low, high
    lane = lanes()
    ends = fold(jnp.where(lax.bitwise_and(lane, 31) < 16, tiles[-1], tiles[0]))
    for k in range(sent.shape[0]):
        sent[k, 0:rows] = total[0:rows]
        sent[k, rows:24] = ends


def near_kernel(slots, sent, near):
    total = jnp.sum(slots[...], axis=0)
    tiles = [slots[k, 16:24] for k in range(NEAR)]
    low, high = near_tiles(tiles)
    near[0], near[1] = low, high
    ends = jnp.where(lanes() < 16, tiles[-1], tiles[0])
    for k in range(sent.shape[0]):
        sent[k, 0:16] = total[0:16]
        sent[k, 16:24] = ends


def face_energy(below, above):
    step = pltpu.roll(above, 112, 1) - below
    return jnp.where(lanes() < 12, pltpu.roll(above, 96, 1) * step * step, 0.0)


def whole_sum(a):
    return jnp.sum(jnp.sum(a, axis=0, keepdims=True), axis=1, keepdims=True)


def last_near_kernel(slots, sent, near):
    total = jnp.sum(slots[...], axis=0)
    tiles = [slots[k, 16:24] for k in range(NEAR)]
    low, high = near_tiles(tiles)
    near[0], near[1] = low, high
    between = whole_sum(tree([face_energy(a, b) for a, b in zip(tiles, tiles[1:])]))
    line = total[15:16] + jnp.where(lanes()[0:1] == 5, between, 0.0)
    ends = jnp.where(lanes() < 16, tiles[-1], tiles[0])
    for k in range(sent.shape[0]):
        sent[k, 0:15] = total[0:15]
        sent[k, 15:16] = line
        sent[k, 16:24] = ends


def first_flow_kernel(right, mobility, diag, off, xl, yl, xh, yh, flow, cond):
    sub = lax.broadcasted_iota(jnp.int32, (8, 128), 0)
    for u in range(3):
        for x in range(4):
            rows = slice(8 * x, 8 * x + 8)
            total = block_row(right, diag, off, u, rows)
            value, own = right[u, rows], mobility[u, rows]
            near = low_views(right, 0, u, x, (xl, yl), sub)
            near += high_views(right, 0, u, x, (xh, yh), sub)
            near_mob = low_views(mobility, 1, u, x, (xl, yl), sub)
            near_mob += high_views(mobility, 1, u, x, (xh, yh), sub)
            for d in range(4):
                weight = 2.0 * own * near_mob[d] / (own + near_mob[d])
                cond[d, u, rows] = weight
                total = total + weight * (value - near[d])
            flow[u, rows] = total


def flow_kernel(field, diag, off, cond, xl, yl, xh, yh, flow):
    sub = lax.broadcasted_iota(jnp.int32, (8, 128), 0)
    for u in range(3):
        for x in range(4):
            rows = slice(8 * x, 8 * x + 8)
            total = block_row(field, diag, off, u, rows)
            value = field[u, rows]
            near = low_views(field, 0, u, x, (xl, yl), sub)
            near += high_views(field, 0, u, x, (xh, yh), sub)
            for d in range(4):
                total = total + cond[d, u, rows] * (value - near[d])
            flow[u, rows] = total


def flow_along(field, flow, cond, low, high):
    lane = lanes()
    out = []
    for u in range(3):
        blocks = []
        for x in range(4):
            rows = slice(8 * x, 8 * x + 8)
            value = field[u, rows]
            step_low = value - low_along(value, low, 4 * u + x, lane)
            step_high = value - high_along(value, high, 16 + 4 * u + x, lane)
            total = flow[u, rows] + cond[0, u, rows] * step_low
            blocks.append(total + cond[1, u, rows] * step_high)
        out.append(jnp.concatenate(blocks, 0))
    return out


def put_cond_along(cond, mobility, low, high):
    lane = lanes()
    for u in range(3):
        for x in range(4):
            rows = slice(8 * x, 8 * x + 8)
            own = mobility[u, rows]
            near = low_along(own, low, 32 + 4 * u + x, lane)
            cond[0, u, rows] = 2.0 * own * near / (own + near)
            near = high_along(own, high, 48 + 4 * u + x, lane)
            cond[1, u, rows] = 2.0 * own * near / (own + near)


def advance(means, flow, field, extra, weight, row, lane, wells):
    picked = gather_wells(means, wells)
    pulled = scatter_cells([weight * m for m in picked], row, lane)
    return [flow[u] + extra * field[u] - pulled[u] for u in range(3)]


def second_kernel(
    slots, near, flow, right, mobility, cell, well, factor,
    field, table, inverse, extra, cond, *faces
):
    total = jnp.sum(slots[...], axis=0)
    low, high = halo_tiles(near, slots, lambda a: unfold(a[4 * WELL_ROWS : 24]))
    put_cond_along(cond, mobility, low, high)
    whole = flow_along(right, flow, cond, low, high)
    scale = 1.0 / (1.0 + total[3 * WELL_ROWS : 4 * WELL_ROWS])
    inverse[...] = jnp.zeros((8, 128), F32)
    inverse[0:WELL_ROWS] = scale
    rows = get_well_rows(total[: 3 * WELL_ROWS], 3)
    scale_row = get_well_rows(scale, 1)[0]
    row, lane = cell_masks(cell[0])
    wells = well_mask(well[0])
    weight = factor[0]
    own = scatter_cells([weight], row, lane)[0]
    extra[...] = own
    fresh = advance([r * scale_row for r in rows], whole, right, own, weight, row, lane, wells)
    for u in range(3):
        field[u] = fresh[u]
    values = gather_cells(fresh, row, lane)
    put_well_rows(table, scatter_wells([weight * v for v in values], wells))
    table[15:16] = jnp.zeros((1, 128), F32)
    table[16:24] = end_tile([(field, 0)], [(field, 16)])
    put_faces(faces, [field])


def third_kernel(
    slots, near, flow, before, extra, inverse, cond, cell, well, factor, field, table, *faces
):
    total = jnp.sum(slots[...], axis=0)
    low, high = halo_tiles(near, slots, lambda a: a[16:24])
    whole = flow_along(before, flow, cond, low, high)
    scale_row = get_well_rows(inverse[...], 1)[0]
    rows = get_well_rows(total, 3)
    row, lane = cell_masks(cell[0])
    wells = well_mask(well[0])
    weight = factor[0]
    fresh = advance([r * scale_row for r in rows], whole, before, extra[...], weight, row, lane, wells)
    for u in range(3):
        field[u] = fresh[u]
    values = gather_cells(fresh, row, lane)
    put_well_rows(table, scatter_wells([weight * v for v in values], wells))
    table[15:16] = jnp.zeros((1, 128), F32)
    table[16:24] = end_tile([(field, 0)], [(field, 16), (cond.at[0], 32)])
    put_faces(faces, [field])


def tree(terms):
    while len(terms) > 1:
        pairs = [a + b for a, b in zip(terms[::2], terms[1::2])]
        terms = pairs + ([terms[-1]] if len(terms) % 2 else [])
    return terms[0]


def moment_kernel(wells_table, w0, w1, w2, extra, diag, off, cond, cond_along, xl, yl, table):
    lane, sub = lanes(), lax.broadcasted_iota(jnp.int32, (8, 128), 0)
    sums = [[] for _ in range(6)]
    for u in range(3):
        for x in range(4):
            rows = slice(8 * x, 8 * x + 8)
            a, b, c = w0[u, rows], w1[u, rows], w2[u, rows]
            for k, (p, q) in enumerate(((a, a), (a, b), (b, b), (b, c), (c, c))):
                sums[k].append(p * q)
            energy = c * (block_row(w2, diag, off, u, rows) + extra[rows] * c)
            for d, near in enumerate(low_views(w2, 0, u, x, (xl, yl), sub)):
                energy = energy + cond[d, u, rows] * (c - near) * (c - near)
            step = jnp.where(lane == 0, 0.0, c - pltpu.roll(c, 1, 1))
            sums[5].append(energy + cond_along[0, u, rows] * step * step)
    line = jnp.zeros((1, 128), F32)
    for k in range(6):
        line = jnp.where(lane[0:1] == k, whole_sum(tree(sums[k])), line)
    table[...] = wells_table[...]
    table[15:16] = line


def scalar_kernel(slots, inverse, sent):
    total = jnp.sum(slots[...], axis=0)
    pull = jnp.zeros((WELL_ROWS, 128), F32)
    scale = inverse[0:WELL_ROWS]
    for u in range(3):
        part = total[u * WELL_ROWS : (u + 1) * WELL_ROWS]
        pull = pull + part * part * scale
    tiles = [slots[k, 16:24] for k in range(slots.shape[0])]
    between = tree([face_energy(a, b) for a, b in zip(tiles, tiles[1:])])
    line = total[15:16]
    lane = lanes()[0:1]
    out = []
    for k in range(6):
        value = jnp.sum(jnp.where(lane == k, line, 0.0), axis=1, keepdims=True)
        if k == 5:
            value = value + (whole_sum(between) - whole_sum(pull))
        out.append(jnp.broadcast_to(value, (1, 128)))
    moments = jnp.concatenate(out + [jnp.zeros((2, 128), F32)], 0)
    for k in range(sent.shape[0]):
        sent[k] = moments


def last_vector_kernel(
    slots, near, flow, before, extra, inverse, cond, cell, well, factor, field
):
    total = jnp.sum(slots[...], axis=0)
    low, high = halo_tiles(near, slots, lambda a: a[16:24])
    whole = flow_along(before, flow, cond, low, high)
    scale_row = get_well_rows(inverse[...], 1)[0]
    rows = get_well_rows(total, 3)
    row, lane = cell_masks(cell[0])
    fresh = advance(
        [r * scale_row for r in rows], whole, before, extra[...], factor[0], row, lane,
        well_mask(well[0]),
    )
    for u in range(3):
        field[u] = fresh[u]


def plus(a, b, scale):
    size = max(len(a), len(b))
    out = []
    for k in range(size):
        p = a[k] if k < len(a) else None
        q = scale * b[k] if k < len(b) else None
        out.append(q if p is None else p if q is None else p + q)
    return out


def image_of(a):
    raised = [None] + list(a)
    return [
        SHIFT * a[0] if k == 0 else raised[k] + SHIFT * a[k] if k < len(a) else raised[k]
        for k in range(len(a) + 1)
    ]


def inner(a, b, moment):
    by_degree = {}
    for i, p in enumerate(a):
        for j, q in enumerate(b):
            by_degree[i + j] = by_degree.get(i + j, 0.0) + p * q
    return tree([by_degree[k] * moment[k] for k in sorted(by_degree)])


def combine_kernel(slots, w0, w1, w2, w3, solved, rest):
    terms = [slots[k] for k in range(slots.shape[0])]
    total = tree(terms)
    moment = [total[k : k + 1] for k in range(6)]
    one = jnp.ones((1, 128), F32)
    residual, direction, solution_field = [one], [one], []
    norm = moment[0]
    for step in range(3):
        image = image_of(direction)
        alpha = norm / inner(direction, image, moment)
        solution_field = plus(solution_field, direction, alpha)
        residual = plus(residual, image, -alpha)
        if step < 2:
            fresh = inner(residual, residual, moment)
            direction = plus(residual, direction, fresh / norm)
            norm = fresh
    solution_field = [jnp.broadcast_to(c, (8, 128)) for c in solution_field]
    residual = [jnp.broadcast_to(c, (8, 128)) for c in residual]
    for u in range(3):
        for x in range(4):
            rows = slice(8 * x, 8 * x + 8)
            basis = [w0[u, rows], w1[u, rows], w2[u, rows], w3[u, rows]]
            solved[u, rows] = tree([c * w for c, w in zip(solution_field, basis)])
            rest[u, rows] = tree([c * w for c, w in zip(residual, basis)])


def call(kernel, shapes, *args, space=pltpu.VMEM, scratch=(), mib=32):
    return pl.pallas_call(
        kernel,
        out_shape=[jax.ShapeDtypeStruct(shape, F32) for shape in shapes],
        in_specs=[pl.BlockSpec(memory_space=space)] * len(args),
        out_specs=[pl.BlockSpec(memory_space=pltpu.VMEM)] * len(shapes),
        scratch_shapes=list(scratch),
        compiler_params=pltpu.CompilerParams(vmem_limit_bytes=mib * 1024 * 1024),
    )(*args)


NEAR = 4


def near_slots(table):
    count = lax.axis_size("gz")
    groups = [[NEAR * g + k for k in range(NEAR)] for g in range(count // NEAR)]
    sent = jnp.broadcast_to(table[None], (NEAR,) + table.shape)
    return lax.all_to_all(sent, "gz", 0, 0, axis_index_groups=groups)


def far_slots(sent):
    count = lax.axis_size("gz")
    groups = [[g + NEAR * k for k in range(count // NEAR)] for g in range(NEAR)]
    return lax.all_to_all(sent, "gz", 0, 0, axis_index_groups=groups)


def forward(piece, axis):
    count = lax.axis_size(axis)
    return lax.ppermute(piece, axis, [(i, i + 1) for i in range(count - 1)])


def backward(piece, axis):
    count = lax.axis_size(axis)
    return lax.ppermute(piece, axis, [(i + 1, i) for i in range(count - 1)])


def low_halos(faces):
    return [forward(faces[0], "gx"), forward(faces[2], "gy")]


def high_halos(faces):
    return [backward(faces[1], "gx"), backward(faces[3], "gy")]


def after(first, *later):
    return lax.optimization_barrier((first, *later))


def face_shapes(fields):
    return [(3 * fields, 8, 128)] * 2 + [(12 * fields, 128)] * 2


def body(right_side, block_diag, block_off, mobility, perf_cell, perf_well, perf_factor):
    block = (3, 32, 128)
    right, diag, off, mob = (
        a.reshape(block) for a in (right_side, block_diag, block_off, mobility)
    )
    perfs = (perf_cell, perf_well, perf_factor)
    sent_shapes = [(lax.axis_size("gz") // NEAR, 24, 128), (2, 8, 128)]

    table, *faces = call(
        first_kernel, [(24, 128)] + face_shapes(2), right, mob, *perfs,
        space=pltpu.HBM, mib=60,
        scratch=[pltpu.VMEM(block, F32)] * 2
        + [pltpu.VMEM(a.shape, a.dtype) for a in perfs]
        + [pltpu.SemaphoreType.DMA((5,))],
    )
    slots, *halos = after(near_slots(table), *low_halos(faces), *high_halos(faces))
    sent, near = call(first_near_kernel, sent_shapes, slots)
    slots = far_slots(sent)
    flow, cond = call(
        first_flow_kernel, [block, (4,) + block], right, mob, diag, off, *halos
    )
    w1, table, inverse, extra, cond_along, *faces = call(
        second_kernel,
        [block, (24, 128), (8, 128), (32, 128), (2,) + block] + face_shapes(1),
        slots, near, flow, right, mob, *perfs,
    )

    slots, *halos = after(near_slots(table), *low_halos(faces), *high_halos(faces))
    sent, near = call(near_kernel, sent_shapes, slots)
    slots = far_slots(sent)
    flow = call(flow_kernel, [block], w1, diag, off, cond, *halos)[0]
    w2, table, *faces = call(
        third_kernel, [block, (24, 128)] + face_shapes(1),
        slots, near, flow, w1, extra, inverse, cond_along, *perfs,
    )

    low = low_halos(faces)
    high = high_halos(faces)
    table = call(
        moment_kernel, [(24, 128)],
        table, right, w1, w2, extra, diag, off, cond, cond_along, *low,
    )[0]
    slots, *high = after(near_slots(table), *high)
    sent, near = call(last_near_kernel, sent_shapes, slots)
    slots = far_slots(sent)
    flow = call(flow_kernel, [block], w2, diag, off, cond, *low, *high)[0]

    count = lax.axis_size("gx") * lax.axis_size("gy")
    sent = call(scalar_kernel, [(count, 8, 128)], slots, inverse)[0]
    moment_slots = lax.all_to_all(sent, ("gx", "gy"), 0, 0)
    w3 = call(
        last_vector_kernel, [block],
        slots, near, flow, w2, extra, inverse, cond_along, *perfs,
    )[0]
    solved, rest = call(combine_kernel, [block, block], moment_slots, right, w1, w2, w3)
    return solved.reshape(right_side.shape), rest.reshape(right_side.shape)


def solution(mesh):
    field = P(None, "gx", "gy", "gz")
    perf = P("gx", "gy", "gz")
    return jax.shard_map(
        body,
        mesh=mesh,
        in_specs=(field, field, field, field, perf, perf, perf),
        out_specs=(field, field),
        check_vma=False,
    )
```

```python
import jax
import jax.numpy as jnp
from jax import lax
from jax.experimental import pallas as pl
from jax.experimental.pallas import tpu as pltpu
from jax.sharding import PartitionSpec as P

W_COL = 640
WELL_ROWS = W_COL // 128
SHIFT = 8.0
F32 = jnp.float32
BF16 = jnp.bfloat16


def split3(a):
    first = a.astype(BF16)
    rest = a - first.astype(F32)
    second = rest.astype(BF16)
    third = (rest - second.astype(F32)).astype(BF16)
    return [first, second, third]


def sum3(a, rows):
    return a[:rows] + a[rows : 2 * rows] + a[2 * rows : 3 * rows]


def one_hot(index, rows):
    ids = lax.broadcasted_iota(jnp.int32, (rows, index.shape[1]), 0)
    return ids == index


def cell_masks(cell):
    row = one_hot(lax.shift_right_logical(cell, 7), 32).astype(F32)
    lane = one_hot(lax.bitwise_and(cell, 127), 128).astype(F32).astype(BF16)
    return row, lane


def well_mask(well):
    return one_hot(well, W_COL).astype(F32).astype(BF16)


def gather_cells(fields, row, lane):
    parts = [part for field in fields for part in split3(field)]
    picked = jnp.dot(jnp.concatenate(parts, 0), lane, preferred_element_type=F32)
    out = []
    for u in range(len(fields)):
        block = sum3(picked[96 * u : 96 * (u + 1)], 32)
        out.append(jnp.sum(block * row, axis=0, keepdims=True))
    return out


def scatter_cells(values, row, lane):
    parts = [part for value in values for part in split3(row * value)]
    placed = lax.dot_general(
        jnp.concatenate(parts, 0), lane, (((1,), (1,)), ((), ())), preferred_element_type=F32
    )
    return [sum3(placed[96 * u : 96 * (u + 1)], 32) for u in range(len(values))]


def scatter_wells(values, wells):
    count = len(values)
    stacked = jnp.concatenate(values + [jnp.zeros_like(values[0])] * (8 - count), 0)
    sums = lax.dot_general(
        jnp.concatenate(split3(stacked), 0), wells, (((1,), (1,)), ((), ())),
        preferred_element_type=F32,
    )
    sums = sum3(sums, 8)
    return [sums[u : u + 1] for u in range(count)]


def gather_wells(rows, wells):
    count = len(rows)
    stacked = jnp.concatenate(rows + [jnp.zeros_like(rows[0])] * (8 - count), 0)
    picked = sum3(jnp.dot(jnp.concatenate(split3(stacked), 0), wells, preferred_element_type=F32), 8)
    return [picked[u : u + 1] for u in range(count)]


def put_well_rows(ref, rows):
    for u, row in enumerate(rows):
        for j in range(WELL_ROWS):
            ref[u * WELL_ROWS + j : u * WELL_ROWS + j + 1, :] = row[:, 128 * j : 128 * (j + 1)]


def get_well_rows(table, count):
    out = []
    for u in range(count):
        pieces = [table[u * WELL_ROWS + j : u * WELL_ROWS + j + 1] for j in range(WELL_ROWS)]
        out.append(jnp.concatenate(pieces, 1))
    return out


def lanes():
    return lax.broadcasted_iota(jnp.int32, (8, 128), 1)


def put_faces(refs, fields):
    gx_high, gx_low, gy_high, gy_low = refs
    for k, field in enumerate(fields):
        for u in range(3):
            gx_high[3 * k + u] = field[u, 24:32]
            gx_low[3 * k + u] = field[u, 0:8]
            for x in range(4):
                at = 12 * k + 4 * u + x
                gy_high[at : at + 1] = field[u, 8 * x + 7 : 8 * x + 8]
                gy_low[at : at + 1] = field[u, 8 * x : 8 * x + 1]


def end_tile(highs, lows):
    lane = lanes()
    tile = jnp.zeros((8, 128), F32)
    for fields, turn in ((highs, 1), (lows, 0)):
        for field, start in fields:
            for u in range(3):
                for x in range(4):
                    at = start + 4 * u + x
                    value = pltpu.roll(field[u, 8 * x : 8 * x + 8], at + turn, 1)
                    tile = jnp.where(lane == at, value, tile)
    return tile


def fold(tile):
    return jnp.where(lanes()[0:4] < 64, tile[0:4], pltpu.roll(tile, 64, 1)[4:8])


def unfold(rows):
    return jnp.concatenate([rows, pltpu.roll(jnp.concatenate([rows, rows], 0), 64, 1)[0:4]], 0)


def low_views(field, k, u, x, halo, sub):
    gx_low, gy_low = halo
    value = field[u, 8 * x : 8 * x + 8]
    view_x = field[u, 8 * x - 8 : 8 * x] if x else gx_low[3 * k + u]
    at = 12 * k + 4 * u + x
    edge = jnp.broadcast_to(gy_low[at : at + 1], (8, 128))
    return [view_x, jnp.where(sub == 0, edge, pltpu.roll(value, 1, 0))]


def high_views(field, k, u, x, halo, sub):
    gx_high, gy_high = halo
    value = field[u, 8 * x : 8 * x + 8]
    view_x = field[u, 8 * x + 8 : 8 * x + 16] if x < 3 else gx_high[3 * k + u]
    at = 12 * k + 4 * u + x
    edge = jnp.broadcast_to(gy_high[at : at + 1], (8, 128))
    return [view_x, jnp.where(sub == 7, edge, pltpu.roll(value, 7, 0))]


def low_along(value, tile, at, lane):
    return jnp.where(lane == 0, pltpu.roll(tile, (128 - at) % 128, 1), pltpu.roll(value, 1, 1))


def high_along(value, tile, at, lane):
    return jnp.where(lane == 127, pltpu.roll(tile, 127 - at, 1), pltpu.roll(value, 127, 1))


def place():
    at = lax.axis_index("gz")
    return lax.div(at, NEAR), lax.rem(at, NEAR)


def near_tiles(tiles):
    _, member = place()
    low, high = tiles[0], tiles[-1]
    for k in range(1, NEAR - 1):
        low = jnp.where(member == k + 1, tiles[k], low)
        high = jnp.where(member == k - 1, tiles[k], high)
    return low, high


def halo_tiles(near, slots, read):
    group, member = place()
    last = slots.shape[0] - 1
    below = jnp.where(group == 0, 0.0, read(slots[jnp.maximum(group - 1, 0)]))
    above = jnp.where(group == last, 0.0, read(slots[jnp.minimum(group + 1, last)]))
    return jnp.where(member == 0, below, near[0]), jnp.where(member == NEAR - 1, above, near[1])


def block_row(field, diag, off, u, rows):
    pick = ((None, 0, 1), (0, None, 2), (1, 2, None))[u]
    total = (diag[u, rows] - SHIFT) * field[u, rows]
    for t in range(3):
        if pick[t] is not None:
            total = total + off[pick[t], rows] * field[t, rows]
    return total


def first_kernel(right_any, mobility_any, cell_any, well_any, factor_any, table, *rest):
    faces, (right, mobility, cell, well, factor, sems) = rest[:4], rest[4:]
    copies = [
        pltpu.make_async_copy(source, target, sems.at[k])
        for k, (source, target) in enumerate(
            (
                (cell_any, cell),
                (right_any, right),
                (factor_any, factor),
                (well_any, well),
                (mobility_any, mobility),
            )
        )
    ]
    for copy in copies:
        copy.start()
    for copy in copies:
        copy.wait()
    row, lane = cell_masks(cell[0])
    values = gather_cells([right[u] for u in range(3)], row, lane)
    weight = factor[0]
    sums = scatter_wells([weight * v for v in values] + [weight], well_mask(well[0]))
    ends = fold(end_tile([(right, 0), (mobility, 32)], [(right, 16), (mobility, 48)]))
    for k in range(NEAR):
        put_well_rows(table.at[k], sums)
        table[k, 4 * WELL_ROWS : 24] = ends
    put_faces(faces, [right, mobility])


def first_near_kernel(slots, sent, near):
    rows = 4 * WELL_ROWS
    total = jnp.sum(slots[...], axis=0)
    tiles = [unfold(slots[k, rows:24]) for k in range(NEAR)]
    low, high = near_tiles(tiles)
    near[0], near[1] = low, high
    lane = lanes()
    ends = fold(jnp.where(lax.bitwise_and(lane, 31) < 16, tiles[-1], tiles[0]))
    for k in range(sent.shape[0]):
        sent[k, 0:rows] = total[0:rows]
        sent[k, rows:24] = ends


def near_kernel(slots, sent, near):
    total = jnp.sum(slots[...], axis=0)
    tiles = [slots[k, 16:24] for k in range(NEAR)]
    low, high = near_tiles(tiles)
    near[0], near[1] = low, high
    ends = jnp.where(lanes() < 16, tiles[-1], tiles[0])
    for k in range(sent.shape[0]):
        sent[k, 0:16] = total[0:16]
        sent[k, 16:24] = ends


def face_energy(below, above):
    step = pltpu.roll(above, 112, 1) - below
    return jnp.where(lanes() < 12, pltpu.roll(above, 96, 1) * step * step, 0.0)


def whole_sum(a):
    return jnp.sum(jnp.sum(a, axis=0, keepdims=True), axis=1, keepdims=True)


def last_near_kernel(slots, sent, near):
    total = jnp.sum(slots[...], axis=0)
    tiles = [slots[k, 16:24] for k in range(NEAR)]
    low, high = near_tiles(tiles)
    near[0], near[1] = low, high
    between = whole_sum(tree([face_energy(a, b) for a, b in zip(tiles, tiles[1:])]))
    line = total[15:16] + jnp.where(lanes()[0:1] == 5, between, 0.0)
    ends = jnp.where(lanes() < 16, tiles[-1], tiles[0])
    for k in range(sent.shape[0]):
        sent[k, 0:15] = total[0:15]
        sent[k, 15:16] = line
        sent[k, 16:24] = ends


def first_flow_kernel(right, mobility, diag, off, xl, yl, xh, yh, flow, cond):
    sub = lax.broadcasted_iota(jnp.int32, (8, 128), 0)
    for u in range(3):
        for x in range(4):
            rows = slice(8 * x, 8 * x + 8)
            total = block_row(right, diag, off, u, rows)
            value, own = right[u, rows], mobility[u, rows]
            near = low_views(right, 0, u, x, (xl, yl), sub)
            near += high_views(right, 0, u, x, (xh, yh), sub)
            near_mob = low_views(mobility, 1, u, x, (xl, yl), sub)
            near_mob += high_views(mobility, 1, u, x, (xh, yh), sub)
            for d in range(4):
                weight = 2.0 * own * near_mob[d] / (own + near_mob[d])
                cond[d, u, rows] = weight
                total = total + weight * (value - near[d])
            flow[u, rows] = total


def flow_kernel(field, diag, off, cond, xl, yl, xh, yh, flow):
    sub = lax.broadcasted_iota(jnp.int32, (8, 128), 0)
    for u in range(3):
        for x in range(4):
            rows = slice(8 * x, 8 * x + 8)
            total = block_row(field, diag, off, u, rows)
            value = field[u, rows]
            near = low_views(field, 0, u, x, (xl, yl), sub)
            near += high_views(field, 0, u, x, (xh, yh), sub)
            for d in range(4):
                total = total + cond[d, u, rows] * (value - near[d])
            flow[u, rows] = total


def flow_along(field, flow, cond, low, high):
    lane = lanes()
    out = []
    for u in range(3):
        blocks = []
        for x in range(4):
            rows = slice(8 * x, 8 * x + 8)
            value = field[u, rows]
            step_low = value - low_along(value, low, 4 * u + x, lane)
            step_high = value - high_along(value, high, 16 + 4 * u + x, lane)
            total = flow[u, rows] + cond[0, u, rows] * step_low
            blocks.append(total + cond[1, u, rows] * step_high)
        out.append(jnp.concatenate(blocks, 0))
    return out


def put_cond_along(cond, mobility, low, high):
    lane = lanes()
    for u in range(3):
        for x in range(4):
            rows = slice(8 * x, 8 * x + 8)
            own = mobility[u, rows]
            near = low_along(own, low, 32 + 4 * u + x, lane)
            cond[0, u, rows] = 2.0 * own * near / (own + near)
            near = high_along(own, high, 48 + 4 * u + x, lane)
            cond[1, u, rows] = 2.0 * own * near / (own + near)


def advance(means, flow, field, extra, weight, row, lane, wells):
    picked = gather_wells(means, wells)
    pulled = scatter_cells([weight * m for m in picked], row, lane)
    return [flow[u] + extra * field[u] - pulled[u] for u in range(3)]


def second_kernel(
    slots, near, flow, right, mobility, cell, well, factor,
    field, table, inverse, extra, cond, *faces
):
    total = jnp.sum(slots[...], axis=0)
    low, high = halo_tiles(near, slots, lambda a: unfold(a[4 * WELL_ROWS : 24]))
    put_cond_along(cond, mobility, low, high)
    whole = flow_along(right, flow, cond, low, high)
    scale = 1.0 / (1.0 + total[3 * WELL_ROWS : 4 * WELL_ROWS])
    inverse[...] = jnp.zeros((8, 128), F32)
    inverse[0:WELL_ROWS] = scale
    rows = get_well_rows(total[: 3 * WELL_ROWS], 3)
    scale_row = get_well_rows(scale, 1)[0]
    row, lane = cell_masks(cell[0])
    wells = well_mask(well[0])
    weight = factor[0]
    own = scatter_cells([weight], row, lane)[0]
    extra[...] = own
    fresh = advance([r * scale_row for r in rows], whole, right, own, weight, row, lane, wells)
    for u in range(3):
        field[u] = fresh[u]
    values = gather_cells(fresh, row, lane)
    put_well_rows(table, scatter_wells([weight * v for v in values], wells))
    table[15:16] = jnp.zeros((1, 128), F32)
    table[16:24] = end_tile([(field, 0)], [(field, 16)])
    put_faces(faces, [field])


def third_kernel(
    slots, near, flow, before, extra, inverse, cond, cell, well, factor, field, table, *faces
):
    total = jnp.sum(slots[...], axis=0)
    low, high = halo_tiles(near, slots, lambda a: a[16:24])
    whole = flow_along(before, flow, cond, low, high)
    scale_row = get_well_rows(inverse[...], 1)[0]
    rows = get_well_rows(total, 3)
    row, lane = cell_masks(cell[0])
    wells = well_mask(well[0])
    weight = factor[0]
    fresh = advance([r * scale_row for r in rows], whole, before, extra[...], weight, row, lane, wells)
    for u in range(3):
        field[u] = fresh[u]
    values = gather_cells(fresh, row, lane)
    put_well_rows(table, scatter_wells([weight * v for v in values], wells))
    table[15:16] = jnp.zeros((1, 128), F32)
    table[16:24] = end_tile([(field, 0)], [(field, 16), (cond.at[0], 32)])
    put_faces(faces, [field])


def tree(terms):
    while len(terms) > 1:
        pairs = [a + b for a, b in zip(terms[::2], terms[1::2])]
        terms = pairs + ([terms[-1]] if len(terms) % 2 else [])
    return terms[0]


def moment_kernel(wells_table, w0, w1, w2, extra, diag, off, cond, cond_along, xl, yl, table):
    lane, sub = lanes(), lax.broadcasted_iota(jnp.int32, (8, 128), 0)
    sums = [[] for _ in range(6)]
    for u in range(3):
        for x in range(4):
            rows = slice(8 * x, 8 * x + 8)
            a, b, c = w0[u, rows], w1[u, rows], w2[u, rows]
            for k, (p, q) in enumerate(((a, a), (a, b), (b, b), (b, c), (c, c))):
                sums[k].append(p * q)
            energy = c * (block_row(w2, diag, off, u, rows) + extra[rows] * c)
            for d, near in enumerate(low_views(w2, 0, u, x, (xl, yl), sub)):
                energy = energy + cond[d, u, rows] * (c - near) * (c - near)
            step = jnp.where(lane == 0, 0.0, c - pltpu.roll(c, 1, 1))
            sums[5].append(energy + cond_along[0, u, rows] * step * step)
    line = jnp.zeros((1, 128), F32)
    for k in range(6):
        line = jnp.where(lane[0:1] == k, whole_sum(tree(sums[k])), line)
    table[...] = wells_table[...]
    table[15:16] = line


def scalar_kernel(slots, inverse, sent):
    total = jnp.sum(slots[...], axis=0)
    pull = jnp.zeros((WELL_ROWS, 128), F32)
    scale = inverse[0:WELL_ROWS]
    for u in range(3):
        part = total[u * WELL_ROWS : (u + 1) * WELL_ROWS]
        pull = pull + part * part * scale
    tiles = [slots[k, 16:24] for k in range(slots.shape[0])]
    between = tree([face_energy(a, b) for a, b in zip(tiles, tiles[1:])])
    last = whole_sum(between) - whole_sum(pull)
    line = total[15:16] + jnp.where(lanes()[0:1] == 5, last, 0.0)
    for k in range(sent.shape[0]):
        sent[k] = line


def plus(a, b, scale):
    size = max(len(a), len(b))
    out = []
    for k in range(size):
        p = a[k] if k < len(a) else None
        q = scale * b[k] if k < len(b) else None
        out.append(q if p is None else p if q is None else p + q)
    return out


def image_of(a):
    raised = [None] + list(a)
    return [
        SHIFT * a[0] if k == 0 else raised[k] + SHIFT * a[k] if k < len(a) else raised[k]
        for k in range(len(a) + 1)
    ]


def inner(a, b, moment):
    by_degree = {}
    for i, p in enumerate(a):
        for j, q in enumerate(b):
            by_degree[i + j] = by_degree.get(i + j, 0.0) + p * q
    return tree([by_degree[k] * moment[k] for k in sorted(by_degree)])


def combine_kernel(
    lines, slots, near, flow, extra, inverse, cond, cell, well, factor, w0, w1, w2, solved, rest
):
    total = jnp.sum(slots[...], axis=0)
    low, high = halo_tiles(near, slots, lambda a: a[16:24])
    whole = flow_along(w2, flow, cond, low, high)
    scale_row = get_well_rows(inverse[...], 1)[0]
    means = [r * scale_row for r in get_well_rows(total, 3)]
    row, lane = cell_masks(cell[0])
    w3 = advance(means, whole, w2, extra[...], factor[0], row, lane, well_mask(well[0]))

    line = tree([lines[k] for k in range(lines.shape[0])])
    first = lanes()[0:1]
    moment = [
        jnp.broadcast_to(jnp.sum(jnp.where(first == k, line, 0.0), axis=1, keepdims=True), (1, 128))
        for k in range(6)
    ]
    one = jnp.ones((1, 128), F32)
    residual, direction, solution_field = [one], [one], []
    norm = moment[0]
    for step in range(3):
        image = image_of(direction)
        alpha = norm / inner(direction, image, moment)
        solution_field = plus(solution_field, direction, alpha)
        residual = plus(residual, image, -alpha)
        if step < 2:
            fresh = inner(residual, residual, moment)
            direction = plus(residual, direction, fresh / norm)
            norm = fresh
    solution_field = [jnp.broadcast_to(c, (8, 128)) for c in solution_field]
    residual = [jnp.broadcast_to(c, (8, 128)) for c in residual]
    for u in range(3):
        for x in range(4):
            rows = slice(8 * x, 8 * x + 8)
            basis = [w0[u, rows], w1[u, rows], w2[u, rows], w3[u][rows]]
            solved[u, rows] = tree([c * w for c, w in zip(solution_field, basis)])
            rest[u, rows] = tree([c * w for c, w in zip(residual, basis)])


def call(kernel, shapes, *args, space=pltpu.VMEM, scratch=(), mib=32):
    return pl.pallas_call(
        kernel,
        out_shape=[jax.ShapeDtypeStruct(shape, F32) for shape in shapes],
        in_specs=[pl.BlockSpec(memory_space=space)] * len(args),
        out_specs=[pl.BlockSpec(memory_space=pltpu.VMEM)] * len(shapes),
        scratch_shapes=list(scratch),
        compiler_params=pltpu.CompilerParams(vmem_limit_bytes=mib * 1024 * 1024),
    )(*args)


NEAR = 4


def near_slots(sent):
    count = lax.axis_size("gz")
    groups = [[NEAR * g + k for k in range(NEAR)] for g in range(count // NEAR)]
    return lax.all_to_all(sent, "gz", 0, 0, axis_index_groups=groups)


def copies(table):
    return jnp.broadcast_to(table[None], (NEAR,) + table.shape)


def far_slots(sent):
    count = lax.axis_size("gz")
    groups = [[g + NEAR * k for k in range(count // NEAR)] for g in range(NEAR)]
    return lax.all_to_all(sent, "gz", 0, 0, axis_index_groups=groups)


def forward(piece, axis):
    count = lax.axis_size(axis)
    return lax.ppermute(piece, axis, [(i, i + 1) for i in range(count - 1)])


def backward(piece, axis):
    count = lax.axis_size(axis)
    return lax.ppermute(piece, axis, [(i + 1, i) for i in range(count - 1)])


def low_halos(faces):
    return [forward(faces[0], "gx"), forward(faces[2], "gy")]


def high_halos(faces):
    return [backward(faces[1], "gx"), backward(faces[3], "gy")]


def after(first, *later):
    return lax.optimization_barrier((first, *later))


def face_shapes(fields):
    return [(3 * fields, 8, 128)] * 2 + [(12 * fields, 128)] * 2


def body(right_side, block_diag, block_off, mobility, perf_cell, perf_well, perf_factor):
    block = (3, 32, 128)
    right, diag, off, mob = (
        a.reshape(block) for a in (right_side, block_diag, block_off, mobility)
    )
    perfs = (perf_cell, perf_well, perf_factor)
    sent_shapes = [(lax.axis_size("gz") // NEAR, 24, 128), (2, 8, 128)]

    table, *faces = call(
        first_kernel, [(NEAR, 24, 128)] + face_shapes(2), right, mob, *perfs,
        space=pltpu.HBM, mib=60,
        scratch=[pltpu.VMEM(block, F32)] * 2
        + [pltpu.VMEM(a.shape, a.dtype) for a in perfs]
        + [pltpu.SemaphoreType.DMA((5,))],
    )
    sent, near = call(first_near_kernel, sent_shapes, near_slots(table))
    sent, *faces = after(sent, *faces)
    slots = far_slots(sent)
    flow, cond = call(
        first_flow_kernel, [block, (4,) + block],
        right, mob, diag, off, *low_halos(faces), *high_halos(faces),
    )
    w1, table, inverse, extra, cond_along, *faces = call(
        second_kernel,
        [block, (24, 128), (8, 128), (32, 128), (2,) + block] + face_shapes(1),
        slots, near, flow, right, mob, *perfs,
    )

    sent, near = call(near_kernel, sent_shapes, near_slots(copies(table)))
    sent, *faces = after(sent, *faces)
    slots = far_slots(sent)
    flow = call(
        flow_kernel, [block], w1, diag, off, cond, *low_halos(faces), *high_halos(faces)
    )[0]
    w2, table, *faces = call(
        third_kernel, [block, (24, 128)] + face_shapes(1),
        slots, near, flow, w1, extra, inverse, cond_along, *perfs,
    )

    low = low_halos(faces)
    table = call(
        moment_kernel, [(24, 128)],
        table, right, w1, w2, extra, diag, off, cond, cond_along, *low,
    )[0]
    sent, near = call(last_near_kernel, sent_shapes, near_slots(copies(table)))
    sent, *faces = after(sent, *faces)
    slots = far_slots(sent)
    high = high_halos(faces)
    flow = call(flow_kernel, [block], w2, diag, off, cond, *low, *high)[0]
    slots, flow = after(slots, flow)

    count = lax.axis_size("gx") * lax.axis_size("gy")
    sent = call(scalar_kernel, [(count, 1, 128)], slots, inverse)[0]
    lines = lax.all_to_all(sent, ("gx", "gy"), 0, 0)
    solved, rest = call(
        combine_kernel, [block, block],
        lines, slots, near, flow, extra, inverse, cond_along, *perfs, right, w1, w2,
    )
    return solved.reshape(right_side.shape), rest.reshape(right_side.shape)


def solution(mesh):
    field = P(None, "gx", "gy", "gz")
    perf = P("gx", "gy", "gz")
    return jax.shard_map(
        body,
        mesh=mesh,
        in_specs=(field, field, field, field, perf, perf, perf),
        out_specs=(field, field),
        check_vma=False,
    )
```

```python
import jax
import jax.numpy as jnp
from jax import lax
from jax.experimental import pallas as pl
from jax.experimental.pallas import tpu as pltpu
from jax.sharding import PartitionSpec as P

W_COL = 640
WELL_ROWS = W_COL // 128
SHIFT = 8.0
F32 = jnp.float32
BF16 = jnp.bfloat16


def split3(a):
    first = a.astype(BF16)
    rest = a - first.astype(F32)
    second = rest.astype(BF16)
    third = (rest - second.astype(F32)).astype(BF16)
    return [first, second, third]


def sum3(a, rows):
    return a[:rows] + a[rows : 2 * rows] + a[2 * rows : 3 * rows]


def one_hot(index, rows):
    ids = lax.broadcasted_iota(jnp.int32, (rows, index.shape[1]), 0)
    return ids == index


def cell_masks(cell):
    row = one_hot(lax.shift_right_logical(cell, 7), 32).astype(F32)
    lane = one_hot(lax.bitwise_and(cell, 127), 128).astype(F32).astype(BF16)
    return row, lane


def well_mask(well):
    return one_hot(well, W_COL).astype(F32).astype(BF16)


def gather_cells(fields, row, lane):
    parts = [part for field in fields for part in split3(field)]
    picked = jnp.dot(jnp.concatenate(parts, 0), lane, preferred_element_type=F32)
    out = []
    for u in range(len(fields)):
        block = sum3(picked[96 * u : 96 * (u + 1)], 32)
        out.append(jnp.sum(block * row, axis=0, keepdims=True))
    return out


def scatter_cells(values, row, lane):
    parts = [part for value in values for part in split3(row * value)]
    placed = lax.dot_general(
        jnp.concatenate(parts, 0), lane, (((1,), (1,)), ((), ())), preferred_element_type=F32
    )
    return [sum3(placed[96 * u : 96 * (u + 1)], 32) for u in range(len(values))]


def scatter_wells(values, wells):
    count = len(values)
    stacked = jnp.concatenate(values + [jnp.zeros_like(values[0])] * (8 - count), 0)
    sums = lax.dot_general(
        jnp.concatenate(split3(stacked), 0), wells, (((1,), (1,)), ((), ())),
        preferred_element_type=F32,
    )
    sums = sum3(sums, 8)
    return [sums[u : u + 1] for u in range(count)]


def gather_wells(rows, wells):
    count = len(rows)
    stacked = jnp.concatenate(rows + [jnp.zeros_like(rows[0])] * (8 - count), 0)
    picked = sum3(jnp.dot(jnp.concatenate(split3(stacked), 0), wells, preferred_element_type=F32), 8)
    return [picked[u : u + 1] for u in range(count)]


def put_well_rows(ref, rows):
    for u, row in enumerate(rows):
        for j in range(WELL_ROWS):
            ref[u * WELL_ROWS + j : u * WELL_ROWS + j + 1, :] = row[:, 128 * j : 128 * (j + 1)]


def get_well_rows(table, count):
    out = []
    for u in range(count):
        pieces = [table[u * WELL_ROWS + j : u * WELL_ROWS + j + 1] for j in range(WELL_ROWS)]
        out.append(jnp.concatenate(pieces, 1))
    return out


def lanes():
    return lax.broadcasted_iota(jnp.int32, (8, 128), 1)


def put_faces(refs, fields):
    gx_high, gx_low, gy_high, gy_low = refs
    for k, field in enumerate(fields):
        for u in range(3):
            gx_high[3 * k + u] = field[u, 24:32]
            gx_low[3 * k + u] = field[u, 0:8]
            for x in range(4):
                at = 12 * k + 4 * u + x
                gy_high[at : at + 1] = field[u, 8 * x + 7 : 8 * x + 8]
                gy_low[at : at + 1] = field[u, 8 * x : 8 * x + 1]


def end_tile(highs, lows):
    lane = lanes()
    tile = jnp.zeros((8, 128), F32)
    for fields, turn in ((highs, 1), (lows, 0)):
        for field, start in fields:
            for u in range(3):
                for x in range(4):
                    at = start + 4 * u + x
                    value = pltpu.roll(field[u, 8 * x : 8 * x + 8], at + turn, 1)
                    tile = jnp.where(lane == at, value, tile)
    return tile


def fold(tile):
    return jnp.where(lanes()[0:4] < 64, tile[0:4], pltpu.roll(tile, 64, 1)[4:8])


def unfold(rows):
    return jnp.concatenate([rows, pltpu.roll(jnp.concatenate([rows, rows], 0), 64, 1)[0:4]], 0)


def low_views(field, k, u, x, halo, sub):
    gx_low, gy_low = halo
    value = field[u, 8 * x : 8 * x + 8]
    view_x = field[u, 8 * x - 8 : 8 * x] if x else gx_low[3 * k + u]
    at = 12 * k + 4 * u + x
    edge = jnp.broadcast_to(gy_low[at : at + 1], (8, 128))
    return [view_x, jnp.where(sub == 0, edge, pltpu.roll(value, 1, 0))]


def high_views(field, k, u, x, halo, sub):
    gx_high, gy_high = halo
    value = field[u, 8 * x : 8 * x + 8]
    view_x = field[u, 8 * x + 8 : 8 * x + 16] if x < 3 else gx_high[3 * k + u]
    at = 12 * k + 4 * u + x
    edge = jnp.broadcast_to(gy_high[at : at + 1], (8, 128))
    return [view_x, jnp.where(sub == 7, edge, pltpu.roll(value, 7, 0))]


def low_along(value, tile, at, lane):
    return jnp.where(lane == 0, pltpu.roll(tile, (128 - at) % 128, 1), pltpu.roll(value, 1, 1))


def high_along(value, tile, at, lane):
    return jnp.where(lane == 127, pltpu.roll(tile, 127 - at, 1), pltpu.roll(value, 127, 1))


def place():
    at = lax.axis_index("gz")
    return lax.div(at, NEAR), lax.rem(at, NEAR)


def slot_of(group, count):
    return (group + count - count // 2) % count


def near_tiles(tiles):
    _, member = place()
    low, high = tiles[0], tiles[-1]
    for k in range(1, NEAR - 1):
        low = jnp.where(member == k + 1, tiles[k], low)
        high = jnp.where(member == k - 1, tiles[k], high)
    return low, high


def halo_tiles(near, slots, read):
    group, member = place()
    last = slots.shape[0] - 1
    below = jnp.where(group == 0, 0.0, read(slots[slot_of(jnp.maximum(group - 1, 0), last + 1)]))
    above = jnp.where(group == last, 0.0, read(slots[slot_of(jnp.minimum(group + 1, last), last + 1)]))
    return jnp.where(member == 0, below, near[0]), jnp.where(member == NEAR - 1, above, near[1])


def block_row(field, diag, off, u, rows):
    pick = ((None, 0, 1), (0, None, 2), (1, 2, None))[u]
    total = (diag[u, rows] - SHIFT) * field[u, rows]
    for t in range(3):
        if pick[t] is not None:
            total = total + off[pick[t], rows] * field[t, rows]
    return total


def first_kernel(right_any, mobility_any, cell_any, well_any, factor_any, table, *rest):
    faces, (right, mobility, cell, well, factor, sems) = rest[:4], rest[4:]
    copies = [
        pltpu.make_async_copy(source, target, sems.at[k])
        for k, (source, target) in enumerate(
            (
                (cell_any, cell),
                (right_any, right),
                (factor_any, factor),
                (well_any, well),
                (mobility_any, mobility),
            )
        )
    ]
    for copy in copies:
        copy.start()
    for copy in copies:
        copy.wait()
    row, lane = cell_masks(cell[0])
    values = gather_cells([right[u] for u in range(3)], row, lane)
    weight = factor[0]
    sums = scatter_wells([weight * v for v in values] + [weight], well_mask(well[0]))
    ends = fold(end_tile([(right, 0), (mobility, 32)], [(right, 16), (mobility, 48)]))
    for k in range(NEAR):
        put_well_rows(table.at[k], sums)
        table[k, 4 * WELL_ROWS : 24] = ends
    put_faces(faces, [right, mobility])


def first_near_kernel(slots, sent, near):
    rows = 4 * WELL_ROWS
    total = jnp.sum(slots[...], axis=0)
    tiles = [unfold(slots[k, rows:24]) for k in range(NEAR)]
    low, high = near_tiles(tiles)
    near[0], near[1] = low, high
    lane = lanes()
    ends = fold(jnp.where(lax.bitwise_and(lane, 31) < 16, tiles[-1], tiles[0]))
    for k in range(sent.shape[0]):
        sent[k, 0:rows] = total[0:rows]
        sent[k, rows:24] = ends


def near_kernel(slots, sent, near):
    total = jnp.sum(slots[...], axis=0)
    tiles = [slots[k, 16:24] for k in range(NEAR)]
    low, high = near_tiles(tiles)
    near[0], near[1] = low, high
    ends = jnp.where(lanes() < 16, tiles[-1], tiles[0])
    for k in range(sent.shape[0]):
        sent[k, 0:16] = total[0:16]
        sent[k, 16:24] = ends


def face_energy(below, above):
    step = pltpu.roll(above, 112, 1) - below
    return jnp.where(lanes() < 12, pltpu.roll(above, 96, 1) * step * step, 0.0)


def whole_sum(a):
    return jnp.sum(jnp.sum(a, axis=0, keepdims=True), axis=1, keepdims=True)


def last_near_kernel(slots, sent, near):
    total = jnp.sum(slots[...], axis=0)
    tiles = [slots[k, 16:24] for k in range(NEAR)]
    low, high = near_tiles(tiles)
    near[0], near[1] = low, high
    between = whole_sum(tree([face_energy(a, b) for a, b in zip(tiles, tiles[1:])]))
    line = total[15:16] + jnp.where(lanes()[0:1] == 5, between, 0.0)
    ends = jnp.where(lanes() < 16, tiles[-1], tiles[0])
    for k in range(sent.shape[0]):
        sent[k, 0:15] = total[0:15]
        sent[k, 15:16] = line
        sent[k, 16:24] = ends


def first_flow_kernel(right, mobility, diag, off, xl, yl, xh, yh, flow, cond):
    sub = lax.broadcasted_iota(jnp.int32, (8, 128), 0)
    for u in range(3):
        for x in range(4):
            rows = slice(8 * x, 8 * x + 8)
            total = block_row(right, diag, off, u, rows)
            value, own = right[u, rows], mobility[u, rows]
            near = low_views(right, 0, u, x, (xl, yl), sub)
            near += high_views(right, 0, u, x, (xh, yh), sub)
            near_mob = low_views(mobility, 1, u, x, (xl, yl), sub)
            near_mob += high_views(mobility, 1, u, x, (xh, yh), sub)
            for d in range(4):
                weight = 2.0 * own * near_mob[d] / (own + near_mob[d])
                cond[d, u, rows] = weight
                total = total + weight * (value - near[d])
            flow[u, rows] = total


def flow_kernel(field, diag, off, cond, xl, yl, xh, yh, flow):
    sub = lax.broadcasted_iota(jnp.int32, (8, 128), 0)
    for u in range(3):
        for x in range(4):
            rows = slice(8 * x, 8 * x + 8)
            total = block_row(field, diag, off, u, rows)
            value = field[u, rows]
            near = low_views(field, 0, u, x, (xl, yl), sub)
            near += high_views(field, 0, u, x, (xh, yh), sub)
            for d in range(4):
                total = total + cond[d, u, rows] * (value - near[d])
            flow[u, rows] = total


def flow_along(field, flow, cond, low, high):
    lane = lanes()
    out = []
    for u in range(3):
        blocks = []
        for x in range(4):
            rows = slice(8 * x, 8 * x + 8)
            value = field[u, rows]
            step_low = value - low_along(value, low, 4 * u + x, lane)
            step_high = value - high_along(value, high, 16 + 4 * u + x, lane)
            total = flow[u, rows] + cond[0, u, rows] * step_low
            blocks.append(total + cond[1, u, rows] * step_high)
        out.append(jnp.concatenate(blocks, 0))
    return out


def put_cond_along(cond, mobility, low, high):
    lane = lanes()
    for u in range(3):
        for x in range(4):
            rows = slice(8 * x, 8 * x + 8)
            own = mobility[u, rows]
            near = low_along(own, low, 32 + 4 * u + x, lane)
            cond[0, u, rows] = 2.0 * own * near / (own + near)
            near = high_along(own, high, 48 + 4 * u + x, lane)
            cond[1, u, rows] = 2.0 * own * near / (own + near)


def advance(means, flow, field, extra, weight, row, lane, wells):
    picked = gather_wells(means, wells)
    pulled = scatter_cells([weight * m for m in picked], row, lane)
    return [flow[u] + extra * field[u] - pulled[u] for u in range(3)]


def second_kernel(
    slots, near, flow, right, mobility, cell, well, factor,
    field, table, inverse, extra, cond, *faces
):
    total = jnp.sum(slots[...], axis=0)
    low, high = halo_tiles(near, slots, lambda a: unfold(a[4 * WELL_ROWS : 24]))
    put_cond_along(cond, mobility, low, high)
    whole = flow_along(right, flow, cond, low, high)
    scale = 1.0 / (1.0 + total[3 * WELL_ROWS : 4 * WELL_ROWS])
    inverse[...] = jnp.zeros((8, 128), F32)
    inverse[0:WELL_ROWS] = scale
    rows = get_well_rows(total[: 3 * WELL_ROWS], 3)
    scale_row = get_well_rows(scale, 1)[0]
    row, lane = cell_masks(cell[0])
    wells = well_mask(well[0])
    weight = factor[0]
    own = scatter_cells([weight], row, lane)[0]
    extra[...] = own
    fresh = advance([r * scale_row for r in rows], whole, right, own, weight, row, lane, wells)
    for u in range(3):
        field[u] = fresh[u]
    values = gather_cells(fresh, row, lane)
    put_well_rows(table, scatter_wells([weight * v for v in values], wells))
    table[15:16] = jnp.zeros((1, 128), F32)
    table[16:24] = end_tile([(field, 0)], [(field, 16)])
    put_faces(faces, [field])


def third_kernel(
    slots, near, flow, before, extra, inverse, cond, cell, well, factor, field, table, *faces
):
    total = jnp.sum(slots[...], axis=0)
    low, high = halo_tiles(near, slots, lambda a: a[16:24])
    whole = flow_along(before, flow, cond, low, high)
    scale_row = get_well_rows(inverse[...], 1)[0]
    rows = get_well_rows(total, 3)
    row, lane = cell_masks(cell[0])
    wells = well_mask(well[0])
    weight = factor[0]
    fresh = advance([r * scale_row for r in rows], whole, before, extra[...], weight, row, lane, wells)
    for u in range(3):
        field[u] = fresh[u]
    values = gather_cells(fresh, row, lane)
    put_well_rows(table, scatter_wells([weight * v for v in values], wells))
    table[15:16] = jnp.zeros((1, 128), F32)
    table[16:24] = end_tile([(field, 0)], [(field, 16), (cond.at[0], 32)])
    put_faces(faces, [field])


def tree(terms):
    while len(terms) > 1:
        pairs = [a + b for a, b in zip(terms[::2], terms[1::2])]
        terms = pairs + ([terms[-1]] if len(terms) % 2 else [])
    return terms[0]


def moment_kernel(wells_table, w0, w1, w2, extra, diag, off, cond, cond_along, xl, yl, table):
    lane, sub = lanes(), lax.broadcasted_iota(jnp.int32, (8, 128), 0)
    sums = [[] for _ in range(6)]
    for u in range(3):
        for x in range(4):
            rows = slice(8 * x, 8 * x + 8)
            a, b, c = w0[u, rows], w1[u, rows], w2[u, rows]
            for k, (p, q) in enumerate(((a, a), (a, b), (b, b), (b, c), (c, c))):
                sums[k].append(p * q)
            energy = c * (block_row(w2, diag, off, u, rows) + extra[rows] * c)
            for d, near in enumerate(low_views(w2, 0, u, x, (xl, yl), sub)):
                energy = energy + cond[d, u, rows] * (c - near) * (c - near)
            step = jnp.where(lane == 0, 0.0, c - pltpu.roll(c, 1, 1))
            sums[5].append(energy + cond_along[0, u, rows] * step * step)
    line = jnp.zeros((1, 128), F32)
    for k in range(6):
        line = jnp.where(lane[0:1] == k, whole_sum(tree(sums[k])), line)
    table[...] = wells_table[...]
    table[15:16] = line


def scalar_kernel(slots, inverse, sent):
    total = jnp.sum(slots[...], axis=0)
    pull = jnp.zeros((WELL_ROWS, 128), F32)
    scale = inverse[0:WELL_ROWS]
    for u in range(3):
        part = total[u * WELL_ROWS : (u + 1) * WELL_ROWS]
        pull = pull + part * part * scale
    count = slots.shape[0]
    tiles = [slots[slot_of(k, count), 16:24] for k in range(count)]
    between = tree([face_energy(a, b) for a, b in zip(tiles, tiles[1:])])
    last = whole_sum(between) - whole_sum(pull)
    line = total[15:16] + jnp.where(lanes()[0:1] == 5, last, 0.0)
    for k in range(sent.shape[0]):
        sent[k] = line


def plus(a, b, scale):
    size = max(len(a), len(b))
    out = []
    for k in range(size):
        p = a[k] if k < len(a) else None
        q = scale * b[k] if k < len(b) else None
        out.append(q if p is None else p if q is None else p + q)
    return out


def image_of(a):
    raised = [None] + list(a)
    return [
        SHIFT * a[0] if k == 0 else raised[k] + SHIFT * a[k] if k < len(a) else raised[k]
        for k in range(len(a) + 1)
    ]


def inner(a, b, moment):
    by_degree = {}
    for i, p in enumerate(a):
        for j, q in enumerate(b):
            by_degree[i + j] = by_degree.get(i + j, 0.0) + p * q
    return tree([by_degree[k] * moment[k] for k in sorted(by_degree)])


def combine_kernel(
    lines, slots, near, flow, extra, inverse, cond, cell, well, factor, w0, w1, w2, solved, rest
):
    total = jnp.sum(slots[...], axis=0)
    low, high = halo_tiles(near, slots, lambda a: a[16:24])
    whole = flow_along(w2, flow, cond, low, high)
    scale_row = get_well_rows(inverse[...], 1)[0]
    means = [r * scale_row for r in get_well_rows(total, 3)]
    row, lane = cell_masks(cell[0])
    w3 = advance(means, whole, w2, extra[...], factor[0], row, lane, well_mask(well[0]))

    line = tree([lines[k] for k in range(lines.shape[0])])
    first = lanes()[0:1]
    moment = [
        jnp.broadcast_to(jnp.sum(jnp.where(first == k, line, 0.0), axis=1, keepdims=True), (1, 128))
        for k in range(6)
    ]
    one = jnp.ones((1, 128), F32)
    residual, direction, solution_field = [one], [one], []
    norm = moment[0]
    for step in range(3):
        image = image_of(direction)
        alpha = norm / inner(direction, image, moment)
        solution_field = plus(solution_field, direction, alpha)
        residual = plus(residual, image, -alpha)
        if step < 2:
            fresh = inner(residual, residual, moment)
            direction = plus(residual, direction, fresh / norm)
            norm = fresh
    solution_field = [jnp.broadcast_to(c, (8, 128)) for c in solution_field]
    residual = [jnp.broadcast_to(c, (8, 128)) for c in residual]
    for u in range(3):
        for x in range(4):
            rows = slice(8 * x, 8 * x + 8)
            basis = [w0[u, rows], w1[u, rows], w2[u, rows], w3[u][rows]]
            solved[u, rows] = tree([c * w for c, w in zip(solution_field, basis)])
            rest[u, rows] = tree([c * w for c, w in zip(residual, basis)])


def call(kernel, shapes, *args, space=pltpu.VMEM, scratch=(), mib=32):
    return pl.pallas_call(
        kernel,
        out_shape=[jax.ShapeDtypeStruct(shape, F32) for shape in shapes],
        in_specs=[pl.BlockSpec(memory_space=space)] * len(args),
        out_specs=[pl.BlockSpec(memory_space=pltpu.VMEM)] * len(shapes),
        scratch_shapes=list(scratch),
        compiler_params=pltpu.CompilerParams(vmem_limit_bytes=mib * 1024 * 1024),
    )(*args)


NEAR = 4


def near_slots(sent):
    count = lax.axis_size("gz")
    groups = [[NEAR * g + k for k in range(NEAR)] for g in range(count // NEAR)]
    return lax.all_to_all(sent, "gz", 0, 0, axis_index_groups=groups)


def copies(table):
    return jnp.broadcast_to(table[None], (NEAR,) + table.shape)


def far_slots(sent):
    count = lax.axis_size("gz")
    slots = count // NEAR
    order = sorted(range(slots), key=lambda group: slot_of(group, slots))
    groups = [[g + NEAR * k for k in order] for g in range(NEAR)]
    return lax.all_to_all(sent, "gz", 0, 0, axis_index_groups=groups)


def forward(piece, axis):
    count = lax.axis_size(axis)
    return lax.ppermute(piece, axis, [(i, i + 1) for i in range(count - 1)])


def backward(piece, axis):
    count = lax.axis_size(axis)
    return lax.ppermute(piece, axis, [(i + 1, i) for i in range(count - 1)])


def low_halos(faces):
    return [forward(faces[0], "gx"), forward(faces[2], "gy")]


def high_halos(faces):
    return [backward(faces[1], "gx"), backward(faces[3], "gy")]


def after(first, *later):
    return lax.optimization_barrier((first, *later))


def face_shapes(fields):
    return [(3 * fields, 8, 128)] * 2 + [(12 * fields, 128)] * 2


def body(right_side, block_diag, block_off, mobility, perf_cell, perf_well, perf_factor):
    block = (3, 32, 128)
    right, diag, off, mob = (
        a.reshape(block) for a in (right_side, block_diag, block_off, mobility)
    )
    perfs = (perf_cell, perf_well, perf_factor)
    sent_shapes = [(lax.axis_size("gz") // NEAR, 24, 128), (2, 8, 128)]

    table, *faces = call(
        first_kernel, [(NEAR, 24, 128)] + face_shapes(2), right, mob, *perfs,
        space=pltpu.HBM, mib=60,
        scratch=[pltpu.VMEM(block, F32)] * 2
        + [pltpu.VMEM(a.shape, a.dtype) for a in perfs]
        + [pltpu.SemaphoreType.DMA((5,))],
    )
    sent, near = call(first_near_kernel, sent_shapes, near_slots(table))
    sent, *faces = after(sent, *faces)
    slots = far_slots(sent)
    flow, cond = call(
        first_flow_kernel, [block, (4,) + block],
        right, mob, diag, off, *low_halos(faces), *high_halos(faces),
    )
    w1, table, inverse, extra, cond_along, *faces = call(
        second_kernel,
        [block, (24, 128), (8, 128), (32, 128), (2,) + block] + face_shapes(1),
        slots, near, flow, right, mob, *perfs,
    )

    sent, near = call(near_kernel, sent_shapes, near_slots(copies(table)))
    sent, *faces = after(sent, *faces)
    slots = far_slots(sent)
    flow = call(
        flow_kernel, [block], w1, diag, off, cond, *low_halos(faces), *high_halos(faces)
    )[0]
    w2, table, *faces = call(
        third_kernel, [block, (24, 128)] + face_shapes(1),
        slots, near, flow, w1, extra, inverse, cond_along, *perfs,
    )

    low = low_halos(faces)
    table = call(
        moment_kernel, [(24, 128)],
        table, right, w1, w2, extra, diag, off, cond, cond_along, *low,
    )[0]
    sent, near = call(last_near_kernel, sent_shapes, near_slots(copies(table)))
    sent, *faces = after(sent, *faces)
    slots = far_slots(sent)
    high = high_halos(faces)
    flow = call(flow_kernel, [block], w2, diag, off, cond, *low, *high)[0]
    slots, flow = after(slots, flow)

    count = lax.axis_size("gx") * lax.axis_size("gy")
    sent = call(scalar_kernel, [(count, 1, 128)], slots, inverse)[0]
    lines = lax.all_to_all(sent, ("gx", "gy"), 0, 0)
    solved, rest = call(
        combine_kernel, [block, block],
        lines, slots, near, flow, extra, inverse, cond_along, *perfs, right, w1, w2,
    )
    return solved.reshape(right_side.shape), rest.reshape(right_side.shape)


def solution(mesh):
    field = P(None, "gx", "gy", "gz")
    perf = P("gx", "gy", "gz")
    return jax.shard_map(
        body,
        mesh=mesh,
        in_specs=(field, field, field, field, perf, perf, perf),
        out_specs=(field, field),
        check_vma=False,
    )
```

```python
import jax
import jax.numpy as jnp
from jax import lax
from jax.experimental import pallas as pl
from jax.experimental.pallas import tpu as pltpu
from jax.sharding import PartitionSpec as P

W_COL = 640
WELL_ROWS = W_COL // 128
SHIFT = 8.0
F32 = jnp.float32
BF16 = jnp.bfloat16


def split3(a):
    first = a.astype(BF16)
    rest = a - first.astype(F32)
    second = rest.astype(BF16)
    third = (rest - second.astype(F32)).astype(BF16)
    return [first, second, third]


def sum3(a, rows):
    return a[:rows] + a[rows : 2 * rows] + a[2 * rows : 3 * rows]


def one_hot(index, rows):
    ids = lax.broadcasted_iota(jnp.int32, (rows, index.shape[1]), 0)
    return ids == index


def cell_masks(cell):
    row = one_hot(lax.shift_right_logical(cell, 7), 32).astype(F32)
    lane = one_hot(lax.bitwise_and(cell, 127), 128).astype(F32).astype(BF16)
    return row, lane


def well_mask(well):
    return one_hot(well, W_COL).astype(F32).astype(BF16)


def gather_cells(fields, row, lane):
    parts = [part for field in fields for part in split3(field)]
    picked = jnp.dot(jnp.concatenate(parts, 0), lane, preferred_element_type=F32)
    out = []
    for u in range(len(fields)):
        block = sum3(picked[96 * u : 96 * (u + 1)], 32)
        out.append(jnp.sum(block * row, axis=0, keepdims=True))
    return out


def scatter_cells(values, row, lane):
    parts = [part for value in values for part in split3(row * value)]
    placed = lax.dot_general(
        jnp.concatenate(parts, 0), lane, (((1,), (1,)), ((), ())), preferred_element_type=F32
    )
    return [sum3(placed[96 * u : 96 * (u + 1)], 32) for u in range(len(values))]


def scatter_wells(values, wells):
    count = len(values)
    stacked = jnp.concatenate(values + [jnp.zeros_like(values[0])] * (8 - count), 0)
    sums = lax.dot_general(
        jnp.concatenate(split3(stacked), 0), wells, (((1,), (1,)), ((), ())),
        preferred_element_type=F32,
    )
    sums = sum3(sums, 8)
    return [sums[u : u + 1] for u in range(count)]


def gather_wells(rows, wells):
    count = len(rows)
    stacked = jnp.concatenate(rows + [jnp.zeros_like(rows[0])] * (8 - count), 0)
    picked = sum3(jnp.dot(jnp.concatenate(split3(stacked), 0), wells, preferred_element_type=F32), 8)
    return [picked[u : u + 1] for u in range(count)]


def put_well_rows(ref, rows):
    for u, row in enumerate(rows):
        for j in range(WELL_ROWS):
            ref[u * WELL_ROWS + j : u * WELL_ROWS + j + 1, :] = row[:, 128 * j : 128 * (j + 1)]


def get_well_rows(table, count):
    out = []
    for u in range(count):
        pieces = [table[u * WELL_ROWS + j : u * WELL_ROWS + j + 1] for j in range(WELL_ROWS)]
        out.append(jnp.concatenate(pieces, 1))
    return out


def lanes():
    return lax.broadcasted_iota(jnp.int32, (8, 128), 1)


def put_faces(refs, fields):
    gx_high, gx_low, gy_high, gy_low = refs
    for k, field in enumerate(fields):
        for u in range(3):
            gx_high[3 * k + u] = field[u, 24:32]
            gx_low[3 * k + u] = field[u, 0:8]
            for x in range(4):
                at = 12 * k + 4 * u + x
                gy_high[at : at + 1] = field[u, 8 * x + 7 : 8 * x + 8]
                gy_low[at : at + 1] = field[u, 8 * x : 8 * x + 1]


def end_tile(highs, lows):
    lane = lanes()
    tile = jnp.zeros((8, 128), F32)
    for fields, turn in ((highs, 1), (lows, 0)):
        for field, start in fields:
            for u in range(3):
                for x in range(4):
                    at = start + 4 * u + x
                    value = pltpu.roll(field[u, 8 * x : 8 * x + 8], at + turn, 1)
                    tile = jnp.where(lane == at, value, tile)
    return tile


def fold(tile):
    return jnp.where(lanes()[0:4] < 64, tile[0:4], pltpu.roll(tile, 64, 1)[4:8])


def unfold(rows):
    return jnp.concatenate([rows, pltpu.roll(jnp.concatenate([rows, rows], 0), 64, 1)[0:4]], 0)


def low_views(field, k, u, x, halo, sub):
    gx_low, gy_low = halo
    value = field[u, 8 * x : 8 * x + 8]
    view_x = field[u, 8 * x - 8 : 8 * x] if x else gx_low[3 * k + u]
    at = 12 * k + 4 * u + x
    edge = jnp.broadcast_to(gy_low[at : at + 1], (8, 128))
    return [view_x, jnp.where(sub == 0, edge, pltpu.roll(value, 1, 0))]


def high_views(field, k, u, x, halo, sub):
    gx_high, gy_high = halo
    value = field[u, 8 * x : 8 * x + 8]
    view_x = field[u, 8 * x + 8 : 8 * x + 16] if x < 3 else gx_high[3 * k + u]
    at = 12 * k + 4 * u + x
    edge = jnp.broadcast_to(gy_high[at : at + 1], (8, 128))
    return [view_x, jnp.where(sub == 7, edge, pltpu.roll(value, 7, 0))]


def low_along(value, tile, at, lane):
    return jnp.where(lane == 0, pltpu.roll(tile, (128 - at) % 128, 1), pltpu.roll(value, 1, 1))


def high_along(value, tile, at, lane):
    return jnp.where(lane == 127, pltpu.roll(tile, 127 - at, 1), pltpu.roll(value, 127, 1))


def place():
    at = lax.axis_index("gz")
    return lax.div(at, NEAR), lax.rem(at, NEAR)


FIRST = (5, 3, 4)


def slot_of(group, count, step):
    return (group + count - FIRST[step] % count) % count


def near_tiles(tiles):
    _, member = place()
    low, high = tiles[0], tiles[-1]
    for k in range(1, NEAR - 1):
        low = jnp.where(member == k + 1, tiles[k], low)
        high = jnp.where(member == k - 1, tiles[k], high)
    return low, high


def halo_tiles(near, slots, read, step):
    group, member = place()
    last = slots.shape[0] - 1
    below = jnp.where(group == 0, 0.0, read(slots[slot_of(jnp.maximum(group - 1, 0), last + 1, step)]))
    above = jnp.where(group == last, 0.0, read(slots[slot_of(jnp.minimum(group + 1, last), last + 1, step)]))
    return jnp.where(member == 0, below, near[0]), jnp.where(member == NEAR - 1, above, near[1])


def block_row(field, diag, off, u, rows):
    pick = ((None, 0, 1), (0, None, 2), (1, 2, None))[u]
    total = (diag[u, rows] - SHIFT) * field[u, rows]
    for t in range(3):
        if pick[t] is not None:
            total = total + off[pick[t], rows] * field[t, rows]
    return total


def first_kernel(right_any, mobility_any, cell_any, well_any, factor_any, table, *rest):
    faces, (right, mobility, cell, well, factor, sems) = rest[:4], rest[4:]
    copies = [
        pltpu.make_async_copy(source, target, sems.at[k])
        for k, (source, target) in enumerate(
            (
                (cell_any, cell),
                (right_any, right),
                (factor_any, factor),
                (well_any, well),
                (mobility_any, mobility),
            )
        )
    ]
    for copy in copies:
        copy.start()
    for copy in copies:
        copy.wait()
    row, lane = cell_masks(cell[0])
    values = gather_cells([right[u] for u in range(3)], row, lane)
    weight = factor[0]
    sums = scatter_wells([weight * v for v in values] + [weight], well_mask(well[0]))
    ends = fold(end_tile([(right, 0), (mobility, 32)], [(right, 16), (mobility, 48)]))
    for k in range(NEAR):
        put_well_rows(table.at[k], sums)
        table[k, 4 * WELL_ROWS : 24] = ends
    put_faces(faces, [right, mobility])


def first_near_kernel(slots, sent, near):
    rows = 4 * WELL_ROWS
    total = jnp.sum(slots[...], axis=0)
    tiles = [unfold(slots[k, rows:24]) for k in range(NEAR)]
    low, high = near_tiles(tiles)
    near[0], near[1] = low, high
    lane = lanes()
    ends = fold(jnp.where(lax.bitwise_and(lane, 31) < 16, tiles[-1], tiles[0]))
    for k in range(sent.shape[0]):
        sent[k, 0:rows] = total[0:rows]
        sent[k, rows:24] = ends


def near_kernel(slots, sent, near):
    total = jnp.sum(slots[...], axis=0)
    tiles = [slots[k, 16:24] for k in range(NEAR)]
    low, high = near_tiles(tiles)
    near[0], near[1] = low, high
    ends = jnp.where(lanes() < 16, tiles[-1], tiles[0])
    for k in range(sent.shape[0]):
        sent[k, 0:16] = total[0:16]
        sent[k, 16:24] = ends


def face_energy(below, above):
    step = pltpu.roll(above, 112, 1) - below
    return jnp.where(lanes() < 12, pltpu.roll(above, 96, 1) * step * step, 0.0)


def whole_sum(a):
    return jnp.sum(jnp.sum(a, axis=0, keepdims=True), axis=1, keepdims=True)


def last_near_kernel(slots, sent, near):
    total = jnp.sum(slots[...], axis=0)
    tiles = [slots[k, 16:24] for k in range(NEAR)]
    low, high = near_tiles(tiles)
    near[0], near[1] = low, high
    between = whole_sum(tree([face_energy(a, b) for a, b in zip(tiles, tiles[1:])]))
    line = total[15:16] + jnp.where(lanes()[0:1] == 5, between, 0.0)
    ends = jnp.where(lanes() < 16, tiles[-1], tiles[0])
    for k in range(sent.shape[0]):
        sent[k, 0:15] = total[0:15]
        sent[k, 15:16] = line
        sent[k, 16:24] = ends


def first_flow_kernel(right, mobility, diag, off, xl, yl, xh, yh, flow, cond):
    sub = lax.broadcasted_iota(jnp.int32, (8, 128), 0)
    for u in range(3):
        for x in range(4):
            rows = slice(8 * x, 8 * x + 8)
            total = block_row(right, diag, off, u, rows)
            value, own = right[u, rows], mobility[u, rows]
            near = low_views(right, 0, u, x, (xl, yl), sub)
            near += high_views(right, 0, u, x, (xh, yh), sub)
            near_mob = low_views(mobility, 1, u, x, (xl, yl), sub)
            near_mob += high_views(mobility, 1, u, x, (xh, yh), sub)
            for d in range(4):
                weight = 2.0 * own * near_mob[d] / (own + near_mob[d])
                cond[d, u, rows] = weight
                total = total + weight * (value - near[d])
            flow[u, rows] = total


def flow_kernel(field, diag, off, cond, xl, yl, xh, yh, flow):
    sub = lax.broadcasted_iota(jnp.int32, (8, 128), 0)
    for u in range(3):
        for x in range(4):
            rows = slice(8 * x, 8 * x + 8)
            total = block_row(field, diag, off, u, rows)
            value = field[u, rows]
            near = low_views(field, 0, u, x, (xl, yl), sub)
            near += high_views(field, 0, u, x, (xh, yh), sub)
            for d in range(4):
                total = total + cond[d, u, rows] * (value - near[d])
            flow[u, rows] = total


def flow_along(field, flow, cond, low, high):
    lane = lanes()
    out = []
    for u in range(3):
        blocks = []
        for x in range(4):
            rows = slice(8 * x, 8 * x + 8)
            value = field[u, rows]
            step_low = value - low_along(value, low, 4 * u + x, lane)
            step_high = value - high_along(value, high, 16 + 4 * u + x, lane)
            total = flow[u, rows] + cond[0, u, rows] * step_low
            blocks.append(total + cond[1, u, rows] * step_high)
        out.append(jnp.concatenate(blocks, 0))
    return out


def put_cond_along(cond, mobility, low, high):
    lane = lanes()
    for u in range(3):
        for x in range(4):
            rows = slice(8 * x, 8 * x + 8)
            own = mobility[u, rows]
            near = low_along(own, low, 32 + 4 * u + x, lane)
            cond[0, u, rows] = 2.0 * own * near / (own + near)
            near = high_along(own, high, 48 + 4 * u + x, lane)
            cond[1, u, rows] = 2.0 * own * near / (own + near)


def advance(means, flow, field, extra, weight, row, lane, wells):
    picked = gather_wells(means, wells)
    pulled = scatter_cells([weight * m for m in picked], row, lane)
    return [flow[u] + extra * field[u] - pulled[u] for u in range(3)]


def second_kernel(
    slots, near, flow, right, mobility, cell, well, factor,
    field, table, inverse, extra, cond, *faces
):
    total = jnp.sum(slots[...], axis=0)
    low, high = halo_tiles(near, slots, lambda a: unfold(a[4 * WELL_ROWS : 24]), 0)
    put_cond_along(cond, mobility, low, high)
    whole = flow_along(right, flow, cond, low, high)
    scale = 1.0 / (1.0 + total[3 * WELL_ROWS : 4 * WELL_ROWS])
    inverse[...] = jnp.zeros((8, 128), F32)
    inverse[0:WELL_ROWS] = scale
    rows = get_well_rows(total[: 3 * WELL_ROWS], 3)
    scale_row = get_well_rows(scale, 1)[0]
    row, lane = cell_masks(cell[0])
    wells = well_mask(well[0])
    weight = factor[0]
    own = scatter_cells([weight], row, lane)[0]
    extra[...] = own
    fresh = advance([r * scale_row for r in rows], whole, right, own, weight, row, lane, wells)
    for u in range(3):
        field[u] = fresh[u]
    values = gather_cells(fresh, row, lane)
    put_well_rows(table, scatter_wells([weight * v for v in values], wells))
    table[15:16] = jnp.zeros((1, 128), F32)
    table[16:24] = end_tile([(field, 0)], [(field, 16)])
    put_faces(faces, [field])


def third_kernel(
    slots, near, flow, before, extra, inverse, cond, cell, well, factor, field, table, *faces
):
    total = jnp.sum(slots[...], axis=0)
    low, high = halo_tiles(near, slots, lambda a: a[16:24], 1)
    whole = flow_along(before, flow, cond, low, high)
    scale_row = get_well_rows(inverse[...], 1)[0]
    rows = get_well_rows(total, 3)
    row, lane = cell_masks(cell[0])
    wells = well_mask(well[0])
    weight = factor[0]
    fresh = advance([r * scale_row for r in rows], whole, before, extra[...], weight, row, lane, wells)
    for u in range(3):
        field[u] = fresh[u]
    values = gather_cells(fresh, row, lane)
    put_well_rows(table, scatter_wells([weight * v for v in values], wells))
    table[15:16] = jnp.zeros((1, 128), F32)
    table[16:24] = end_tile([(field, 0)], [(field, 16), (cond.at[0], 32)])
    put_faces(faces, [field])


def tree(terms):
    while len(terms) > 1:
        pairs = [a + b for a, b in zip(terms[::2], terms[1::2])]
        terms = pairs + ([terms[-1]] if len(terms) % 2 else [])
    return terms[0]


def moment_kernel(wells_table, w0, w1, w2, extra, diag, off, cond, cond_along, xl, yl, table):
    lane, sub = lanes(), lax.broadcasted_iota(jnp.int32, (8, 128), 0)
    sums = [[] for _ in range(6)]
    for u in range(3):
        for x in range(4):
            rows = slice(8 * x, 8 * x + 8)
            a, b, c = w0[u, rows], w1[u, rows], w2[u, rows]
            for k, (p, q) in enumerate(((a, a), (a, b), (b, b), (b, c), (c, c))):
                sums[k].append(p * q)
            energy = c * (block_row(w2, diag, off, u, rows) + extra[rows] * c)
            for d, near in enumerate(low_views(w2, 0, u, x, (xl, yl), sub)):
                energy = energy + cond[d, u, rows] * (c - near) * (c - near)
            step = jnp.where(lane == 0, 0.0, c - pltpu.roll(c, 1, 1))
            sums[5].append(energy + cond_along[0, u, rows] * step * step)
    line = jnp.zeros((1, 128), F32)
    for k in range(6):
        line = jnp.where(lane[0:1] == k, whole_sum(tree(sums[k])), line)
    table[...] = wells_table[...]
    table[15:16] = line


def scalar_kernel(slots, inverse, sent):
    total = jnp.sum(slots[...], axis=0)
    pull = jnp.zeros((WELL_ROWS, 128), F32)
    scale = inverse[0:WELL_ROWS]
    for u in range(3):
        part = total[u * WELL_ROWS : (u + 1) * WELL_ROWS]
        pull = pull + part * part * scale
    count = slots.shape[0]
    tiles = [slots[slot_of(k, count, 2), 16:24] for k in range(count)]
    between = tree([face_energy(a, b) for a, b in zip(tiles, tiles[1:])])
    last = whole_sum(between) - whole_sum(pull)
    line = total[15:16] + jnp.where(lanes()[0:1] == 5, last, 0.0)
    for k in range(sent.shape[0]):
        sent[k] = line


def plus(a, b, scale):
    size = max(len(a), len(b))
    out = []
    for k in range(size):
        p = a[k] if k < len(a) else None
        q = scale * b[k] if k < len(b) else None
        out.append(q if p is None else p if q is None else p + q)
    return out


def image_of(a):
    raised = [None] + list(a)
    return [
        SHIFT * a[0] if k == 0 else raised[k] + SHIFT * a[k] if k < len(a) else raised[k]
        for k in range(len(a) + 1)
    ]


def inner(a, b, moment):
    by_degree = {}
    for i, p in enumerate(a):
        for j, q in enumerate(b):
            by_degree[i + j] = by_degree.get(i + j, 0.0) + p * q
    return tree([by_degree[k] * moment[k] for k in sorted(by_degree)])


def combine_kernel(
    lines, slots, near, flow, extra, inverse, cond, cell, well, factor, w0, w1, w2, solved, rest
):
    total = jnp.sum(slots[...], axis=0)
    low, high = halo_tiles(near, slots, lambda a: a[16:24], 2)
    whole = flow_along(w2, flow, cond, low, high)
    scale_row = get_well_rows(inverse[...], 1)[0]
    means = [r * scale_row for r in get_well_rows(total, 3)]
    row, lane = cell_masks(cell[0])
    w3 = advance(means, whole, w2, extra[...], factor[0], row, lane, well_mask(well[0]))

    line = tree([lines[k] for k in range(lines.shape[0])])
    first = lanes()[0:1]
    moment = [
        jnp.broadcast_to(jnp.sum(jnp.where(first == k, line, 0.0), axis=1, keepdims=True), (1, 128))
        for k in range(6)
    ]
    one = jnp.ones((1, 128), F32)
    residual, direction, solution_field = [one], [one], []
    norm = moment[0]
    for step in range(3):
        image = image_of(direction)
        alpha = norm / inner(direction, image, moment)
        solution_field = plus(solution_field, direction, alpha)
        residual = plus(residual, image, -alpha)
        if step < 2:
            fresh = inner(residual, residual, moment)
            direction = plus(residual, direction, fresh / norm)
            norm = fresh
    solution_field = [jnp.broadcast_to(c, (8, 128)) for c in solution_field]
    residual = [jnp.broadcast_to(c, (8, 128)) for c in residual]
    for u in range(3):
        for x in range(4):
            rows = slice(8 * x, 8 * x + 8)
            basis = [w0[u, rows], w1[u, rows], w2[u, rows], w3[u][rows]]
            solved[u, rows] = tree([c * w for c, w in zip(solution_field, basis)])
            rest[u, rows] = tree([c * w for c, w in zip(residual, basis)])


def call(kernel, shapes, *args, space=pltpu.VMEM, scratch=(), mib=32):
    return pl.pallas_call(
        kernel,
        out_shape=[jax.ShapeDtypeStruct(shape, F32) for shape in shapes],
        in_specs=[pl.BlockSpec(memory_space=space)] * len(args),
        out_specs=[pl.BlockSpec(memory_space=pltpu.VMEM)] * len(shapes),
        scratch_shapes=list(scratch),
        compiler_params=pltpu.CompilerParams(vmem_limit_bytes=mib * 1024 * 1024),
    )(*args)


NEAR = 4


def near_slots(sent):
    count = lax.axis_size("gz")
    groups = [[NEAR * g + k for k in range(NEAR)] for g in range(count // NEAR)]
    return lax.all_to_all(sent, "gz", 0, 0, axis_index_groups=groups)


def copies(table):
    return jnp.broadcast_to(table[None], (NEAR,) + table.shape)


def far_slots(sent, step):
    count = lax.axis_size("gz")
    slots = count // NEAR
    order = sorted(range(slots), key=lambda group: slot_of(group, slots, step))
    groups = [[g + NEAR * k for k in order] for g in range(NEAR)]
    return lax.all_to_all(sent, "gz", 0, 0, axis_index_groups=groups)


def forward(piece, axis):
    count = lax.axis_size(axis)
    return lax.ppermute(piece, axis, [(i, i + 1) for i in range(count - 1)])


def backward(piece, axis):
    count = lax.axis_size(axis)
    return lax.ppermute(piece, axis, [(i + 1, i) for i in range(count - 1)])


def low_halos(faces):
    return [forward(faces[0], "gx"), forward(faces[2], "gy")]


def high_halos(faces):
    return [backward(faces[1], "gx"), backward(faces[3], "gy")]


def after(first, *later):
    return lax.optimization_barrier((first, *later))


def face_shapes(fields):
    return [(3 * fields, 8, 128)] * 2 + [(12 * fields, 128)] * 2


def body(right_side, block_diag, block_off, mobility, perf_cell, perf_well, perf_factor):
    block = (3, 32, 128)
    right, diag, off, mob = (
        a.reshape(block) for a in (right_side, block_diag, block_off, mobility)
    )
    perfs = (perf_cell, perf_well, perf_factor)
    sent_shapes = [(lax.axis_size("gz") // NEAR, 24, 128), (2, 8, 128)]

    table, *faces = call(
        first_kernel, [(NEAR, 24, 128)] + face_shapes(2), right, mob, *perfs,
        space=pltpu.HBM, mib=60,
        scratch=[pltpu.VMEM(block, F32)] * 2
        + [pltpu.VMEM(a.shape, a.dtype) for a in perfs]
        + [pltpu.SemaphoreType.DMA((5,))],
    )
    sent, near = call(first_near_kernel, sent_shapes, near_slots(table))
    sent, *faces = after(sent, *faces)
    slots = far_slots(sent, 0)
    flow, cond = call(
        first_flow_kernel, [block, (4,) + block],
        right, mob, diag, off, *low_halos(faces), *high_halos(faces),
    )
    w1, table, inverse, extra, cond_along, *faces = call(
        second_kernel,
        [block, (24, 128), (8, 128), (32, 128), (2,) + block] + face_shapes(1),
        slots, near, flow, right, mob, *perfs,
    )

    sent, near = call(near_kernel, sent_shapes, near_slots(copies(table)))
    sent, *faces = after(sent, *faces)
    slots = far_slots(sent, 1)
    flow = call(
        flow_kernel, [block], w1, diag, off, cond, *low_halos(faces), *high_halos(faces)
    )[0]
    w2, table, *faces = call(
        third_kernel, [block, (24, 128)] + face_shapes(1),
        slots, near, flow, w1, extra, inverse, cond_along, *perfs,
    )

    low = low_halos(faces)
    table = call(
        moment_kernel, [(24, 128)],
        table, right, w1, w2, extra, diag, off, cond, cond_along, *low,
    )[0]
    sent, near = call(last_near_kernel, sent_shapes, near_slots(copies(table)))
    sent, *faces = after(sent, *faces)
    slots = far_slots(sent, 2)
    high = high_halos(faces)
    flow = call(flow_kernel, [block], w2, diag, off, cond, *low, *high)[0]
    slots, flow = after(slots, flow)

    count = lax.axis_size("gx") * lax.axis_size("gy")
    sent = call(scalar_kernel, [(count, 1, 128)], slots, inverse)[0]
    lines = lax.all_to_all(sent, ("gx", "gy"), 0, 0)
    solved, rest = call(
        combine_kernel, [block, block],
        lines, slots, near, flow, extra, inverse, cond_along, *perfs, right, w1, w2,
    )
    return solved.reshape(right_side.shape), rest.reshape(right_side.shape)


def solution(mesh):
    field = P(None, "gx", "gy", "gz")
    perf = P("gx", "gy", "gz")
    return jax.shard_map(
        body,
        mesh=mesh,
        in_specs=(field, field, field, field, perf, perf, perf),
        out_specs=(field, field),
        check_vma=False,
    )
```

```python
import jax
import jax.numpy as jnp
from jax import lax
from jax.experimental import pallas as pl
from jax.experimental.pallas import tpu as pltpu
from jax.sharding import PartitionSpec as P

W_COL = 640
WELL_ROWS = W_COL // 128
SHIFT = 8.0
F32 = jnp.float32
BF16 = jnp.bfloat16


def split3(a):
    first = a.astype(BF16)
    rest = a - first.astype(F32)
    second = rest.astype(BF16)
    third = (rest - second.astype(F32)).astype(BF16)
    return [first, second, third]


def sum3(a, rows):
    return a[:rows] + a[rows : 2 * rows] + a[2 * rows : 3 * rows]


def one_hot(index, rows):
    ids = lax.broadcasted_iota(jnp.int32, (rows, index.shape[1]), 0)
    return ids == index


def cell_masks(cell):
    row = one_hot(lax.shift_right_logical(cell, 7), 32).astype(F32)
    lane = one_hot(lax.bitwise_and(cell, 127), 128).astype(F32).astype(BF16)
    return row, lane


def well_mask(well):
    return one_hot(well, W_COL).astype(F32).astype(BF16)


def gather_cells(fields, row, lane):
    parts = [part for field in fields for part in split3(field)]
    picked = jnp.dot(jnp.concatenate(parts, 0), lane, preferred_element_type=F32)
    out = []
    for u in range(len(fields)):
        block = sum3(picked[96 * u : 96 * (u + 1)], 32)
        out.append(jnp.sum(block * row, axis=0, keepdims=True))
    return out


def scatter_cells(values, row, lane):
    parts = [part for value in values for part in split3(row * value)]
    placed = lax.dot_general(
        jnp.concatenate(parts, 0), lane, (((1,), (1,)), ((), ())), preferred_element_type=F32
    )
    return [sum3(placed[96 * u : 96 * (u + 1)], 32) for u in range(len(values))]


def scatter_wells(values, wells):
    count = len(values)
    stacked = jnp.concatenate(values + [jnp.zeros_like(values[0])] * (8 - count), 0)
    sums = lax.dot_general(
        jnp.concatenate(split3(stacked), 0), wells, (((1,), (1,)), ((), ())),
        preferred_element_type=F32,
    )
    sums = sum3(sums, 8)
    return [sums[u : u + 1] for u in range(count)]


def gather_wells(rows, wells):
    count = len(rows)
    stacked = jnp.concatenate(rows + [jnp.zeros_like(rows[0])] * (8 - count), 0)
    picked = sum3(jnp.dot(jnp.concatenate(split3(stacked), 0), wells, preferred_element_type=F32), 8)
    return [picked[u : u + 1] for u in range(count)]


def put_well_rows(ref, rows):
    for u, row in enumerate(rows):
        for j in range(WELL_ROWS):
            ref[u * WELL_ROWS + j : u * WELL_ROWS + j + 1, :] = row[:, 128 * j : 128 * (j + 1)]


def get_well_rows(table, count):
    out = []
    for u in range(count):
        pieces = [table[u * WELL_ROWS + j : u * WELL_ROWS + j + 1] for j in range(WELL_ROWS)]
        out.append(jnp.concatenate(pieces, 1))
    return out


def lanes():
    return lax.broadcasted_iota(jnp.int32, (8, 128), 1)


def put_faces(refs, fields):
    gx_high, gx_low, gy_high, gy_low = refs
    for k, field in enumerate(fields):
        for u in range(3):
            gx_high[3 * k + u] = field[u, 24:32]
            gx_low[3 * k + u] = field[u, 0:8]
            for x in range(4):
                at = 12 * k + 4 * u + x
                gy_high[at : at + 1] = field[u, 8 * x + 7 : 8 * x + 8]
                gy_low[at : at + 1] = field[u, 8 * x : 8 * x + 1]


def end_tile(highs, lows):
    lane = lanes()
    tile = jnp.zeros((8, 128), F32)
    for fields, turn in ((highs, 1), (lows, 0)):
        for field, start in fields:
            for u in range(3):
                for x in range(4):
                    at = start + 4 * u + x
                    value = pltpu.roll(field[u, 8 * x : 8 * x + 8], at + turn, 1)
                    tile = jnp.where(lane == at, value, tile)
    return tile


def fold(tile):
    return jnp.where(lanes()[0:4] < 64, tile[0:4], pltpu.roll(tile, 64, 1)[4:8])


def unfold(rows):
    return jnp.concatenate([rows, pltpu.roll(jnp.concatenate([rows, rows], 0), 64, 1)[0:4]], 0)


def fold_narrow(tile):
    kept = jnp.where(lanes() < 32, tile, 0.0)
    turned = [kept[0:2]] + [pltpu.roll(kept, 32 * k, 1)[2 * k : 2 * k + 2] for k in (1, 2, 3)]
    return tree(turned)


def unfold_narrow(rows):
    sub = lax.broadcasted_iota(jnp.int32, (8, 128), 0)
    spread = jnp.concatenate(rows * 4, 0)
    tile = spread
    for k in (1, 2, 3):
        tile = jnp.where(sub >= 2 * k, pltpu.roll(spread, 128 - 32 * k, 1), tile)
    return tile


def slot_rows(slots, first, last):
    return [tree([slots[k, r] for k in range(slots.shape[0])]) for r in range(first, last)]


def well_rows(rows):
    return [
        jnp.concatenate(rows[u * WELL_ROWS : (u + 1) * WELL_ROWS], 1) for u in range(3)
    ]


def narrow_tile(slots):
    return lambda k: unfold_narrow([slots[k, 15], slots[k, 16]])


def wide_tile(slots):
    return lambda k: unfold(jnp.concatenate([slots[k, r] for r in range(16, 20)], 0))


def low_views(field, k, u, x, halo, sub):
    gx_low, gy_low = halo
    value = field[u, 8 * x : 8 * x + 8]
    view_x = field[u, 8 * x - 8 : 8 * x] if x else gx_low[3 * k + u]
    at = 12 * k + 4 * u + x
    edge = jnp.broadcast_to(gy_low[at : at + 1], (8, 128))
    return [view_x, jnp.where(sub == 0, edge, pltpu.roll(value, 1, 0))]


def high_views(field, k, u, x, halo, sub):
    gx_high, gy_high = halo
    value = field[u, 8 * x : 8 * x + 8]
    view_x = field[u, 8 * x + 8 : 8 * x + 16] if x < 3 else gx_high[3 * k + u]
    at = 12 * k + 4 * u + x
    edge = jnp.broadcast_to(gy_high[at : at + 1], (8, 128))
    return [view_x, jnp.where(sub == 7, edge, pltpu.roll(value, 7, 0))]


def low_along(value, tile, at, lane):
    return jnp.where(lane == 0, pltpu.roll(tile, (128 - at) % 128, 1), pltpu.roll(value, 1, 1))


def high_along(value, tile, at, lane):
    return jnp.where(lane == 127, pltpu.roll(tile, 127 - at, 1), pltpu.roll(value, 127, 1))


def place():
    at = lax.axis_index("gz")
    return lax.div(at, NEAR), lax.rem(at, NEAR)


FIRST = (5, 6, 4)


def slot_of(group, count, step):
    return (group + count - FIRST[step] % count) % count


def near_tiles(tiles):
    _, member = place()
    low, high = tiles[0], tiles[-1]
    for k in range(1, NEAR - 1):
        low = jnp.where(member == k + 1, tiles[k], low)
        high = jnp.where(member == k - 1, tiles[k], high)
    return low, high


def halo_tiles(near, slots, read, step):
    group, member = place()
    last = slots.shape[0] - 1
    below = jnp.where(group == 0, 0.0, read(slot_of(jnp.maximum(group - 1, 0), last + 1, step)))
    above = jnp.where(
        group == last, 0.0, read(slot_of(jnp.minimum(group + 1, last), last + 1, step))
    )
    return jnp.where(member == 0, below, near[0]), jnp.where(member == NEAR - 1, above, near[1])


def block_row(field, diag, off, u, rows):
    pick = ((None, 0, 1), (0, None, 2), (1, 2, None))[u]
    total = (diag[u, rows] - SHIFT) * field[u, rows]
    for t in range(3):
        if pick[t] is not None:
            total = total + off[pick[t], rows] * field[t, rows]
    return total


def first_kernel(right_any, mobility_any, cell_any, well_any, factor_any, table, *rest):
    faces, (right, mobility, cell, well, factor, sems) = rest[:4], rest[4:]
    copies = [
        pltpu.make_async_copy(source, target, sems.at[k])
        for k, (source, target) in enumerate(
            (
                (cell_any, cell),
                (right_any, right),
                (factor_any, factor),
                (well_any, well),
                (mobility_any, mobility),
            )
        )
    ]
    for copy in copies:
        copy.start()
    for copy in copies:
        copy.wait()
    row, lane = cell_masks(cell[0])
    values = gather_cells([right[u] for u in range(3)], row, lane)
    weight = factor[0]
    sums = scatter_wells([weight * v for v in values] + [weight], well_mask(well[0]))
    ends = fold(end_tile([(right, 0), (mobility, 32)], [(right, 16), (mobility, 48)]))
    for k in range(NEAR):
        put_well_rows(table.at[k], sums)
        table[k, 4 * WELL_ROWS : 24] = ends
    put_faces(faces, [right, mobility])


def first_near_kernel(slots, sent, near):
    rows = 4 * WELL_ROWS
    total = jnp.sum(slots[...], axis=0)
    tiles = [unfold(slots[k, rows:24]) for k in range(NEAR)]
    low, high = near_tiles(tiles)
    near[0], near[1] = low, high
    lane = lanes()
    ends = fold(jnp.where(lax.bitwise_and(lane, 31) < 16, tiles[-1], tiles[0]))
    for k in range(sent.shape[0]):
        sent[k, 0:rows] = total[0:rows]
        sent[k, rows:24] = ends


def near_kernel(slots, sent, near):
    total = jnp.sum(slots[...], axis=0)
    tiles = [slots[k, 16:24] for k in range(NEAR)]
    low, high = near_tiles(tiles)
    near[0], near[1] = low, high
    ends = jnp.where(lanes() < 16, tiles[-1], tiles[0])
    ends = fold_narrow(ends)
    for k in range(sent.shape[0]):
        for r in range(15):
            sent[k, r] = total[r : r + 1]
        for r in range(2):
            sent[k, 15 + r] = ends[r : r + 1]


def face_energy(below, above):
    step = pltpu.roll(above, 112, 1) - below
    return jnp.where(lanes() < 12, pltpu.roll(above, 96, 1) * step * step, 0.0)


def whole_sum(a):
    return jnp.sum(jnp.sum(a, axis=0, keepdims=True), axis=1, keepdims=True)


def last_near_kernel(slots, sent, near):
    total = jnp.sum(slots[...], axis=0)
    tiles = [slots[k, 16:24] for k in range(NEAR)]
    low, high = near_tiles(tiles)
    near[0], near[1] = low, high
    between = whole_sum(tree([face_energy(a, b) for a, b in zip(tiles, tiles[1:])]))
    line = total[15:16] + jnp.where(lanes()[0:1] == 5, between, 0.0)
    ends = jnp.where(lanes() < 16, tiles[-1], tiles[0])
    ends = fold(ends)
    for k in range(sent.shape[0]):
        for r in range(15):
            sent[k, r] = total[r : r + 1]
        sent[k, 15] = line
        for r in range(4):
            sent[k, 16 + r] = ends[r : r + 1]


def first_flow_kernel(right, mobility, diag, off, xl, yl, xh, yh, flow, cond):
    sub = lax.broadcasted_iota(jnp.int32, (8, 128), 0)
    for u in range(3):
        for x in range(4):
            rows = slice(8 * x, 8 * x + 8)
            total = block_row(right, diag, off, u, rows)
            value, own = right[u, rows], mobility[u, rows]
            near = low_views(right, 0, u, x, (xl, yl), sub)
            near += high_views(right, 0, u, x, (xh, yh), sub)
            near_mob = low_views(mobility, 1, u, x, (xl, yl), sub)
            near_mob += high_views(mobility, 1, u, x, (xh, yh), sub)
            for d in range(4):
                weight = 2.0 * own * near_mob[d] / (own + near_mob[d])
                cond[d, u, rows] = weight
                total = total + weight * (value - near[d])
            flow[u, rows] = total


def flow_kernel(field, diag, off, cond, xl, yl, xh, yh, flow):
    sub = lax.broadcasted_iota(jnp.int32, (8, 128), 0)
    for u in range(3):
        for x in range(4):
            rows = slice(8 * x, 8 * x + 8)
            total = block_row(field, diag, off, u, rows)
            value = field[u, rows]
            near = low_views(field, 0, u, x, (xl, yl), sub)
            near += high_views(field, 0, u, x, (xh, yh), sub)
            for d in range(4):
                total = total + cond[d, u, rows] * (value - near[d])
            flow[u, rows] = total


def flow_along(field, flow, cond, low, high):
    lane = lanes()
    out = []
    for u in range(3):
        blocks = []
        for x in range(4):
            rows = slice(8 * x, 8 * x + 8)
            value = field[u, rows]
            step_low = value - low_along(value, low, 4 * u + x, lane)
            step_high = value - high_along(value, high, 16 + 4 * u + x, lane)
            total = flow[u, rows] + cond[0, u, rows] * step_low
            blocks.append(total + cond[1, u, rows] * step_high)
        out.append(jnp.concatenate(blocks, 0))
    return out


def put_cond_along(cond, mobility, low, high):
    lane = lanes()
    for u in range(3):
        for x in range(4):
            rows = slice(8 * x, 8 * x + 8)
            own = mobility[u, rows]
            near = low_along(own, low, 32 + 4 * u + x, lane)
            cond[0, u, rows] = 2.0 * own * near / (own + near)
            near = high_along(own, high, 48 + 4 * u + x, lane)
            cond[1, u, rows] = 2.0 * own * near / (own + near)


def advance(means, flow, field, extra, weight, row, lane, wells):
    picked = gather_wells(means, wells)
    pulled = scatter_cells([weight * m for m in picked], row, lane)
    return [flow[u] + extra * field[u] - pulled[u] for u in range(3)]


def second_kernel(
    slots, near, flow, right, mobility, cell, well, factor,
    field, table, inverse, extra, cond, *faces
):
    total = jnp.sum(slots[...], axis=0)
    low, high = halo_tiles(near, slots, lambda k: unfold(slots[k, 4 * WELL_ROWS : 24]), 0)
    put_cond_along(cond, mobility, low, high)
    whole = flow_along(right, flow, cond, low, high)
    scale = 1.0 / (1.0 + total[3 * WELL_ROWS : 4 * WELL_ROWS])
    inverse[...] = jnp.zeros((8, 128), F32)
    inverse[0:WELL_ROWS] = scale
    rows = get_well_rows(total[: 3 * WELL_ROWS], 3)
    scale_row = get_well_rows(scale, 1)[0]
    row, lane = cell_masks(cell[0])
    wells = well_mask(well[0])
    weight = factor[0]
    own = scatter_cells([weight], row, lane)[0]
    extra[...] = own
    fresh = advance([r * scale_row for r in rows], whole, right, own, weight, row, lane, wells)
    for u in range(3):
        field[u] = fresh[u]
    values = gather_cells(fresh, row, lane)
    put_well_rows(table, scatter_wells([weight * v for v in values], wells))
    table[15:16] = jnp.zeros((1, 128), F32)
    table[16:24] = end_tile([(field, 0)], [(field, 16)])
    put_faces(faces, [field])


def third_kernel(
    slots, near, flow, before, extra, inverse, cond, cell, well, factor, field, table, *faces
):
    low, high = halo_tiles(near, slots, narrow_tile(slots), 1)
    whole = flow_along(before, flow, cond, low, high)
    scale_row = get_well_rows(inverse[...], 1)[0]
    rows = well_rows(slot_rows(slots, 0, 15))
    row, lane = cell_masks(cell[0])
    wells = well_mask(well[0])
    weight = factor[0]
    fresh = advance([r * scale_row for r in rows], whole, before, extra[...], weight, row, lane, wells)
    for u in range(3):
        field[u] = fresh[u]
    values = gather_cells(fresh, row, lane)
    put_well_rows(table, scatter_wells([weight * v for v in values], wells))
    table[15:16] = jnp.zeros((1, 128), F32)
    table[16:24] = end_tile([(field, 0)], [(field, 16), (cond.at[0], 32)])
    put_faces(faces, [field])


def tree(terms):
    while len(terms) > 1:
        pairs = [a + b for a, b in zip(terms[::2], terms[1::2])]
        terms = pairs + ([terms[-1]] if len(terms) % 2 else [])
    return terms[0]


def moment_kernel(wells_table, w0, w1, w2, extra, diag, off, cond, cond_along, xl, yl, table):
    lane, sub = lanes(), lax.broadcasted_iota(jnp.int32, (8, 128), 0)
    sums = [[] for _ in range(6)]
    for u in range(3):
        for x in range(4):
            rows = slice(8 * x, 8 * x + 8)
            a, b, c = w0[u, rows], w1[u, rows], w2[u, rows]
            for k, (p, q) in enumerate(((a, a), (a, b), (b, b), (b, c), (c, c))):
                sums[k].append(p * q)
            energy = c * (block_row(w2, diag, off, u, rows) + extra[rows] * c)
            for d, near in enumerate(low_views(w2, 0, u, x, (xl, yl), sub)):
                energy = energy + cond[d, u, rows] * (c - near) * (c - near)
            step = jnp.where(lane == 0, 0.0, c - pltpu.roll(c, 1, 1))
            sums[5].append(energy + cond_along[0, u, rows] * step * step)
    line = jnp.zeros((1, 128), F32)
    for k in range(6):
        line = jnp.where(lane[0:1] == k, whole_sum(tree(sums[k])), line)
    table[...] = wells_table[...]
    table[15:16] = line


def scalar_kernel(slots, inverse, sent):
    rows = slot_rows(slots, 0, 16)
    pull = tree([row * row * inverse[k % WELL_ROWS : k % WELL_ROWS + 1] for k, row in enumerate(rows[:15])])
    count = slots.shape[0]
    tiles = [wide_tile(slots)(slot_of(k, count, 2)) for k in range(count)]
    between = tree([face_energy(a, b) for a, b in zip(tiles, tiles[1:])])
    last = whole_sum(between) - whole_sum(pull)
    line = rows[15] + jnp.where(lanes()[0:1] == 5, last, 0.0)
    for k in range(sent.shape[0]):
        sent[k] = line


def plus(a, b, scale):
    size = max(len(a), len(b))
    out = []
    for k in range(size):
        p = a[k] if k < len(a) else None
        q = scale * b[k] if k < len(b) else None
        out.append(q if p is None else p if q is None else p + q)
    return out


def image_of(a):
    raised = [None] + list(a)
    return [
        SHIFT * a[0] if k == 0 else raised[k] + SHIFT * a[k] if k < len(a) else raised[k]
        for k in range(len(a) + 1)
    ]


def inner(a, b, moment):
    by_degree = {}
    for i, p in enumerate(a):
        for j, q in enumerate(b):
            by_degree[i + j] = by_degree.get(i + j, 0.0) + p * q
    return tree([by_degree[k] * moment[k] for k in sorted(by_degree)])


def combine_kernel(
    lines, slots, near, flow, extra, inverse, cond, cell, well, factor, w0, w1, w2, solved, rest
):
    low, high = halo_tiles(near, slots, wide_tile(slots), 2)
    whole = flow_along(w2, flow, cond, low, high)
    scale_row = get_well_rows(inverse[...], 1)[0]
    means = [r * scale_row for r in well_rows(slot_rows(slots, 0, 15))]
    row, lane = cell_masks(cell[0])
    w3 = advance(means, whole, w2, extra[...], factor[0], row, lane, well_mask(well[0]))

    line = tree([lines[k] for k in range(lines.shape[0])])
    first = lanes()[0:1]
    moment = [
        jnp.broadcast_to(jnp.sum(jnp.where(first == k, line, 0.0), axis=1, keepdims=True), (1, 128))
        for k in range(6)
    ]
    one = jnp.ones((1, 128), F32)
    residual, direction, solution_field = [one], [one], []
    norm = moment[0]
    for step in range(3):
        image = image_of(direction)
        alpha = norm / inner(direction, image, moment)
        solution_field = plus(solution_field, direction, alpha)
        residual = plus(residual, image, -alpha)
        if step < 2:
            fresh = inner(residual, residual, moment)
            direction = plus(residual, direction, fresh / norm)
            norm = fresh
    solution_field = [jnp.broadcast_to(c, (8, 128)) for c in solution_field]
    residual = [jnp.broadcast_to(c, (8, 128)) for c in residual]
    for u in range(3):
        for x in range(4):
            rows = slice(8 * x, 8 * x + 8)
            basis = [w0[u, rows], w1[u, rows], w2[u, rows], w3[u][rows]]
            solved[u, rows] = tree([c * w for c, w in zip(solution_field, basis)])
            rest[u, rows] = tree([c * w for c, w in zip(residual, basis)])


def call(kernel, shapes, *args, space=pltpu.VMEM, scratch=(), mib=32):
    return pl.pallas_call(
        kernel,
        out_shape=[jax.ShapeDtypeStruct(shape, F32) for shape in shapes],
        in_specs=[pl.BlockSpec(memory_space=space)] * len(args),
        out_specs=[pl.BlockSpec(memory_space=pltpu.VMEM)] * len(shapes),
        scratch_shapes=list(scratch),
        compiler_params=pltpu.CompilerParams(vmem_limit_bytes=mib * 1024 * 1024),
    )(*args)


NEAR = 4


def near_slots(sent):
    count = lax.axis_size("gz")
    groups = [[NEAR * g + k for k in range(NEAR)] for g in range(count // NEAR)]
    return lax.all_to_all(sent, "gz", 0, 0, axis_index_groups=groups)


def copies(table):
    return jnp.broadcast_to(table[None], (NEAR,) + table.shape)


def far_slots(sent, step):
    count = lax.axis_size("gz")
    slots = count // NEAR
    order = sorted(range(slots), key=lambda group: slot_of(group, slots, step))
    groups = [[g + NEAR * k for k in order] for g in range(NEAR)]
    return lax.all_to_all(sent, "gz", 0, 0, axis_index_groups=groups)


def forward(piece, axis):
    count = lax.axis_size(axis)
    return lax.ppermute(piece, axis, [(i, i + 1) for i in range(count - 1)])


def backward(piece, axis):
    count = lax.axis_size(axis)
    return lax.ppermute(piece, axis, [(i + 1, i) for i in range(count - 1)])


def low_halos(faces):
    return [forward(faces[0], "gx"), forward(faces[2], "gy")]


def high_halos(faces):
    return [backward(faces[1], "gx"), backward(faces[3], "gy")]


def after(first, *later):
    return lax.optimization_barrier((first, *later))


def face_shapes(fields):
    return [(3 * fields, 8, 128)] * 2 + [(12 * fields, 128)] * 2


def body(right_side, block_diag, block_off, mobility, perf_cell, perf_well, perf_factor):
    block = (3, 32, 128)
    right, diag, off, mob = (
        a.reshape(block) for a in (right_side, block_diag, block_off, mobility)
    )
    perfs = (perf_cell, perf_well, perf_factor)
    groups = lax.axis_size("gz") // NEAR
    near_shape = (2, 8, 128)

    table, *faces = call(
        first_kernel, [(NEAR, 24, 128)] + face_shapes(2), right, mob, *perfs,
        space=pltpu.HBM, mib=60,
        scratch=[pltpu.VMEM(block, F32)] * 2
        + [pltpu.VMEM(a.shape, a.dtype) for a in perfs]
        + [pltpu.SemaphoreType.DMA((5,))],
    )
    sent, near = call(first_near_kernel, [(groups, 24, 128), near_shape], near_slots(table))
    sent, *faces = after(sent, *faces)
    slots = far_slots(sent, 0)
    flow, cond = call(
        first_flow_kernel, [block, (4,) + block],
        right, mob, diag, off, *low_halos(faces), *high_halos(faces),
    )
    w1, table, inverse, extra, cond_along, *faces = call(
        second_kernel,
        [block, (24, 128), (8, 128), (32, 128), (2,) + block] + face_shapes(1),
        slots, near, flow, right, mob, *perfs,
    )

    sent, near = call(near_kernel, [(groups, 17, 1, 128), near_shape], near_slots(copies(table)))
    sent, *faces = after(sent, *faces)
    slots = far_slots(sent, 1)
    flow = call(
        flow_kernel, [block], w1, diag, off, cond, *low_halos(faces), *high_halos(faces)
    )[0]
    w2, table, *faces = call(
        third_kernel, [block, (24, 128)] + face_shapes(1),
        slots, near, flow, w1, extra, inverse, cond_along, *perfs,
    )

    low = low_halos(faces)
    table = call(
        moment_kernel, [(24, 128)],
        table, right, w1, w2, extra, diag, off, cond, cond_along, *low,
    )[0]
    sent, near = call(last_near_kernel, [(groups, 20, 1, 128), near_shape], near_slots(copies(table)))
    sent, *faces = after(sent, *faces)
    slots = far_slots(sent, 2)
    high = high_halos(faces)
    flow = call(flow_kernel, [block], w2, diag, off, cond, *low, *high)[0]
    slots, flow = after(slots, flow)

    count = lax.axis_size("gx") * lax.axis_size("gy")
    sent = call(scalar_kernel, [(count, 1, 128)], slots, inverse)[0]
    lines = lax.all_to_all(sent, ("gx", "gy"), 0, 0)
    solved, rest = call(
        combine_kernel, [block, block],
        lines, slots, near, flow, extra, inverse, cond_along, *perfs, right, w1, w2,
    )
    return solved.reshape(right_side.shape), rest.reshape(right_side.shape)


def solution(mesh):
    field = P(None, "gx", "gy", "gz")
    perf = P("gx", "gy", "gz")
    return jax.shard_map(
        body,
        mesh=mesh,
        in_specs=(field, field, field, field, perf, perf, perf),
        out_specs=(field, field),
        check_vma=False,
    )
```

```python
import jax
import jax.numpy as jnp
from jax import lax
from jax.experimental import pallas as pl
from jax.experimental.pallas import tpu as pltpu
from jax.sharding import PartitionSpec as P

W_COL = 640
WELL_ROWS = W_COL // 128
SHIFT = 8.0
F32 = jnp.float32
BF16 = jnp.bfloat16


def split3(a):
    first = a.astype(BF16)
    rest = a - first.astype(F32)
    second = rest.astype(BF16)
    third = (rest - second.astype(F32)).astype(BF16)
    return [first, second, third]


def sum3(a, rows):
    return a[:rows] + a[rows : 2 * rows] + a[2 * rows : 3 * rows]


def one_hot(index, rows):
    ids = lax.broadcasted_iota(jnp.int32, (rows, index.shape[1]), 0)
    return ids == index


def cell_masks(cell):
    row = one_hot(lax.shift_right_logical(cell, 7), 32).astype(F32)
    lane = one_hot(lax.bitwise_and(cell, 127), 128).astype(F32).astype(BF16)
    return row, lane


def well_mask(well):
    return one_hot(well, W_COL).astype(F32).astype(BF16)


def gather_cells(fields, row, lane):
    parts = [part for field in fields for part in split3(field)]
    picked = jnp.dot(jnp.concatenate(parts, 0), lane, preferred_element_type=F32)
    out = []
    for u in range(len(fields)):
        block = sum3(picked[96 * u : 96 * (u + 1)], 32)
        out.append(jnp.sum(block * row, axis=0, keepdims=True))
    return out


def scatter_cells(values, row, lane):
    parts = [part for value in values for part in split3(row * value)]
    placed = lax.dot_general(
        jnp.concatenate(parts, 0), lane, (((1,), (1,)), ((), ())), preferred_element_type=F32
    )
    return [sum3(placed[96 * u : 96 * (u + 1)], 32) for u in range(len(values))]


def scatter_wells(values, wells):
    count = len(values)
    stacked = jnp.concatenate(values + [jnp.zeros_like(values[0])] * (8 - count), 0)
    sums = lax.dot_general(
        jnp.concatenate(split3(stacked), 0), wells, (((1,), (1,)), ((), ())),
        preferred_element_type=F32,
    )
    sums = sum3(sums, 8)
    return [sums[u : u + 1] for u in range(count)]


def gather_wells(rows, wells):
    count = len(rows)
    stacked = jnp.concatenate(rows + [jnp.zeros_like(rows[0])] * (8 - count), 0)
    picked = sum3(jnp.dot(jnp.concatenate(split3(stacked), 0), wells, preferred_element_type=F32), 8)
    return [picked[u : u + 1] for u in range(count)]


def put_well_rows(ref, rows):
    for u, row in enumerate(rows):
        for j in range(WELL_ROWS):
            ref[u * WELL_ROWS + j : u * WELL_ROWS + j + 1, :] = row[:, 128 * j : 128 * (j + 1)]


def get_well_rows(table, count):
    out = []
    for u in range(count):
        pieces = [table[u * WELL_ROWS + j : u * WELL_ROWS + j + 1] for j in range(WELL_ROWS)]
        out.append(jnp.concatenate(pieces, 1))
    return out


def lanes():
    return lax.broadcasted_iota(jnp.int32, (8, 128), 1)


def put_faces(refs, fields):
    gx_high, gx_low, gy_high, gy_low = refs
    for k, field in enumerate(fields):
        for u in range(3):
            gx_high[3 * k + u] = field[u, 24:32]
            gx_low[3 * k + u] = field[u, 0:8]
            for x in range(4):
                at = 12 * k + 4 * u + x
                gy_high[at : at + 1] = field[u, 8 * x + 7 : 8 * x + 8]
                gy_low[at : at + 1] = field[u, 8 * x : 8 * x + 1]


def end_tile(highs, lows):
    lane = lanes()
    tile = jnp.zeros((8, 128), F32)
    for fields, turn in ((highs, 1), (lows, 0)):
        for field, start in fields:
            for u in range(3):
                for x in range(4):
                    at = start + 4 * u + x
                    value = pltpu.roll(field[u, 8 * x : 8 * x + 8], at + turn, 1)
                    tile = jnp.where(lane == at, value, tile)
    return tile


def fold(tile):
    return jnp.where(lanes()[0:4] < 64, tile[0:4], pltpu.roll(tile, 64, 1)[4:8])


def unfold(rows):
    return jnp.concatenate([rows, pltpu.roll(jnp.concatenate([rows, rows], 0), 64, 1)[0:4]], 0)


def fold_narrow(tile):
    kept = jnp.where(lanes() < 32, tile, 0.0)
    turned = [kept[0:2]] + [pltpu.roll(kept, 32 * k, 1)[2 * k : 2 * k + 2] for k in (1, 2, 3)]
    return tree(turned)


def unfold_narrow(rows):
    sub = lax.broadcasted_iota(jnp.int32, (8, 128), 0)
    spread = jnp.concatenate(rows * 4, 0)
    tile = spread
    for k in (1, 2, 3):
        tile = jnp.where(sub >= 2 * k, pltpu.roll(spread, 128 - 32 * k, 1), tile)
    return tile


def slot_rows(slots, first, last):
    return [tree([slots[k, r] for k in range(slots.shape[0])]) for r in range(first, last)]


def well_rows(rows):
    return [
        jnp.concatenate(rows[u * WELL_ROWS : (u + 1) * WELL_ROWS], 1) for u in range(3)
    ]


def narrow_tile(slots):
    return lambda k: unfold_narrow([slots[k, 15], slots[k, 16]])


def wide_tile(slots):
    return lambda k: unfold(jnp.concatenate([slots[k, r] for r in range(16, 20)], 0))


def low_views(field, k, u, x, halo, sub):
    gx_low, gy_low = halo
    value = field[u, 8 * x : 8 * x + 8]
    view_x = field[u, 8 * x - 8 : 8 * x] if x else gx_low[3 * k + u]
    at = 12 * k + 4 * u + x
    edge = jnp.broadcast_to(gy_low[at : at + 1], (8, 128))
    return [view_x, jnp.where(sub == 0, edge, pltpu.roll(value, 1, 0))]


def high_views(field, k, u, x, halo, sub):
    gx_high, gy_high = halo
    value = field[u, 8 * x : 8 * x + 8]
    view_x = field[u, 8 * x + 8 : 8 * x + 16] if x < 3 else gx_high[3 * k + u]
    at = 12 * k + 4 * u + x
    edge = jnp.broadcast_to(gy_high[at : at + 1], (8, 128))
    return [view_x, jnp.where(sub == 7, edge, pltpu.roll(value, 7, 0))]


def low_along(value, tile, at, lane):
    return jnp.where(lane == 0, pltpu.roll(tile, (128 - at) % 128, 1), pltpu.roll(value, 1, 1))


def high_along(value, tile, at, lane):
    return jnp.where(lane == 127, pltpu.roll(tile, 127 - at, 1), pltpu.roll(value, 127, 1))


def place():
    at = lax.axis_index("gz")
    return lax.div(at, NEAR), lax.rem(at, NEAR)


FIRST = (5, 6, 4)


def slot_of(group, count, step):
    return (group + count - FIRST[step] % count) % count


def near_tiles(tiles):
    _, member = place()
    low, high = tiles[0], tiles[-1]
    for k in range(1, NEAR - 1):
        low = jnp.where(member == k + 1, tiles[k], low)
        high = jnp.where(member == k - 1, tiles[k], high)
    return low, high


def halo_tiles(near, slots, read, step):
    group, member = place()
    last = slots.shape[0] - 1
    below = jnp.where(group == 0, 0.0, read(slot_of(jnp.maximum(group - 1, 0), last + 1, step)))
    above = jnp.where(
        group == last, 0.0, read(slot_of(jnp.minimum(group + 1, last), last + 1, step))
    )
    return jnp.where(member == 0, below, near[0]), jnp.where(member == NEAR - 1, above, near[1])


def block_row(field, diag, off, u, rows):
    pick = ((None, 0, 1), (0, None, 2), (1, 2, None))[u]
    total = (diag[u, rows] - SHIFT) * field[u, rows]
    for t in range(3):
        if pick[t] is not None:
            total = total + off[pick[t], rows] * field[t, rows]
    return total


def first_kernel(right_any, mobility_any, cell_any, well_any, factor_any, table, *rest):
    faces, (right, mobility, cell, well, factor, sems) = rest[:4], rest[4:]
    copies = [
        pltpu.make_async_copy(source, target, sems.at[k])
        for k, (source, target) in enumerate(
            (
                (cell_any, cell),
                (right_any, right),
                (factor_any, factor),
                (well_any, well),
                (mobility_any, mobility),
            )
        )
    ]
    for copy in copies:
        copy.start()
    for copy in copies:
        copy.wait()
    row, lane = cell_masks(cell[0])
    values = gather_cells([right[u] for u in range(3)], row, lane)
    weight = factor[0]
    sums = scatter_wells([weight * v for v in values] + [weight], well_mask(well[0]))
    ends = fold(end_tile([(right, 0), (mobility, 32)], [(right, 16), (mobility, 48)]))
    for k in range(NEAR):
        put_well_rows(table.at[k], sums)
        table[k, 4 * WELL_ROWS : 24] = ends
    put_faces(faces, [right, mobility])


def first_near_kernel(slots, sent, near):
    rows = 4 * WELL_ROWS
    total = jnp.sum(slots[...], axis=0)
    tiles = [unfold(slots[k, rows:24]) for k in range(NEAR)]
    low, high = near_tiles(tiles)
    near[0], near[1] = low, high
    lane = lanes()
    ends = fold(jnp.where(lax.bitwise_and(lane, 31) < 16, tiles[-1], tiles[0]))
    for k in range(sent.shape[0]):
        sent[k, 0:rows] = total[0:rows]
        sent[k, rows:24] = ends


def near_kernel(slots, sent, near):
    total = jnp.sum(slots[...], axis=0)
    tiles = [slots[k, 16:24] for k in range(NEAR)]
    low, high = near_tiles(tiles)
    near[0], near[1] = low, high
    ends = jnp.where(lanes() < 16, tiles[-1], tiles[0])
    ends = fold_narrow(ends)
    for k in range(sent.shape[0]):
        for r in range(15):
            sent[k, r] = total[r : r + 1]
        for r in range(2):
            sent[k, 15 + r] = ends[r : r + 1]


def face_energy(below, above):
    step = pltpu.roll(above, 112, 1) - below
    return jnp.where(lanes() < 12, pltpu.roll(above, 96, 1) * step * step, 0.0)


def whole_sum(a):
    return jnp.sum(jnp.sum(a, axis=0, keepdims=True), axis=1, keepdims=True)


def last_near_kernel(slots, sent, near):
    total = jnp.sum(slots[...], axis=0)
    tiles = [slots[k, 16:24] for k in range(NEAR)]
    low, high = near_tiles(tiles)
    near[0], near[1] = low, high
    between = whole_sum(tree([face_energy(a, b) for a, b in zip(tiles, tiles[1:])]))
    line = total[15:16] + jnp.where(lanes()[0:1] == 5, between, 0.0)
    ends = jnp.where(lanes() < 16, tiles[-1], tiles[0])
    ends = fold(ends)
    for k in range(sent.shape[0]):
        for r in range(15):
            sent[k, r] = total[r : r + 1]
        sent[k, 15] = line
        for r in range(4):
            sent[k, 16 + r] = ends[r : r + 1]


def first_flow_kernel(right, mobility, diag, off, xl, yl, xh, yh, flow, cond):
    sub = lax.broadcasted_iota(jnp.int32, (8, 128), 0)
    for u in range(3):
        for x in range(4):
            rows = slice(8 * x, 8 * x + 8)
            total = block_row(right, diag, off, u, rows)
            value, own = right[u, rows], mobility[u, rows]
            near = low_views(right, 0, u, x, (xl, yl), sub)
            near += high_views(right, 0, u, x, (xh, yh), sub)
            near_mob = low_views(mobility, 1, u, x, (xl, yl), sub)
            near_mob += high_views(mobility, 1, u, x, (xh, yh), sub)
            for d in range(4):
                weight = 2.0 * own * near_mob[d] / (own + near_mob[d])
                cond[d, u, rows] = weight
                total = total + weight * (value - near[d])
            flow[u, rows] = total


def flow_kernel(field, diag, off, cond, xl, yl, xh, yh, flow):
    sub = lax.broadcasted_iota(jnp.int32, (8, 128), 0)
    for u in range(3):
        for x in range(4):
            rows = slice(8 * x, 8 * x + 8)
            total = block_row(field, diag, off, u, rows)
            value = field[u, rows]
            near = low_views(field, 0, u, x, (xl, yl), sub)
            near += high_views(field, 0, u, x, (xh, yh), sub)
            for d in range(4):
                total = total + cond[d, u, rows] * (value - near[d])
            flow[u, rows] = total


def flow_along(field, flow, cond, low, high):
    lane = lanes()
    out = []
    for u in range(3):
        blocks = []
        for x in range(4):
            rows = slice(8 * x, 8 * x + 8)
            value = field[u, rows]
            step_low = value - low_along(value, low, 4 * u + x, lane)
            step_high = value - high_along(value, high, 16 + 4 * u + x, lane)
            total = flow[u, rows] + cond[0, u, rows] * step_low
            blocks.append(total + cond[1, u, rows] * step_high)
        out.append(jnp.concatenate(blocks, 0))
    return out


def put_cond_along(cond, mobility, low, high):
    lane = lanes()
    for u in range(3):
        for x in range(4):
            rows = slice(8 * x, 8 * x + 8)
            own = mobility[u, rows]
            near = low_along(own, low, 32 + 4 * u + x, lane)
            cond[0, u, rows] = 2.0 * own * near / (own + near)
            near = high_along(own, high, 48 + 4 * u + x, lane)
            cond[1, u, rows] = 2.0 * own * near / (own + near)


def advance(means, flow, field, extra, weight, row, lane, wells):
    picked = gather_wells(means, wells)
    pulled = scatter_cells([weight * m for m in picked], row, lane)
    return [flow[u] + extra * field[u] - pulled[u] for u in range(3)]


def second_kernel(
    slots, near, flow, right, mobility, cell, well, factor,
    field, table, inverse, extra, cond, *faces
):
    total = jnp.sum(slots[...], axis=0)
    low, high = halo_tiles(near, slots, lambda k: unfold(slots[k, 4 * WELL_ROWS : 24]), 0)
    put_cond_along(cond, mobility, low, high)
    whole = flow_along(right, flow, cond, low, high)
    scale = 1.0 / (1.0 + total[3 * WELL_ROWS : 4 * WELL_ROWS])
    inverse[...] = jnp.zeros((8, 128), F32)
    inverse[0:WELL_ROWS] = scale
    rows = get_well_rows(total[: 3 * WELL_ROWS], 3)
    scale_row = get_well_rows(scale, 1)[0]
    row, lane = cell_masks(cell[0])
    wells = well_mask(well[0])
    weight = factor[0]
    own = scatter_cells([weight], row, lane)[0]
    extra[...] = own
    fresh = advance([r * scale_row for r in rows], whole, right, own, weight, row, lane, wells)
    for u in range(3):
        field[u] = fresh[u]
    values = gather_cells(fresh, row, lane)
    put_well_rows(table, scatter_wells([weight * v for v in values], wells))
    table[15:16] = jnp.zeros((1, 128), F32)
    table[16:24] = end_tile([(field, 0)], [(field, 16)])
    put_faces(faces, [field])


def third_kernel(
    slots, near, flow, before, extra, inverse, cond, cell, well, factor, field, table, *faces
):
    low, high = halo_tiles(near, slots, narrow_tile(slots), 1)
    whole = flow_along(before, flow, cond, low, high)
    scale_row = get_well_rows(inverse[...], 1)[0]
    rows = well_rows(slot_rows(slots, 0, 15))
    row, lane = cell_masks(cell[0])
    wells = well_mask(well[0])
    weight = factor[0]
    fresh = advance([r * scale_row for r in rows], whole, before, extra[...], weight, row, lane, wells)
    for u in range(3):
        field[u] = fresh[u]
    values = gather_cells(fresh, row, lane)
    put_well_rows(table, scatter_wells([weight * v for v in values], wells))
    table[15:16] = jnp.zeros((1, 128), F32)
    table[16:24] = end_tile([(field, 0)], [(field, 16), (cond.at[0], 32)])
    put_faces(faces, [field])


def tree(terms):
    while len(terms) > 1:
        pairs = [a + b for a, b in zip(terms[::2], terms[1::2])]
        terms = pairs + ([terms[-1]] if len(terms) % 2 else [])
    return terms[0]


def moment_kernel(
    wells_table, w0, w1, w2, extra, diag, off, cond, cond_along, xl, yl, xh, yh, table, flow
):
    lane, sub = lanes(), lax.broadcasted_iota(jnp.int32, (8, 128), 0)
    sums = [[] for _ in range(6)]
    for u in range(3):
        for x in range(4):
            rows = slice(8 * x, 8 * x + 8)
            a, b, c = w0[u, rows], w1[u, rows], w2[u, rows]
            for k, (p, q) in enumerate(((a, a), (a, b), (b, b), (b, c), (c, c))):
                sums[k].append(p * q)
            total = block_row(w2, diag, off, u, rows)
            near = low_views(w2, 0, u, x, (xl, yl), sub)
            near += high_views(w2, 0, u, x, (xh, yh), sub)
            for d in range(4):
                total = total + cond[d, u, rows] * (c - near[d])
            flow[u, rows] = total
            energy = c * (total + extra[rows] * c)
            step = jnp.where(lane == 0, 0.0, c - pltpu.roll(c, 1, 1))
            sums[5].append(energy + cond_along[0, u, rows] * step * step)
    line = jnp.zeros((1, 128), F32)
    for k in range(6):
        line = jnp.where(lane[0:1] == k, whole_sum(tree(sums[k])), line)
    table[...] = wells_table[...]
    table[15:16] = line


def scalar_kernel(slots, inverse, sent):
    rows = slot_rows(slots, 0, 16)
    pull = tree([row * row * inverse[k % WELL_ROWS : k % WELL_ROWS + 1] for k, row in enumerate(rows[:15])])
    count = slots.shape[0]
    tiles = [wide_tile(slots)(slot_of(k, count, 2)) for k in range(count)]
    between = tree([face_energy(a, b) for a, b in zip(tiles, tiles[1:])])
    last = whole_sum(between) - whole_sum(pull)
    line = rows[15] + jnp.where(lanes()[0:1] == 5, last, 0.0)
    for k in range(sent.shape[0]):
        sent[k] = line


def plus(a, b, scale):
    size = max(len(a), len(b))
    out = []
    for k in range(size):
        p = a[k] if k < len(a) else None
        q = scale * b[k] if k < len(b) else None
        out.append(q if p is None else p if q is None else p + q)
    return out


def image_of(a):
    raised = [None] + list(a)
    return [
        SHIFT * a[0] if k == 0 else raised[k] + SHIFT * a[k] if k < len(a) else raised[k]
        for k in range(len(a) + 1)
    ]


def inner(a, b, moment):
    by_degree = {}
    for i, p in enumerate(a):
        for j, q in enumerate(b):
            by_degree[i + j] = by_degree.get(i + j, 0.0) + p * q
    return tree([by_degree[k] * moment[k] for k in sorted(by_degree)])


def combine_kernel(
    lines, slots, near, flow, extra, inverse, cond, cell, well, factor, w0, w1, w2, solved, rest
):
    low, high = halo_tiles(near, slots, wide_tile(slots), 2)
    whole = flow_along(w2, flow, cond, low, high)
    scale_row = get_well_rows(inverse[...], 1)[0]
    means = [r * scale_row for r in well_rows(slot_rows(slots, 0, 15))]
    row, lane = cell_masks(cell[0])
    w3 = advance(means, whole, w2, extra[...], factor[0], row, lane, well_mask(well[0]))

    line = tree([lines[k] for k in range(lines.shape[0])])
    first = lanes()[0:1]
    moment = [
        jnp.broadcast_to(jnp.sum(jnp.where(first == k, line, 0.0), axis=1, keepdims=True), (1, 128))
        for k in range(6)
    ]
    one = jnp.ones((1, 128), F32)
    residual, direction, solution_field = [one], [one], []
    norm = moment[0]
    for step in range(3):
        image = image_of(direction)
        alpha = norm / inner(direction, image, moment)
        solution_field = plus(solution_field, direction, alpha)
        residual = plus(residual, image, -alpha)
        if step < 2:
            fresh = inner(residual, residual, moment)
            direction = plus(residual, direction, fresh / norm)
            norm = fresh
    solution_field = [jnp.broadcast_to(c, (8, 128)) for c in solution_field]
    residual = [jnp.broadcast_to(c, (8, 128)) for c in residual]
    for u in range(3):
        for x in range(4):
            rows = slice(8 * x, 8 * x + 8)
            basis = [w0[u, rows], w1[u, rows], w2[u, rows], w3[u][rows]]
            solved[u, rows] = tree([c * w for c, w in zip(solution_field, basis)])
            rest[u, rows] = tree([c * w for c, w in zip(residual, basis)])


def call(kernel, shapes, *args, space=pltpu.VMEM, scratch=(), mib=32):
    return pl.pallas_call(
        kernel,
        out_shape=[jax.ShapeDtypeStruct(shape, F32) for shape in shapes],
        in_specs=[pl.BlockSpec(memory_space=space)] * len(args),
        out_specs=[pl.BlockSpec(memory_space=pltpu.VMEM)] * len(shapes),
        scratch_shapes=list(scratch),
        compiler_params=pltpu.CompilerParams(vmem_limit_bytes=mib * 1024 * 1024),
    )(*args)


NEAR = 4


def near_slots(sent):
    count = lax.axis_size("gz")
    groups = [[NEAR * g + k for k in range(NEAR)] for g in range(count // NEAR)]
    return lax.all_to_all(sent, "gz", 0, 0, axis_index_groups=groups)


def copies(table):
    return jnp.broadcast_to(table[None], (NEAR,) + table.shape)


def far_slots(sent, step):
    count = lax.axis_size("gz")
    slots = count // NEAR
    order = sorted(range(slots), key=lambda group: slot_of(group, slots, step))
    groups = [[g + NEAR * k for k in order] for g in range(NEAR)]
    return lax.all_to_all(sent, "gz", 0, 0, axis_index_groups=groups)


def forward(piece, axis):
    count = lax.axis_size(axis)
    return lax.ppermute(piece, axis, [(i, i + 1) for i in range(count - 1)])


def backward(piece, axis):
    count = lax.axis_size(axis)
    return lax.ppermute(piece, axis, [(i + 1, i) for i in range(count - 1)])


def low_halos(faces):
    return [forward(faces[0], "gx"), forward(faces[2], "gy")]


def high_halos(faces):
    return [backward(faces[1], "gx"), backward(faces[3], "gy")]


def after(first, *later):
    return lax.optimization_barrier((first, *later))


def face_shapes(fields):
    return [(3 * fields, 8, 128)] * 2 + [(12 * fields, 128)] * 2


def body(right_side, block_diag, block_off, mobility, perf_cell, perf_well, perf_factor):
    block = (3, 32, 128)
    right, diag, off, mob = (
        a.reshape(block) for a in (right_side, block_diag, block_off, mobility)
    )
    perfs = (perf_cell, perf_well, perf_factor)
    groups = lax.axis_size("gz") // NEAR
    near_shape = (2, 8, 128)

    table, *faces = call(
        first_kernel, [(NEAR, 24, 128)] + face_shapes(2), right, mob, *perfs,
        space=pltpu.HBM, mib=60,
        scratch=[pltpu.VMEM(block, F32)] * 2
        + [pltpu.VMEM(a.shape, a.dtype) for a in perfs]
        + [pltpu.SemaphoreType.DMA((5,))],
    )
    sent, near = call(first_near_kernel, [(groups, 24, 128), near_shape], near_slots(table))
    sent, *faces = after(sent, *faces)
    slots = far_slots(sent, 0)
    flow, cond = call(
        first_flow_kernel, [block, (4,) + block],
        right, mob, diag, off, *low_halos(faces), *high_halos(faces),
    )
    w1, table, inverse, extra, cond_along, *faces = call(
        second_kernel,
        [block, (24, 128), (8, 128), (32, 128), (2,) + block] + face_shapes(1),
        slots, near, flow, right, mob, *perfs,
    )

    sent, near = call(near_kernel, [(groups, 17, 1, 128), near_shape], near_slots(copies(table)))
    sent, *faces = after(sent, *faces)
    slots = far_slots(sent, 1)
    flow = call(
        flow_kernel, [block], w1, diag, off, cond, *low_halos(faces), *high_halos(faces)
    )[0]
    w2, table, *faces = call(
        third_kernel, [block, (24, 128)] + face_shapes(1),
        slots, near, flow, w1, extra, inverse, cond_along, *perfs,
    )

    table, flow = call(
        moment_kernel, [(24, 128), block],
        table, right, w1, w2, extra, diag, off, cond, cond_along,
        *low_halos(faces), *high_halos(faces),
    )
    sent, near = call(
        last_near_kernel, [(groups, 20, 1, 128), near_shape], near_slots(copies(table))
    )
    slots = far_slots(sent, 2)

    count = lax.axis_size("gx") * lax.axis_size("gy")
    sent = call(scalar_kernel, [(count, 1, 128)], slots, inverse)[0]
    lines = lax.all_to_all(sent, ("gx", "gy"), 0, 0)
    solved, rest = call(
        combine_kernel, [block, block],
        lines, slots, near, flow, extra, inverse, cond_along, *perfs, right, w1, w2,
    )
    return solved.reshape(right_side.shape), rest.reshape(right_side.shape)


def solution(mesh):
    field = P(None, "gx", "gy", "gz")
    perf = P("gx", "gy", "gz")
    return jax.shard_map(
        body,
        mesh=mesh,
        in_specs=(field, field, field, field, perf, perf, perf),
        out_specs=(field, field),
        check_vma=False,
    )
```

```python
import jax
import jax.numpy as jnp
from jax import lax
from jax.experimental import pallas as pl
from jax.experimental.pallas import tpu as pltpu
from jax.sharding import PartitionSpec as P

W_COL = 640
WELL_ROWS = W_COL // 128
SHIFT = 8.0
F32 = jnp.float32
BF16 = jnp.bfloat16


def split3(a):
    first = a.astype(BF16)
    rest = a - first.astype(F32)
    second = rest.astype(BF16)
    third = (rest - second.astype(F32)).astype(BF16)
    return [first, second, third]


def sum3(a, rows):
    return a[:rows] + a[rows : 2 * rows] + a[2 * rows : 3 * rows]


def one_hot(index, rows):
    ids = lax.broadcasted_iota(jnp.int32, (rows, index.shape[1]), 0)
    return ids == index


def cell_masks(cell):
    row = one_hot(lax.shift_right_logical(cell, 7), 32).astype(F32)
    lane = one_hot(lax.bitwise_and(cell, 127), 128).astype(F32).astype(BF16)
    return row, lane


def well_mask(well):
    return one_hot(well, W_COL).astype(F32).astype(BF16)


def gather_cells(fields, row, lane):
    parts = [part for field in fields for part in split3(field)]
    picked = jnp.dot(jnp.concatenate(parts, 0), lane, preferred_element_type=F32)
    out = []
    for u in range(len(fields)):
        block = sum3(picked[96 * u : 96 * (u + 1)], 32)
        out.append(jnp.sum(block * row, axis=0, keepdims=True))
    return out


def scatter_cells(values, row, lane):
    parts = [part for value in values for part in split3(row * value)]
    placed = lax.dot_general(
        jnp.concatenate(parts, 0), lane, (((1,), (1,)), ((), ())), preferred_element_type=F32
    )
    return [sum3(placed[96 * u : 96 * (u + 1)], 32) for u in range(len(values))]


def scatter_wells(values, wells):
    count = len(values)
    stacked = jnp.concatenate(values + [jnp.zeros_like(values[0])] * (8 - count), 0)
    sums = lax.dot_general(
        jnp.concatenate(split3(stacked), 0), wells, (((1,), (1,)), ((), ())),
        preferred_element_type=F32,
    )
    sums = sum3(sums, 8)
    return [sums[u : u + 1] for u in range(count)]


def gather_wells(rows, wells):
    count = len(rows)
    stacked = jnp.concatenate(rows + [jnp.zeros_like(rows[0])] * (8 - count), 0)
    picked = sum3(jnp.dot(jnp.concatenate(split3(stacked), 0), wells, preferred_element_type=F32), 8)
    return [picked[u : u + 1] for u in range(count)]


def put_well_rows(ref, rows):
    for u, row in enumerate(rows):
        for j in range(WELL_ROWS):
            ref[u * WELL_ROWS + j : u * WELL_ROWS + j + 1, :] = row[:, 128 * j : 128 * (j + 1)]


def get_well_rows(table, count):
    out = []
    for u in range(count):
        pieces = [table[u * WELL_ROWS + j : u * WELL_ROWS + j + 1] for j in range(WELL_ROWS)]
        out.append(jnp.concatenate(pieces, 1))
    return out


def lanes():
    return lax.broadcasted_iota(jnp.int32, (8, 128), 1)


def put_faces(refs, fields):
    gx_high, gx_low, gy_high, gy_low = refs
    for k, field in enumerate(fields):
        for u in range(3):
            gx_high[3 * k + u] = field[u, 24:32]
            gx_low[3 * k + u] = field[u, 0:8]
            for x in range(4):
                at = 12 * k + 4 * u + x
                gy_high[at : at + 1] = field[u, 8 * x + 7 : 8 * x + 8]
                gy_low[at : at + 1] = field[u, 8 * x : 8 * x + 1]


def end_tile(highs, lows):
    lane = lanes()
    tile = jnp.zeros((8, 128), F32)
    for fields, turn in ((highs, 1), (lows, 0)):
        for field, start in fields:
            for u in range(3):
                for x in range(4):
                    at = start + 4 * u + x
                    value = pltpu.roll(field[u, 8 * x : 8 * x + 8], at + turn, 1)
                    tile = jnp.where(lane == at, value, tile)
    return tile


def fold(tile):
    return jnp.where(lanes()[0:4] < 64, tile[0:4], pltpu.roll(tile, 64, 1)[4:8])


def unfold(rows):
    return jnp.concatenate([rows, pltpu.roll(jnp.concatenate([rows, rows], 0), 64, 1)[0:4]], 0)


def fold_narrow(tile):
    kept = jnp.where(lanes() < 32, tile, 0.0)
    turned = [kept[0:2]] + [pltpu.roll(kept, 32 * k, 1)[2 * k : 2 * k + 2] for k in (1, 2, 3)]
    return tree(turned)


def unfold_narrow(rows):
    sub = lax.broadcasted_iota(jnp.int32, (8, 128), 0)
    spread = jnp.concatenate(rows * 4, 0)
    tile = spread
    for k in (1, 2, 3):
        tile = jnp.where(sub >= 2 * k, pltpu.roll(spread, 128 - 32 * k, 1), tile)
    return tile


def slot_rows(slots, first, last):
    return [tree([slots[k, r] for k in range(slots.shape[0])]) for r in range(first, last)]


def well_rows(rows):
    return [
        jnp.concatenate(rows[u * WELL_ROWS : (u + 1) * WELL_ROWS], 1) for u in range(3)
    ]


def narrow_tile(slots):
    return lambda k: unfold_narrow([slots[k, 15], slots[k, 16]])


def wide_tile(slots):
    return lambda k: unfold(jnp.concatenate([slots[k, r] for r in range(16, 20)], 0))


def low_views(field, k, u, x, halo, sub):
    gx_low, gy_low = halo
    value = field[u, 8 * x : 8 * x + 8]
    view_x = field[u, 8 * x - 8 : 8 * x] if x else gx_low[3 * k + u]
    at = 12 * k + 4 * u + x
    edge = jnp.broadcast_to(gy_low[at : at + 1], (8, 128))
    return [view_x, jnp.where(sub == 0, edge, pltpu.roll(value, 1, 0))]


def high_views(field, k, u, x, halo, sub):
    gx_high, gy_high = halo
    value = field[u, 8 * x : 8 * x + 8]
    view_x = field[u, 8 * x + 8 : 8 * x + 16] if x < 3 else gx_high[3 * k + u]
    at = 12 * k + 4 * u + x
    edge = jnp.broadcast_to(gy_high[at : at + 1], (8, 128))
    return [view_x, jnp.where(sub == 7, edge, pltpu.roll(value, 7, 0))]


def low_along(value, tile, at, lane):
    return jnp.where(lane == 0, pltpu.roll(tile, (128 - at) % 128, 1), pltpu.roll(value, 1, 1))


def high_along(value, tile, at, lane):
    return jnp.where(lane == 127, pltpu.roll(tile, 127 - at, 1), pltpu.roll(value, 127, 1))


def place():
    at = lax.axis_index("gz")
    return lax.div(at, NEAR), lax.rem(at, NEAR)


FIRST = (5, 6, 4)


def slot_of(group, count, step):
    return (group + count - FIRST[step] % count) % count


def near_tiles(tiles):
    _, member = place()
    low, high = tiles[0], tiles[-1]
    for k in range(1, NEAR - 1):
        low = jnp.where(member == k + 1, tiles[k], low)
        high = jnp.where(member == k - 1, tiles[k], high)
    return low, high


def halo_tiles(near, slots, read, step):
    group, member = place()
    last = slots.shape[0] - 1
    below = jnp.where(group == 0, 0.0, read(slot_of(jnp.maximum(group - 1, 0), last + 1, step)))
    above = jnp.where(
        group == last, 0.0, read(slot_of(jnp.minimum(group + 1, last), last + 1, step))
    )
    return jnp.where(member == 0, below, near[0]), jnp.where(member == NEAR - 1, above, near[1])


def block_row(field, diag, off, u, rows):
    pick = ((None, 0, 1), (0, None, 2), (1, 2, None))[u]
    total = (diag[u, rows] - SHIFT) * field[u, rows]
    for t in range(3):
        if pick[t] is not None:
            total = total + off[pick[t], rows] * field[t, rows]
    return total


def first_kernel(right_any, mobility_any, cell_any, well_any, factor_any, table, *rest):
    faces, (right, mobility, cell, well, factor, sems) = rest[:4], rest[4:]
    copies = [
        pltpu.make_async_copy(source, target, sems.at[k])
        for k, (source, target) in enumerate(
            (
                (cell_any, cell),
                (right_any, right),
                (factor_any, factor),
                (well_any, well),
                (mobility_any, mobility),
            )
        )
    ]
    for copy in copies:
        copy.start()
    for copy in copies:
        copy.wait()
    row, lane = cell_masks(cell[0])
    values = gather_cells([right[u] for u in range(3)], row, lane)
    weight = factor[0]
    sums = scatter_wells([weight * v for v in values] + [weight], well_mask(well[0]))
    ends = fold(end_tile([(right, 0), (mobility, 32)], [(right, 16), (mobility, 48)]))
    for k in range(NEAR):
        put_well_rows(table.at[k], sums)
        table[k, 4 * WELL_ROWS : 24] = ends
    put_faces(faces, [right, mobility])


def first_near_kernel(slots, sent, near):
    rows = 4 * WELL_ROWS
    total = jnp.sum(slots[...], axis=0)
    tiles = [unfold(slots[k, rows:24]) for k in range(NEAR)]
    low, high = near_tiles(tiles)
    near[0], near[1] = low, high
    lane = lanes()
    ends = fold(jnp.where(lax.bitwise_and(lane, 31) < 16, tiles[-1], tiles[0]))
    for k in range(sent.shape[0]):
        sent[k, 0:rows] = total[0:rows]
        sent[k, rows:24] = ends


def near_kernel(slots, sent, near):
    total = jnp.sum(slots[...], axis=0)
    tiles = [slots[k, 16:24] for k in range(NEAR)]
    low, high = near_tiles(tiles)
    near[0], near[1] = low, high
    ends = jnp.where(lanes() < 16, tiles[-1], tiles[0])
    ends = fold_narrow(ends)
    for k in range(sent.shape[0]):
        for r in range(15):
            sent[k, r] = total[r : r + 1]
        for r in range(2):
            sent[k, 15 + r] = ends[r : r + 1]


def face_energy(below, above):
    step = pltpu.roll(above, 112, 1) - below
    return jnp.where(lanes() < 12, pltpu.roll(above, 96, 1) * step * step, 0.0)


def whole_sum(a):
    return jnp.sum(jnp.sum(a, axis=0, keepdims=True), axis=1, keepdims=True)


def last_near_kernel(slots, sent, near):
    total = jnp.sum(slots[...], axis=0)
    tiles = [slots[k, 16:24] for k in range(NEAR)]
    low, high = near_tiles(tiles)
    near[0], near[1] = low, high
    between = whole_sum(tree([face_energy(a, b) for a, b in zip(tiles, tiles[1:])]))
    line = total[15:16] + jnp.where(lanes()[0:1] == 5, between, 0.0)
    ends = jnp.where(lanes() < 16, tiles[-1], tiles[0])
    ends = fold(ends)
    for k in range(sent.shape[0]):
        for r in range(15):
            sent[k, r] = total[r : r + 1]
        sent[k, 15] = line
        for r in range(4):
            sent[k, 16 + r] = ends[r : r + 1]


def first_flow_kernel(right, mobility, diag, off, xl, yl, xh, yh, flow, cond):
    sub = lax.broadcasted_iota(jnp.int32, (8, 128), 0)
    for u in range(3):
        for x in range(4):
            rows = slice(8 * x, 8 * x + 8)
            total = block_row(right, diag, off, u, rows)
            value, own = right[u, rows], mobility[u, rows]
            near = low_views(right, 0, u, x, (xl, yl), sub)
            near += high_views(right, 0, u, x, (xh, yh), sub)
            near_mob = low_views(mobility, 1, u, x, (xl, yl), sub)
            near_mob += high_views(mobility, 1, u, x, (xh, yh), sub)
            for d in range(4):
                weight = 2.0 * own * near_mob[d] / (own + near_mob[d])
                cond[d, u, rows] = weight
                total = total + weight * (value - near[d])
            flow[u, rows] = total


def flow_kernel(field, diag, off, cond, xl, yl, xh, yh, flow):
    sub = lax.broadcasted_iota(jnp.int32, (8, 128), 0)
    for u in range(3):
        for x in range(4):
            rows = slice(8 * x, 8 * x + 8)
            total = block_row(field, diag, off, u, rows)
            value = field[u, rows]
            near = low_views(field, 0, u, x, (xl, yl), sub)
            near += high_views(field, 0, u, x, (xh, yh), sub)
            for d in range(4):
                total = total + cond[d, u, rows] * (value - near[d])
            flow[u, rows] = total


def flow_along(field, flow, cond, low, high):
    lane = lanes()
    out = []
    for u in range(3):
        blocks = []
        for x in range(4):
            rows = slice(8 * x, 8 * x + 8)
            value = field[u, rows]
            step_low = value - low_along(value, low, 4 * u + x, lane)
            step_high = value - high_along(value, high, 16 + 4 * u + x, lane)
            total = flow[u, rows] + cond[0, u, rows] * step_low
            blocks.append(total + cond[1, u, rows] * step_high)
        out.append(jnp.concatenate(blocks, 0))
    return out


def put_cond_along(cond, mobility, low, high):
    lane = lanes()
    for u in range(3):
        for x in range(4):
            rows = slice(8 * x, 8 * x + 8)
            own = mobility[u, rows]
            near = low_along(own, low, 32 + 4 * u + x, lane)
            cond[0, u, rows] = 2.0 * own * near / (own + near)
            near = high_along(own, high, 48 + 4 * u + x, lane)
            cond[1, u, rows] = 2.0 * own * near / (own + near)


def advance(means, flow, field, extra, weight, row, lane, wells):
    picked = gather_wells(means, wells)
    pulled = scatter_cells([weight * m for m in picked], row, lane)
    return [flow[u] + extra * field[u] - pulled[u] for u in range(3)]


def second_kernel(
    slots, near, flow, right, mobility, cell, well, factor,
    field, table, inverse, extra, cond, *faces
):
    total = jnp.sum(slots[...], axis=0)
    low, high = halo_tiles(near, slots, lambda k: unfold(slots[k, 4 * WELL_ROWS : 24]), 0)
    put_cond_along(cond, mobility, low, high)
    whole = flow_along(right, flow, cond, low, high)
    scale = 1.0 / (1.0 + total[3 * WELL_ROWS : 4 * WELL_ROWS])
    inverse[...] = jnp.zeros((8, 128), F32)
    inverse[0:WELL_ROWS] = scale
    rows = get_well_rows(total[: 3 * WELL_ROWS], 3)
    scale_row = get_well_rows(scale, 1)[0]
    row, lane = cell_masks(cell[0])
    wells = well_mask(well[0])
    weight = factor[0]
    own = scatter_cells([weight], row, lane)[0]
    extra[...] = own
    fresh = advance([r * scale_row for r in rows], whole, right, own, weight, row, lane, wells)
    for u in range(3):
        field[u] = fresh[u]
    values = gather_cells(fresh, row, lane)
    put_well_rows(table, scatter_wells([weight * v for v in values], wells))
    table[15:16] = jnp.zeros((1, 128), F32)
    table[16:24] = end_tile([(field, 0)], [(field, 16)])
    put_faces(faces, [field])


def third_kernel(
    slots, near, flow, before, extra, inverse, cond, cell, well, factor, field, table, *faces
):
    low, high = halo_tiles(near, slots, narrow_tile(slots), 1)
    whole = flow_along(before, flow, cond, low, high)
    scale_row = get_well_rows(inverse[...], 1)[0]
    rows = well_rows(slot_rows(slots, 0, 15))
    row, lane = cell_masks(cell[0])
    wells = well_mask(well[0])
    weight = factor[0]
    fresh = advance([r * scale_row for r in rows], whole, before, extra[...], weight, row, lane, wells)
    for u in range(3):
        field[u] = fresh[u]
    values = gather_cells(fresh, row, lane)
    put_well_rows(table, scatter_wells([weight * v for v in values], wells))
    table[15:16] = jnp.zeros((1, 128), F32)
    table[16:24] = end_tile([(field, 0)], [(field, 16), (cond.at[0], 32)])
    put_faces(faces, [field])


def tree(terms):
    while len(terms) > 1:
        pairs = [a + b for a, b in zip(terms[::2], terms[1::2])]
        terms = pairs + ([terms[-1]] if len(terms) % 2 else [])
    return terms[0]


def moment_kernel(wells_table, w0, w1, w2, extra, diag, off, cond, cond_along, xl, yl, table):
    lane, sub = lanes(), lax.broadcasted_iota(jnp.int32, (8, 128), 0)
    sums = [[] for _ in range(6)]
    for u in range(3):
        for x in range(4):
            rows = slice(8 * x, 8 * x + 8)
            a, b, c = w0[u, rows], w1[u, rows], w2[u, rows]
            for k, (p, q) in enumerate(((a, a), (a, b), (b, b), (b, c), (c, c))):
                sums[k].append(p * q)
            energy = c * (block_row(w2, diag, off, u, rows) + extra[rows] * c)
            for d, near in enumerate(low_views(w2, 0, u, x, (xl, yl), sub)):
                energy = energy + cond[d, u, rows] * (c - near) * (c - near)
            step = jnp.where(lane == 0, 0.0, c - pltpu.roll(c, 1, 1))
            sums[5].append(energy + cond_along[0, u, rows] * step * step)
    line = jnp.zeros((1, 128), F32)
    for k in range(6):
        line = jnp.where(lane[0:1] == k, whole_sum(tree(sums[k])), line)
    table[...] = wells_table[...]
    table[15:16] = line


def scalar_kernel(slots, inverse, sent):
    rows = slot_rows(slots, 0, 16)
    pull = tree([row * row * inverse[k % WELL_ROWS : k % WELL_ROWS + 1] for k, row in enumerate(rows[:15])])
    count = slots.shape[0]
    tiles = [wide_tile(slots)(slot_of(k, count, 2)) for k in range(count)]
    between = tree([face_energy(a, b) for a, b in zip(tiles, tiles[1:])])
    last = whole_sum(between) - whole_sum(pull)
    line = rows[15] + jnp.where(lanes()[0:1] == 5, last, 0.0)
    for k in range(sent.shape[0]):
        sent[k] = line


def plus(a, b, scale):
    size = max(len(a), len(b))
    out = []
    for k in range(size):
        p = a[k] if k < len(a) else None
        q = scale * b[k] if k < len(b) else None
        out.append(q if p is None else p if q is None else p + q)
    return out


def image_of(a):
    raised = [None] + list(a)
    return [
        SHIFT * a[0] if k == 0 else raised[k] + SHIFT * a[k] if k < len(a) else raised[k]
        for k in range(len(a) + 1)
    ]


def inner(a, b, moment):
    by_degree = {}
    for i, p in enumerate(a):
        for j, q in enumerate(b):
            by_degree[i + j] = by_degree.get(i + j, 0.0) + p * q
    return tree([by_degree[k] * moment[k] for k in sorted(by_degree)])


def combine_kernel(
    lines, slots, near, flow, extra, inverse, cond, cell, well, factor, w0, w1, w2, solved, rest
):
    low, high = halo_tiles(near, slots, wide_tile(slots), 2)
    whole = flow_along(w2, flow, cond, low, high)
    scale_row = get_well_rows(inverse[...], 1)[0]
    means = [r * scale_row for r in well_rows(slot_rows(slots, 0, 15))]
    row, lane = cell_masks(cell[0])
    w3 = advance(means, whole, w2, extra[...], factor[0], row, lane, well_mask(well[0]))

    line = tree([lines[k] for k in range(lines.shape[0])])
    first = lanes()[0:1]
    moment = [
        jnp.broadcast_to(jnp.sum(jnp.where(first == k, line, 0.0), axis=1, keepdims=True), (1, 128))
        for k in range(6)
    ]
    one = jnp.ones((1, 128), F32)
    residual, direction, solution_field = [one], [one], []
    norm = moment[0]
    for step in range(3):
        image = image_of(direction)
        alpha = norm / inner(direction, image, moment)
        solution_field = plus(solution_field, direction, alpha)
        residual = plus(residual, image, -alpha)
        if step < 2:
            fresh = inner(residual, residual, moment)
            direction = plus(residual, direction, fresh / norm)
            norm = fresh
    solution_field = [jnp.broadcast_to(c, (8, 128)) for c in solution_field]
    residual = [jnp.broadcast_to(c, (8, 128)) for c in residual]
    for u in range(3):
        for x in range(4):
            rows = slice(8 * x, 8 * x + 8)
            basis = [w0[u, rows], w1[u, rows], w2[u, rows], w3[u][rows]]
            solved[u, rows] = tree([c * w for c, w in zip(solution_field, basis)])
            rest[u, rows] = tree([c * w for c, w in zip(residual, basis)])


def call(kernel, shapes, *args, space=pltpu.VMEM, scratch=(), mib=32):
    return pl.pallas_call(
        kernel,
        out_shape=[jax.ShapeDtypeStruct(shape, F32) for shape in shapes],
        in_specs=[pl.BlockSpec(memory_space=space)] * len(args),
        out_specs=[pl.BlockSpec(memory_space=pltpu.VMEM)] * len(shapes),
        scratch_shapes=list(scratch),
        compiler_params=pltpu.CompilerParams(vmem_limit_bytes=mib * 1024 * 1024),
    )(*args)


NEAR = 4


def near_slots(sent):
    count = lax.axis_size("gz")
    groups = [[NEAR * g + k for k in range(NEAR)] for g in range(count // NEAR)]
    return lax.all_to_all(sent, "gz", 0, 0, axis_index_groups=groups)


def copies(table):
    return jnp.broadcast_to(table[None], (NEAR,) + table.shape)


def far_slots(sent, step):
    count = lax.axis_size("gz")
    slots = count // NEAR
    order = sorted(range(slots), key=lambda group: slot_of(group, slots, step))
    groups = [[g + NEAR * k for k in order] for g in range(NEAR)]
    return lax.all_to_all(sent, "gz", 0, 0, axis_index_groups=groups)


def forward(piece, axis):
    count = lax.axis_size(axis)
    return lax.ppermute(piece, axis, [(i, i + 1) for i in range(count - 1)])


def backward(piece, axis):
    count = lax.axis_size(axis)
    return lax.ppermute(piece, axis, [(i + 1, i) for i in range(count - 1)])


def low_halos(faces):
    return [forward(faces[0], "gx"), forward(faces[2], "gy")]


def high_halos(faces):
    return [backward(faces[1], "gx"), backward(faces[3], "gy")]


def after(first, *later):
    return lax.optimization_barrier((first, *later))


def face_shapes(fields):
    return [(3 * fields, 8, 128)] * 2 + [(12 * fields, 128)] * 2


def body(right_side, block_diag, block_off, mobility, perf_cell, perf_well, perf_factor):
    block = (3, 32, 128)
    right, diag, off, mob = (
        a.reshape(block) for a in (right_side, block_diag, block_off, mobility)
    )
    perfs = (perf_cell, perf_well, perf_factor)
    groups = lax.axis_size("gz") // NEAR
    near_shape = (2, 8, 128)

    table, *faces = call(
        first_kernel, [(NEAR, 24, 128)] + face_shapes(2), right, mob, *perfs,
        space=pltpu.HBM, mib=60,
        scratch=[pltpu.VMEM(block, F32)] * 2
        + [pltpu.VMEM(a.shape, a.dtype) for a in perfs]
        + [pltpu.SemaphoreType.DMA((5,))],
    )
    sent, near = call(first_near_kernel, [(groups, 24, 128), near_shape], near_slots(table))
    sent, *faces = after(sent, *faces)
    slots = far_slots(sent, 0)
    flow, cond = call(
        first_flow_kernel, [block, (4,) + block],
        right, mob, diag, off, *low_halos(faces), *high_halos(faces),
    )
    w1, table, inverse, extra, cond_along, *faces = call(
        second_kernel,
        [block, (24, 128), (8, 128), (32, 128), (2,) + block] + face_shapes(1),
        slots, near, flow, right, mob, *perfs,
    )

    sent, near = call(near_kernel, [(groups, 17, 1, 128), near_shape], near_slots(copies(table)))
    sent, *faces = after(sent, *faces)
    slots = far_slots(sent, 1)
    flow = call(
        flow_kernel, [block], w1, diag, off, cond, *low_halos(faces), *high_halos(faces)
    )[0]
    w2, table, *faces = call(
        third_kernel, [block, (24, 128)] + face_shapes(1),
        slots, near, flow, w1, extra, inverse, cond_along, *perfs,
    )

    low = low_halos(faces)
    table = call(
        moment_kernel, [(24, 128)],
        table, right, w1, w2, extra, diag, off, cond, cond_along, *low,
    )[0]
    sent, near = call(last_near_kernel, [(groups, 20, 1, 128), near_shape], near_slots(copies(table)))
    sent, *faces = after(sent, *faces)
    slots = far_slots(sent, 2)
    high = high_halos(faces)
    flow = call(flow_kernel, [block], w2, diag, off, cond, *low, *high)[0]
    slots, flow = after(slots, flow)

    count = lax.axis_size("gx") * lax.axis_size("gy")
    sent = call(scalar_kernel, [(count, 1, 128)], slots, inverse)[0]
    order = [[(k + count // 2 + lax.axis_size("gy") // 2) % count for k in range(count)]]
    lines = lax.all_to_all(sent, ("gx", "gy"), 0, 0, axis_index_groups=order)
    solved, rest = call(
        combine_kernel, [block, block],
        lines, slots, near, flow, extra, inverse, cond_along, *perfs, right, w1, w2,
    )
    return solved.reshape(right_side.shape), rest.reshape(right_side.shape)


def solution(mesh):
    field = P(None, "gx", "gy", "gz")
    perf = P("gx", "gy", "gz")
    return jax.shard_map(
        body,
        mesh=mesh,
        in_specs=(field, field, field, field, perf, perf, perf),
        out_specs=(field, field),
        check_vma=False,
    )
```

```python
import jax
import jax.numpy as jnp
from jax import lax
from jax.experimental import pallas as pl
from jax.experimental.pallas import tpu as pltpu
from jax.sharding import PartitionSpec as P

W_COL = 640
WELL_ROWS = W_COL // 128
SHIFT = 8.0
F32 = jnp.float32
BF16 = jnp.bfloat16


def split3(a):
    first = a.astype(BF16)
    rest = a - first.astype(F32)
    second = rest.astype(BF16)
    third = (rest - second.astype(F32)).astype(BF16)
    return [first, second, third]


def sum3(a, rows):
    return a[:rows] + a[rows : 2 * rows] + a[2 * rows : 3 * rows]


def one_hot(index, rows):
    ids = lax.broadcasted_iota(jnp.int32, (rows, index.shape[1]), 0)
    return ids == index


def cell_masks(cell):
    row = one_hot(lax.shift_right_logical(cell, 7), 32).astype(F32)
    lane = one_hot(lax.bitwise_and(cell, 127), 128).astype(F32).astype(BF16)
    return row, lane


def well_mask(well):
    return one_hot(well, W_COL).astype(F32).astype(BF16)


def gather_cells(fields, row, lane):
    parts = [part for field in fields for part in split3(field)]
    picked = jnp.dot(jnp.concatenate(parts, 0), lane, preferred_element_type=F32)
    out = []
    for u in range(len(fields)):
        block = sum3(picked[96 * u : 96 * (u + 1)], 32)
        out.append(jnp.sum(block * row, axis=0, keepdims=True))
    return out


def scatter_cells(values, row, lane):
    parts = [part for value in values for part in split3(row * value)]
    placed = lax.dot_general(
        jnp.concatenate(parts, 0), lane, (((1,), (1,)), ((), ())), preferred_element_type=F32
    )
    return [sum3(placed[96 * u : 96 * (u + 1)], 32) for u in range(len(values))]


def scatter_wells(values, wells):
    count = len(values)
    stacked = jnp.concatenate(values + [jnp.zeros_like(values[0])] * (8 - count), 0)
    sums = lax.dot_general(
        jnp.concatenate(split3(stacked), 0), wells, (((1,), (1,)), ((), ())),
        preferred_element_type=F32,
    )
    sums = sum3(sums, 8)
    return [sums[u : u + 1] for u in range(count)]


def gather_wells(rows, wells):
    count = len(rows)
    stacked = jnp.concatenate(rows + [jnp.zeros_like(rows[0])] * (8 - count), 0)
    picked = sum3(jnp.dot(jnp.concatenate(split3(stacked), 0), wells, preferred_element_type=F32), 8)
    return [picked[u : u + 1] for u in range(count)]


def put_well_rows(ref, rows):
    for u, row in enumerate(rows):
        for j in range(WELL_ROWS):
            ref[u * WELL_ROWS + j : u * WELL_ROWS + j + 1, :] = row[:, 128 * j : 128 * (j + 1)]


def get_well_rows(table, count):
    out = []
    for u in range(count):
        pieces = [table[u * WELL_ROWS + j : u * WELL_ROWS + j + 1] for j in range(WELL_ROWS)]
        out.append(jnp.concatenate(pieces, 1))
    return out


def lanes():
    return lax.broadcasted_iota(jnp.int32, (8, 128), 1)


def put_faces(refs, fields):
    gx_high, gx_low, gy_high, gy_low = refs
    for k, field in enumerate(fields):
        for u in range(3):
            gx_high[3 * k + u] = field[u, 24:32]
            gx_low[3 * k + u] = field[u, 0:8]
            for x in range(4):
                at = 12 * k + 4 * u + x
                gy_high[at : at + 1] = field[u, 8 * x + 7 : 8 * x + 8]
                gy_low[at : at + 1] = field[u, 8 * x : 8 * x + 1]


def end_tile(highs, lows):
    lane = lanes()
    tile = jnp.zeros((8, 128), F32)
    for fields, turn in ((highs, 1), (lows, 0)):
        for field, start in fields:
            for u in range(3):
                for x in range(4):
                    at = start + 4 * u + x
                    value = pltpu.roll(field[u, 8 * x : 8 * x + 8], at + turn, 1)
                    tile = jnp.where(lane == at, value, tile)
    return tile


def fold(tile):
    return jnp.where(lanes()[0:4] < 64, tile[0:4], pltpu.roll(tile, 64, 1)[4:8])


def unfold(rows):
    return jnp.concatenate([rows, pltpu.roll(jnp.concatenate([rows, rows], 0), 64, 1)[0:4]], 0)


def fold_narrow(tile):
    kept = jnp.where(lanes() < 32, tile, 0.0)
    turned = [kept[0:2]] + [pltpu.roll(kept, 32 * k, 1)[2 * k : 2 * k + 2] for k in (1, 2, 3)]
    return tree(turned)


def unfold_narrow(rows):
    sub = lax.broadcasted_iota(jnp.int32, (8, 128), 0)
    spread = jnp.concatenate(rows * 4, 0)
    tile = spread
    for k in (1, 2, 3):
        tile = jnp.where(sub >= 2 * k, pltpu.roll(spread, 128 - 32 * k, 1), tile)
    return tile


def slot_rows(slots, first, last):
    return [tree([slots[k, r] for k in range(slots.shape[0])]) for r in range(first, last)]


def well_rows(rows):
    return [
        jnp.concatenate(rows[u * WELL_ROWS : (u + 1) * WELL_ROWS], 1) for u in range(3)
    ]


def narrow_tile(slots):
    return lambda k: unfold_narrow([slots[k, 15], slots[k, 16]])


def wide_tile(slots):
    return lambda k: unfold(jnp.concatenate([slots[k, r] for r in range(16, 20)], 0))


def low_views(field, k, u, x, halo, sub):
    gx_low, gy_low = halo
    value = field[u, 8 * x : 8 * x + 8]
    view_x = field[u, 8 * x - 8 : 8 * x] if x else gx_low[3 * k + u]
    at = 12 * k + 4 * u + x
    edge = jnp.broadcast_to(gy_low[at : at + 1], (8, 128))
    return [view_x, jnp.where(sub == 0, edge, pltpu.roll(value, 1, 0))]


def high_views(field, k, u, x, halo, sub):
    gx_high, gy_high = halo
    value = field[u, 8 * x : 8 * x + 8]
    view_x = field[u, 8 * x + 8 : 8 * x + 16] if x < 3 else gx_high[3 * k + u]
    at = 12 * k + 4 * u + x
    edge = jnp.broadcast_to(gy_high[at : at + 1], (8, 128))
    return [view_x, jnp.where(sub == 7, edge, pltpu.roll(value, 7, 0))]


def low_along(value, tile, at, lane):
    return jnp.where(lane == 0, pltpu.roll(tile, (128 - at) % 128, 1), pltpu.roll(value, 1, 1))


def high_along(value, tile, at, lane):
    return jnp.where(lane == 127, pltpu.roll(tile, 127 - at, 1), pltpu.roll(value, 127, 1))


def place():
    at = lax.axis_index("gz")
    return lax.div(at, NEAR), lax.rem(at, NEAR)


FIRST = (5, 6, 4)


def slot_of(group, count, step):
    return (group + count - FIRST[step] % count) % count


def near_tiles(tiles):
    _, member = place()
    low, high = tiles[0], tiles[-1]
    for k in range(1, NEAR - 1):
        low = jnp.where(member == k + 1, tiles[k], low)
        high = jnp.where(member == k - 1, tiles[k], high)
    return low, high


def halo_tiles(near, slots, read, step):
    group, member = place()
    last = slots.shape[0] - 1
    below = jnp.where(group == 0, 0.0, read(slot_of(jnp.maximum(group - 1, 0), last + 1, step)))
    above = jnp.where(
        group == last, 0.0, read(slot_of(jnp.minimum(group + 1, last), last + 1, step))
    )
    return jnp.where(member == 0, below, near[0]), jnp.where(member == NEAR - 1, above, near[1])


def block_row(field, diag, off, u, rows):
    pick = ((None, 0, 1), (0, None, 2), (1, 2, None))[u]
    total = (diag[u, rows] - SHIFT) * field[u, rows]
    for t in range(3):
        if pick[t] is not None:
            total = total + off[pick[t], rows] * field[t, rows]
    return total


def first_kernel(right_any, mobility_any, cell_any, well_any, factor_any, table, *rest):
    faces, (right, mobility, cell, well, factor, sems) = rest[:4], rest[4:]
    copies = [
        pltpu.make_async_copy(source, target, sems.at[k])
        for k, (source, target) in enumerate(
            (
                (cell_any, cell),
                (right_any, right),
                (factor_any, factor),
                (well_any, well),
                (mobility_any, mobility),
            )
        )
    ]
    for copy in copies:
        copy.start()
    for copy in copies:
        copy.wait()
    row, lane = cell_masks(cell[0])
    values = gather_cells([right[u] for u in range(3)], row, lane)
    weight = factor[0]
    sums = scatter_wells([weight * v for v in values] + [weight], well_mask(well[0]))
    ends = fold(end_tile([(right, 0), (mobility, 32)], [(right, 16), (mobility, 48)]))
    for k in range(NEAR):
        put_well_rows(table.at[k], sums)
        table[k, 4 * WELL_ROWS : 24] = ends
    put_faces(faces, [right, mobility])


def first_near_kernel(slots, sent, near):
    rows = 4 * WELL_ROWS
    total = jnp.sum(slots[...], axis=0)
    tiles = [unfold(slots[k, rows:24]) for k in range(NEAR)]
    low, high = near_tiles(tiles)
    near[0], near[1] = low, high
    lane = lanes()
    ends = fold(jnp.where(lax.bitwise_and(lane, 31) < 16, tiles[-1], tiles[0]))
    for k in range(sent.shape[0]):
        sent[k, 0:rows] = total[0:rows]
        sent[k, rows:24] = ends


def near_kernel(slots, sent, near):
    total = jnp.sum(slots[...], axis=0)
    tiles = [slots[k, 16:24] for k in range(NEAR)]
    low, high = near_tiles(tiles)
    near[0], near[1] = low, high
    ends = jnp.where(lanes() < 16, tiles[-1], tiles[0])
    ends = fold_narrow(ends)
    for k in range(sent.shape[0]):
        for r in range(15):
            sent[k, r] = total[r : r + 1]
        for r in range(2):
            sent[k, 15 + r] = ends[r : r + 1]


def face_energy(below, above):
    step = pltpu.roll(above, 112, 1) - below
    return jnp.where(lanes() < 12, pltpu.roll(above, 96, 1) * step * step, 0.0)


def whole_sum(a):
    return jnp.sum(jnp.sum(a, axis=0, keepdims=True), axis=1, keepdims=True)


def last_near_kernel(slots, sent, near):
    total = jnp.sum(slots[...], axis=0)
    tiles = [slots[k, 16:24] for k in range(NEAR)]
    low, high = near_tiles(tiles)
    near[0], near[1] = low, high
    between = whole_sum(tree([face_energy(a, b) for a, b in zip(tiles, tiles[1:])]))
    line = total[15:16] + jnp.where(lanes()[0:1] == 5, between, 0.0)
    ends = jnp.where(lanes() < 16, tiles[-1], tiles[0])
    ends = fold(ends)
    for k in range(sent.shape[0]):
        for r in range(15):
            sent[k, r] = total[r : r + 1]
        sent[k, 15] = line
        for r in range(4):
            sent[k, 16 + r] = ends[r : r + 1]


def first_flow_kernel(right, mobility, diag, off, xl, yl, xh, yh, flow, cond):
    sub = lax.broadcasted_iota(jnp.int32, (8, 128), 0)
    for u in range(3):
        for x in range(4):
            rows = slice(8 * x, 8 * x + 8)
            total = block_row(right, diag, off, u, rows)
            value, own = right[u, rows], mobility[u, rows]
            near = low_views(right, 0, u, x, (xl, yl), sub)
            near += high_views(right, 0, u, x, (xh, yh), sub)
            near_mob = low_views(mobility, 1, u, x, (xl, yl), sub)
            near_mob += high_views(mobility, 1, u, x, (xh, yh), sub)
            for d in range(4):
                weight = 2.0 * own * near_mob[d] / (own + near_mob[d])
                cond[d, u, rows] = weight
                total = total + weight * (value - near[d])
            flow[u, rows] = total


def flow_kernel(field, diag, off, cond, xl, yl, xh, yh, flow):
    sub = lax.broadcasted_iota(jnp.int32, (8, 128), 0)
    for u in range(3):
        for x in range(4):
            rows = slice(8 * x, 8 * x + 8)
            total = block_row(field, diag, off, u, rows)
            value = field[u, rows]
            near = low_views(field, 0, u, x, (xl, yl), sub)
            near += high_views(field, 0, u, x, (xh, yh), sub)
            for d in range(4):
                total = total + cond[d, u, rows] * (value - near[d])
            flow[u, rows] = total


def flow_along(field, flow, cond, low, high):
    lane = lanes()
    out = []
    for u in range(3):
        blocks = []
        for x in range(4):
            rows = slice(8 * x, 8 * x + 8)
            value = field[u, rows]
            step_low = value - low_along(value, low, 4 * u + x, lane)
            step_high = value - high_along(value, high, 16 + 4 * u + x, lane)
            total = flow[u, rows] + cond[0, u, rows] * step_low
            blocks.append(total + cond[1, u, rows] * step_high)
        out.append(jnp.concatenate(blocks, 0))
    return out


def put_cond_along(cond, mobility, low, high):
    lane = lanes()
    for u in range(3):
        for x in range(4):
            rows = slice(8 * x, 8 * x + 8)
            own = mobility[u, rows]
            near = low_along(own, low, 32 + 4 * u + x, lane)
            cond[0, u, rows] = 2.0 * own * near / (own + near)
            near = high_along(own, high, 48 + 4 * u + x, lane)
            cond[1, u, rows] = 2.0 * own * near / (own + near)


def advance(means, flow, field, extra, weight, row, lane, wells):
    picked = gather_wells(means, wells)
    pulled = scatter_cells([weight * m for m in picked], row, lane)
    return [flow[u] + extra * field[u] - pulled[u] for u in range(3)]


def second_kernel(
    slots, near, flow, right, mobility, cell, well, factor,
    field, table, inverse, extra, cond, *faces
):
    total = jnp.sum(slots[...], axis=0)
    low, high = halo_tiles(near, slots, lambda k: unfold(slots[k, 4 * WELL_ROWS : 24]), 0)
    put_cond_along(cond, mobility, low, high)
    whole = flow_along(right, flow, cond, low, high)
    scale = 1.0 / (1.0 + total[3 * WELL_ROWS : 4 * WELL_ROWS])
    inverse[...] = jnp.zeros((8, 128), F32)
    inverse[0:WELL_ROWS] = scale
    rows = get_well_rows(total[: 3 * WELL_ROWS], 3)
    scale_row = get_well_rows(scale, 1)[0]
    row, lane = cell_masks(cell[0])
    wells = well_mask(well[0])
    weight = factor[0]
    own = scatter_cells([weight], row, lane)[0]
    extra[...] = own
    fresh = advance([r * scale_row for r in rows], whole, right, own, weight, row, lane, wells)
    for u in range(3):
        field[u] = fresh[u]
    values = gather_cells(fresh, row, lane)
    put_well_rows(table, scatter_wells([weight * v for v in values], wells))
    table[15:16] = jnp.zeros((1, 128), F32)
    table[16:24] = end_tile([(field, 0)], [(field, 16)])
    put_faces(faces, [field])


def third_kernel(
    slots, near, flow, before, extra, inverse, cond, cell, well, factor, field, table, *faces
):
    low, high = halo_tiles(near, slots, narrow_tile(slots), 1)
    whole = flow_along(before, flow, cond, low, high)
    scale_row = get_well_rows(inverse[...], 1)[0]
    rows = well_rows(slot_rows(slots, 0, 15))
    row, lane = cell_masks(cell[0])
    wells = well_mask(well[0])
    weight = factor[0]
    fresh = advance([r * scale_row for r in rows], whole, before, extra[...], weight, row, lane, wells)
    for u in range(3):
        field[u] = fresh[u]
    values = gather_cells(fresh, row, lane)
    put_well_rows(table, scatter_wells([weight * v for v in values], wells))
    table[15:16] = jnp.zeros((1, 128), F32)
    table[16:24] = end_tile([(field, 0)], [(field, 16), (cond.at[0], 32)])
    put_faces(faces, [field])


def tree(terms):
    while len(terms) > 1:
        pairs = [a + b for a, b in zip(terms[::2], terms[1::2])]
        terms = pairs + ([terms[-1]] if len(terms) % 2 else [])
    return terms[0]


def moment_kernel(wells_table, w0, w1, w2, extra, diag, off, cond, cond_along, xl, yl, table):
    lane, sub = lanes(), lax.broadcasted_iota(jnp.int32, (8, 128), 0)
    sums = [[] for _ in range(6)]
    for u in range(3):
        for x in range(4):
            rows = slice(8 * x, 8 * x + 8)
            a, b, c = w0[u, rows], w1[u, rows], w2[u, rows]
            for k, (p, q) in enumerate(((a, a), (a, b), (b, b), (b, c), (c, c))):
                sums[k].append(p * q)
            energy = c * (block_row(w2, diag, off, u, rows) + extra[rows] * c)
            for d, near in enumerate(low_views(w2, 0, u, x, (xl, yl), sub)):
                energy = energy + cond[d, u, rows] * (c - near) * (c - near)
            step = jnp.where(lane == 0, 0.0, c - pltpu.roll(c, 1, 1))
            sums[5].append(energy + cond_along[0, u, rows] * step * step)
    line = jnp.zeros((1, 128), F32)
    for k in range(6):
        line = jnp.where(lane[0:1] == k, whole_sum(tree(sums[k])), line)
    table[...] = wells_table[...]
    table[15:16] = line


def scalar_kernel(slots, inverse, sent):
    rows = slot_rows(slots, 0, 16)
    pull = tree([row * row * inverse[k % WELL_ROWS : k % WELL_ROWS + 1] for k, row in enumerate(rows[:15])])
    count = slots.shape[0]
    tiles = [wide_tile(slots)(slot_of(k, count, 2)) for k in range(count)]
    between = tree([face_energy(a, b) for a, b in zip(tiles, tiles[1:])])
    last = whole_sum(between) - whole_sum(pull)
    line = rows[15] + jnp.where(lanes()[0:1] == 5, last, 0.0)
    for k in range(sent.shape[0]):
        sent[k] = line


def plus(a, b, scale):
    size = max(len(a), len(b))
    out = []
    for k in range(size):
        p = a[k] if k < len(a) else None
        q = scale * b[k] if k < len(b) else None
        out.append(q if p is None else p if q is None else p + q)
    return out


def image_of(a):
    raised = [None] + list(a)
    return [
        SHIFT * a[0] if k == 0 else raised[k] + SHIFT * a[k] if k < len(a) else raised[k]
        for k in range(len(a) + 1)
    ]


def inner(a, b, moment):
    by_degree = {}
    for i, p in enumerate(a):
        for j, q in enumerate(b):
            by_degree[i + j] = by_degree.get(i + j, 0.0) + p * q
    return tree([by_degree[k] * moment[k] for k in sorted(by_degree)])


def combine_kernel(
    lines, slots, near, flow, extra, inverse, cond, cell, well, factor, w0, w1, w2, solved, rest
):
    low, high = halo_tiles(near, slots, wide_tile(slots), 2)
    whole = flow_along(w2, flow, cond, low, high)
    scale_row = get_well_rows(inverse[...], 1)[0]
    means = [r * scale_row for r in well_rows(slot_rows(slots, 0, 15))]
    row, lane = cell_masks(cell[0])
    w3 = advance(means, whole, w2, extra[...], factor[0], row, lane, well_mask(well[0]))

    line = tree([lines[k] for k in range(lines.shape[0])])
    first = lanes()[0:1]
    moment = [
        jnp.broadcast_to(jnp.sum(jnp.where(first == k, line, 0.0), axis=1, keepdims=True), (1, 128))
        for k in range(6)
    ]
    one = jnp.ones((1, 128), F32)
    residual, direction, solution_field = [one], [one], []
    norm = moment[0]
    for step in range(3):
        image = image_of(direction)
        alpha = norm / inner(direction, image, moment)
        solution_field = plus(solution_field, direction, alpha)
        residual = plus(residual, image, -alpha)
        if step < 2:
            fresh = inner(residual, residual, moment)
            direction = plus(residual, direction, fresh / norm)
            norm = fresh
    solution_field = [jnp.broadcast_to(c, (8, 128)) for c in solution_field]
    residual = [jnp.broadcast_to(c, (8, 128)) for c in residual]
    for u in range(3):
        for x in range(4):
            rows = slice(8 * x, 8 * x + 8)
            basis = [w0[u, rows], w1[u, rows], w2[u, rows], w3[u][rows]]
            solved[u, rows] = tree([c * w for c, w in zip(solution_field, basis)])
            rest[u, rows] = tree([c * w for c, w in zip(residual, basis)])


def call(kernel, shapes, *args, space=pltpu.VMEM, scratch=(), mib=32):
    return pl.pallas_call(
        kernel,
        out_shape=[jax.ShapeDtypeStruct(shape, F32) for shape in shapes],
        in_specs=[pl.BlockSpec(memory_space=space)] * len(args),
        out_specs=[pl.BlockSpec(memory_space=pltpu.VMEM)] * len(shapes),
        scratch_shapes=list(scratch),
        compiler_params=pltpu.CompilerParams(vmem_limit_bytes=mib * 1024 * 1024),
    )(*args)


NEAR = 4


def near_slots(sent):
    count = lax.axis_size("gz")
    groups = [[NEAR * g + k for k in range(NEAR)] for g in range(count // NEAR)]
    return lax.all_to_all(sent, "gz", 0, 0, axis_index_groups=groups)


def copies(table):
    return jnp.broadcast_to(table[None], (NEAR,) + table.shape)


def far_slots(sent, step):
    count = lax.axis_size("gz")
    slots = count // NEAR
    order = sorted(range(slots), key=lambda group: slot_of(group, slots, step))
    groups = [[g + NEAR * k for k in order] for g in range(NEAR)]
    return lax.all_to_all(sent, "gz", 0, 0, axis_index_groups=groups)


def forward(piece, axis):
    count = lax.axis_size(axis)
    return lax.ppermute(piece, axis, [(i, i + 1) for i in range(count - 1)])


def backward(piece, axis):
    count = lax.axis_size(axis)
    return lax.ppermute(piece, axis, [(i + 1, i) for i in range(count - 1)])


def low_halos(faces):
    return [forward(faces[0], "gx"), forward(faces[2], "gy")]


def high_halos(faces):
    return [backward(faces[1], "gx"), backward(faces[3], "gy")]


def after(first, *later):
    return lax.optimization_barrier((first, *later))


def face_shapes(fields):
    return [(3 * fields, 8, 128)] * 2 + [(12 * fields, 128)] * 2


def body(right_side, block_diag, block_off, mobility, perf_cell, perf_well, perf_factor):
    block = (3, 32, 128)
    right, diag, off, mob = (
        a.reshape(block) for a in (right_side, block_diag, block_off, mobility)
    )
    perfs = (perf_cell, perf_well, perf_factor)
    groups = lax.axis_size("gz") // NEAR
    near_shape = (2, 8, 128)

    table, *faces = call(
        first_kernel, [(NEAR, 24, 128)] + face_shapes(2), right, mob, *perfs,
        space=pltpu.HBM, mib=60,
        scratch=[pltpu.VMEM(block, F32)] * 2
        + [pltpu.VMEM(a.shape, a.dtype) for a in perfs]
        + [pltpu.SemaphoreType.DMA((5,))],
    )
    sent, near = call(first_near_kernel, [(groups, 24, 128), near_shape], near_slots(table))
    sent, *faces = after(sent, *faces)
    slots = far_slots(sent, 0)
    flow, cond = call(
        first_flow_kernel, [block, (4,) + block],
        right, mob, diag, off, *low_halos(faces), *high_halos(faces),
    )
    w1, table, inverse, extra, cond_along, *faces = call(
        second_kernel,
        [block, (24, 128), (8, 128), (32, 128), (2,) + block] + face_shapes(1),
        slots, near, flow, right, mob, *perfs,
    )

    sent, near = call(near_kernel, [(groups, 17, 1, 128), near_shape], near_slots(copies(table)))
    sent, *faces = after(sent, *faces)
    slots = far_slots(sent, 1)
    flow = call(
        flow_kernel, [block], w1, diag, off, cond, *low_halos(faces), *high_halos(faces)
    )[0]
    w2, table, *faces = call(
        third_kernel, [block, (24, 128)] + face_shapes(1),
        slots, near, flow, w1, extra, inverse, cond_along, *perfs,
    )

    low = low_halos(faces)
    table = call(
        moment_kernel, [(24, 128)],
        table, right, w1, w2, extra, diag, off, cond, cond_along, *low,
    )[0]
    sent, near = call(last_near_kernel, [(groups, 20, 1, 128), near_shape], near_slots(copies(table)))
    sent, *faces = after(sent, *faces)
    slots = far_slots(sent, 2)
    high = high_halos(faces)

    count = lax.axis_size("gx") * lax.axis_size("gy")
    sent = call(scalar_kernel, [(count, 1, 128)], slots, inverse)[0]
    order = [[(k + count // 2 + lax.axis_size("gy") // 2) % count for k in range(count)]]
    lines = lax.all_to_all(sent, ("gx", "gy"), 0, 0, axis_index_groups=order)
    lines, *high = after(lines, *high)
    flow = call(flow_kernel, [block], w2, diag, off, cond, *low, *high)[0]
    solved, rest = call(
        combine_kernel, [block, block],
        lines, slots, near, flow, extra, inverse, cond_along, *perfs, right, w1, w2,
    )
    return solved.reshape(right_side.shape), rest.reshape(right_side.shape)


def solution(mesh):
    field = P(None, "gx", "gy", "gz")
    perf = P("gx", "gy", "gz")
    return jax.shard_map(
        body,
        mesh=mesh,
        in_specs=(field, field, field, field, perf, perf, perf),
        out_specs=(field, field),
        check_vma=False,
    )
```

```python
import jax
import jax.numpy as jnp
from jax import lax
from jax.experimental import pallas as pl
from jax.experimental.pallas import tpu as pltpu
from jax.sharding import PartitionSpec as P

W_COL = 640
WELL_ROWS = W_COL // 128
SHIFT = 8.0
F32 = jnp.float32
BF16 = jnp.bfloat16


def split3(a):
    first = a.astype(BF16)
    rest = a - first.astype(F32)
    second = rest.astype(BF16)
    third = (rest - second.astype(F32)).astype(BF16)
    return [first, second, third]


def sum3(a, rows):
    return a[:rows] + a[rows : 2 * rows] + a[2 * rows : 3 * rows]


def one_hot(index, rows):
    ids = lax.broadcasted_iota(jnp.int32, (rows, index.shape[1]), 0)
    return ids == index


def cell_masks(cell):
    row = one_hot(lax.shift_right_logical(cell, 7), 32).astype(F32)
    lane = one_hot(lax.bitwise_and(cell, 127), 128).astype(F32).astype(BF16)
    return row, lane


def well_mask(well):
    return one_hot(well, W_COL).astype(F32).astype(BF16)


def gather_cells(fields, row, lane):
    parts = [part for field in fields for part in split3(field)]
    picked = jnp.dot(jnp.concatenate(parts, 0), lane, preferred_element_type=F32)
    out = []
    for u in range(len(fields)):
        block = sum3(picked[96 * u : 96 * (u + 1)], 32)
        out.append(jnp.sum(block * row, axis=0, keepdims=True))
    return out


def scatter_cells(values, row, lane):
    parts = [part for value in values for part in split3(row * value)]
    placed = lax.dot_general(
        jnp.concatenate(parts, 0), lane, (((1,), (1,)), ((), ())), preferred_element_type=F32
    )
    return [sum3(placed[96 * u : 96 * (u + 1)], 32) for u in range(len(values))]


def scatter_wells(values, wells):
    count = len(values)
    stacked = jnp.concatenate(values + [jnp.zeros_like(values[0])] * (8 - count), 0)
    sums = lax.dot_general(
        jnp.concatenate(split3(stacked), 0), wells, (((1,), (1,)), ((), ())),
        preferred_element_type=F32,
    )
    sums = sum3(sums, 8)
    return [sums[u : u + 1] for u in range(count)]


def gather_wells(rows, wells):
    count = len(rows)
    stacked = jnp.concatenate(rows + [jnp.zeros_like(rows[0])] * (8 - count), 0)
    picked = sum3(jnp.dot(jnp.concatenate(split3(stacked), 0), wells, preferred_element_type=F32), 8)
    return [picked[u : u + 1] for u in range(count)]


def put_well_rows(ref, rows):
    for u, row in enumerate(rows):
        for j in range(WELL_ROWS):
            ref[u * WELL_ROWS + j : u * WELL_ROWS + j + 1, :] = row[:, 128 * j : 128 * (j + 1)]


def get_well_rows(table, count):
    out = []
    for u in range(count):
        pieces = [table[u * WELL_ROWS + j : u * WELL_ROWS + j + 1] for j in range(WELL_ROWS)]
        out.append(jnp.concatenate(pieces, 1))
    return out


def lanes():
    return lax.broadcasted_iota(jnp.int32, (8, 128), 1)


def put_faces(refs, fields):
    gx_high, gx_low, gy_high, gy_low = refs
    for k, field in enumerate(fields):
        for u in range(3):
            gx_high[3 * k + u] = field[u, 24:32]
            gx_low[3 * k + u] = field[u, 0:8]
            for x in range(4):
                at = 12 * k + 4 * u + x
                gy_high[at : at + 1] = field[u, 8 * x + 7 : 8 * x + 8]
                gy_low[at : at + 1] = field[u, 8 * x : 8 * x + 1]


def end_tile(highs, lows):
    lane = lanes()
    tile = jnp.zeros((8, 128), F32)
    for fields, turn in ((highs, 1), (lows, 0)):
        for field, start in fields:
            for u in range(3):
                for x in range(4):
                    at = start + 4 * u + x
                    value = pltpu.roll(field[u, 8 * x : 8 * x + 8], at + turn, 1)
                    tile = jnp.where(lane == at, value, tile)
    return tile


def fold(tile):
    return jnp.where(lanes()[0:4] < 64, tile[0:4], pltpu.roll(tile, 64, 1)[4:8])


def unfold(rows):
    return jnp.concatenate([rows, pltpu.roll(jnp.concatenate([rows, rows], 0), 64, 1)[0:4]], 0)


def fold_narrow(tile):
    kept = jnp.where(lanes() < 32, tile, 0.0)
    turned = [kept[0:2]] + [pltpu.roll(kept, 32 * k, 1)[2 * k : 2 * k + 2] for k in (1, 2, 3)]
    return tree(turned)


def unfold_narrow(rows):
    sub = lax.broadcasted_iota(jnp.int32, (8, 128), 0)
    spread = jnp.concatenate(rows * 4, 0)
    tile = spread
    for k in (1, 2, 3):
        tile = jnp.where(sub >= 2 * k, pltpu.roll(spread, 128 - 32 * k, 1), tile)
    return tile


def slot_rows(slots, first, last):
    return [tree([slots[k, r] for k in range(slots.shape[0])]) for r in range(first, last)]


def well_rows(rows):
    return [
        jnp.concatenate(rows[u * WELL_ROWS : (u + 1) * WELL_ROWS], 1) for u in range(3)
    ]


def narrow_tile(slots):
    return lambda k: unfold_narrow([slots[k, 15], slots[k, 16]])


def wide_tile(slots):
    return lambda k: unfold(jnp.concatenate([slots[k, r] for r in range(16, 20)], 0))


def low_views(field, k, u, x, halo, sub):
    gx_low, gy_low = halo
    value = field[u, 8 * x : 8 * x + 8]
    view_x = field[u, 8 * x - 8 : 8 * x] if x else gx_low[3 * k + u]
    at = 12 * k + 4 * u + x
    edge = jnp.broadcast_to(gy_low[at : at + 1], (8, 128))
    return [view_x, jnp.where(sub == 0, edge, pltpu.roll(value, 1, 0))]


def high_views(field, k, u, x, halo, sub):
    gx_high, gy_high = halo
    value = field[u, 8 * x : 8 * x + 8]
    view_x = field[u, 8 * x + 8 : 8 * x + 16] if x < 3 else gx_high[3 * k + u]
    at = 12 * k + 4 * u + x
    edge = jnp.broadcast_to(gy_high[at : at + 1], (8, 128))
    return [view_x, jnp.where(sub == 7, edge, pltpu.roll(value, 7, 0))]


def low_along(value, tile, at, lane):
    return jnp.where(lane == 0, pltpu.roll(tile, (128 - at) % 128, 1), pltpu.roll(value, 1, 1))


def high_along(value, tile, at, lane):
    return jnp.where(lane == 127, pltpu.roll(tile, 127 - at, 1), pltpu.roll(value, 127, 1))


def place():
    at = lax.axis_index("gz")
    return lax.div(at, NEAR), lax.rem(at, NEAR)


FIRST = (5, 3, 4)


def slot_of(group, count, step):
    return (group + count - FIRST[step] % count) % count


def near_tiles(tiles):
    _, member = place()
    low, high = tiles[0], tiles[-1]
    for k in range(1, NEAR - 1):
        low = jnp.where(member == k + 1, tiles[k], low)
        high = jnp.where(member == k - 1, tiles[k], high)
    return low, high


def halo_tiles(near, slots, read, step):
    group, member = place()
    last = slots.shape[0] - 1
    below = jnp.where(group == 0, 0.0, read(slot_of(jnp.maximum(group - 1, 0), last + 1, step)))
    above = jnp.where(
        group == last, 0.0, read(slot_of(jnp.minimum(group + 1, last), last + 1, step))
    )
    return jnp.where(member == 0, below, near[0]), jnp.where(member == NEAR - 1, above, near[1])


def block_row(field, diag, off, u, rows):
    pick = ((None, 0, 1), (0, None, 2), (1, 2, None))[u]
    total = (diag[u, rows] - SHIFT) * field[u, rows]
    for t in range(3):
        if pick[t] is not None:
            total = total + off[pick[t], rows] * field[t, rows]
    return total


def first_kernel(right_any, mobility_any, cell_any, well_any, factor_any, table, *rest):
    faces, (right, mobility, cell, well, factor, sems) = rest[:4], rest[4:]
    copies = [
        pltpu.make_async_copy(source, target, sems.at[k])
        for k, (source, target) in enumerate(
            (
                (cell_any, cell),
                (right_any, right),
                (factor_any, factor),
                (well_any, well),
                (mobility_any, mobility),
            )
        )
    ]
    for copy in copies:
        copy.start()
    for copy in copies:
        copy.wait()
    row, lane = cell_masks(cell[0])
    values = gather_cells([right[u] for u in range(3)], row, lane)
    weight = factor[0]
    sums = scatter_wells([weight * v for v in values] + [weight], well_mask(well[0]))
    ends = fold(end_tile([(right, 0), (mobility, 32)], [(right, 16), (mobility, 48)]))
    for k in range(NEAR):
        put_well_rows(table.at[k], sums)
        table[k, 4 * WELL_ROWS : 24] = ends
    put_faces(faces, [right, mobility])


def first_near_kernel(slots, sent, near):
    rows = 4 * WELL_ROWS
    total = jnp.sum(slots[...], axis=0)
    tiles = [unfold(slots[k, rows:24]) for k in range(NEAR)]
    low, high = near_tiles(tiles)
    near[0], near[1] = low, high
    lane = lanes()
    ends = fold(jnp.where(lax.bitwise_and(lane, 31) < 16, tiles[-1], tiles[0]))
    for k in range(sent.shape[0]):
        sent[k, 0:rows] = total[0:rows]
        sent[k, rows:24] = ends


def near_kernel(slots, sent, near):
    total = jnp.sum(slots[...], axis=0)
    tiles = [slots[k, 16:24] for k in range(NEAR)]
    low, high = near_tiles(tiles)
    near[0], near[1] = low, high
    ends = jnp.where(lanes() < 16, tiles[-1], tiles[0])
    ends = fold_narrow(ends)
    for k in range(sent.shape[0]):
        for r in range(15):
            sent[k, r] = total[r : r + 1]
        for r in range(2):
            sent[k, 15 + r] = ends[r : r + 1]


def face_energy(below, above):
    step = pltpu.roll(above, 112, 1) - below
    return jnp.where(lanes() < 12, pltpu.roll(above, 96, 1) * step * step, 0.0)


def whole_sum(a):
    return jnp.sum(jnp.sum(a, axis=0, keepdims=True), axis=1, keepdims=True)


def last_near_kernel(slots, sent, near):
    total = jnp.sum(slots[...], axis=0)
    tiles = [slots[k, 16:24] for k in range(NEAR)]
    low, high = near_tiles(tiles)
    near[0], near[1] = low, high
    between = whole_sum(tree([face_energy(a, b) for a, b in zip(tiles, tiles[1:])]))
    line = total[15:16] + jnp.where(lanes()[0:1] == 5, between, 0.0)
    ends = jnp.where(lanes() < 16, tiles[-1], tiles[0])
    ends = fold(ends)
    for k in range(sent.shape[0]):
        for r in range(15):
            sent[k, r] = total[r : r + 1]
        sent[k, 15] = line
        for r in range(4):
            sent[k, 16 + r] = ends[r : r + 1]


def first_flow_kernel(right, mobility, diag, off, xl, yl, xh, yh, flow, cond):
    sub = lax.broadcasted_iota(jnp.int32, (8, 128), 0)
    for u in range(3):
        for x in range(4):
            rows = slice(8 * x, 8 * x + 8)
            total = block_row(right, diag, off, u, rows)
            value, own = right[u, rows], mobility[u, rows]
            near = low_views(right, 0, u, x, (xl, yl), sub)
            near += high_views(right, 0, u, x, (xh, yh), sub)
            near_mob = low_views(mobility, 1, u, x, (xl, yl), sub)
            near_mob += high_views(mobility, 1, u, x, (xh, yh), sub)
            for d in range(4):
                weight = 2.0 * own * near_mob[d] / (own + near_mob[d])
                cond[d, u, rows] = weight
                total = total + weight * (value - near[d])
            flow[u, rows] = total


def flow_kernel(field, diag, off, cond, xl, yl, xh, yh, flow):
    sub = lax.broadcasted_iota(jnp.int32, (8, 128), 0)
    for u in range(3):
        for x in range(4):
            rows = slice(8 * x, 8 * x + 8)
            total = block_row(field, diag, off, u, rows)
            value = field[u, rows]
            near = low_views(field, 0, u, x, (xl, yl), sub)
            near += high_views(field, 0, u, x, (xh, yh), sub)
            for d in range(4):
                total = total + cond[d, u, rows] * (value - near[d])
            flow[u, rows] = total


def flow_along(field, flow, cond, low, high):
    lane = lanes()
    out = []
    for u in range(3):
        blocks = []
        for x in range(4):
            rows = slice(8 * x, 8 * x + 8)
            value = field[u, rows]
            step_low = value - low_along(value, low, 4 * u + x, lane)
            step_high = value - high_along(value, high, 16 + 4 * u + x, lane)
            total = flow[u, rows] + cond[0, u, rows] * step_low
            blocks.append(total + cond[1, u, rows] * step_high)
        out.append(jnp.concatenate(blocks, 0))
    return out


def put_cond_along(cond, mobility, low, high):
    lane = lanes()
    for u in range(3):
        for x in range(4):
            rows = slice(8 * x, 8 * x + 8)
            own = mobility[u, rows]
            near = low_along(own, low, 32 + 4 * u + x, lane)
            cond[0, u, rows] = 2.0 * own * near / (own + near)
            near = high_along(own, high, 48 + 4 * u + x, lane)
            cond[1, u, rows] = 2.0 * own * near / (own + near)


def advance(means, flow, field, extra, weight, row, lane, wells):
    picked = gather_wells(means, wells)
    pulled = scatter_cells([weight * m for m in picked], row, lane)
    return [flow[u] + extra * field[u] - pulled[u] for u in range(3)]


def second_kernel(
    slots, near, flow, right, mobility, cell, well, factor,
    field, table, inverse, extra, cond, *faces
):
    total = jnp.sum(slots[...], axis=0)
    low, high = halo_tiles(near, slots, lambda k: unfold(slots[k, 4 * WELL_ROWS : 24]), 0)
    put_cond_along(cond, mobility, low, high)
    whole = flow_along(right, flow, cond, low, high)
    scale = 1.0 / (1.0 + total[3 * WELL_ROWS : 4 * WELL_ROWS])
    inverse[...] = jnp.zeros((8, 128), F32)
    inverse[0:WELL_ROWS] = scale
    rows = get_well_rows(total[: 3 * WELL_ROWS], 3)
    scale_row = get_well_rows(scale, 1)[0]
    row, lane = cell_masks(cell[0])
    wells = well_mask(well[0])
    weight = factor[0]
    own = scatter_cells([weight], row, lane)[0]
    extra[...] = own
    fresh = advance([r * scale_row for r in rows], whole, right, own, weight, row, lane, wells)
    for u in range(3):
        field[u] = fresh[u]
    values = gather_cells(fresh, row, lane)
    put_well_rows(table, scatter_wells([weight * v for v in values], wells))
    table[15:16] = jnp.zeros((1, 128), F32)
    table[16:24] = end_tile([(field, 0)], [(field, 16)])
    put_faces(faces, [field])


def third_kernel(
    slots, near, flow, before, extra, inverse, cond, cell, well, factor, field, table, *faces
):
    low, high = halo_tiles(near, slots, narrow_tile(slots), 1)
    whole = flow_along(before, flow, cond, low, high)
    scale_row = get_well_rows(inverse[...], 1)[0]
    rows = well_rows(slot_rows(slots, 0, 15))
    row, lane = cell_masks(cell[0])
    wells = well_mask(well[0])
    weight = factor[0]
    fresh = advance([r * scale_row for r in rows], whole, before, extra[...], weight, row, lane, wells)
    for u in range(3):
        field[u] = fresh[u]
    values = gather_cells(fresh, row, lane)
    put_well_rows(table, scatter_wells([weight * v for v in values], wells))
    table[15:16] = jnp.zeros((1, 128), F32)
    table[16:24] = end_tile([(field, 0)], [(field, 16), (cond.at[0], 32)])
    put_faces(faces, [field])


def tree(terms):
    while len(terms) > 1:
        pairs = [a + b for a, b in zip(terms[::2], terms[1::2])]
        terms = pairs + ([terms[-1]] if len(terms) % 2 else [])
    return terms[0]


def moment_kernel(wells_table, w0, w1, w2, extra, diag, off, cond, cond_along, xl, yl, table):
    lane, sub = lanes(), lax.broadcasted_iota(jnp.int32, (8, 128), 0)
    sums = [[] for _ in range(6)]
    for u in range(3):
        for x in range(4):
            rows = slice(8 * x, 8 * x + 8)
            a, b, c = w0[u, rows], w1[u, rows], w2[u, rows]
            for k, (p, q) in enumerate(((a, a), (a, b), (b, b), (b, c), (c, c))):
                sums[k].append(p * q)
            energy = c * (block_row(w2, diag, off, u, rows) + extra[rows] * c)
            for d, near in enumerate(low_views(w2, 0, u, x, (xl, yl), sub)):
                energy = energy + cond[d, u, rows] * (c - near) * (c - near)
            step = jnp.where(lane == 0, 0.0, c - pltpu.roll(c, 1, 1))
            sums[5].append(energy + cond_along[0, u, rows] * step * step)
    line = jnp.zeros((1, 128), F32)
    for k in range(6):
        line = jnp.where(lane[0:1] == k, whole_sum(tree(sums[k])), line)
    table[...] = wells_table[...]
    table[15:16] = line


def scalar_kernel(slots, inverse, sent):
    rows = slot_rows(slots, 0, 16)
    pull = tree([row * row * inverse[k % WELL_ROWS : k % WELL_ROWS + 1] for k, row in enumerate(rows[:15])])
    count = slots.shape[0]
    tiles = [wide_tile(slots)(slot_of(k, count, 2)) for k in range(count)]
    between = tree([face_energy(a, b) for a, b in zip(tiles, tiles[1:])])
    last = whole_sum(between) - whole_sum(pull)
    line = rows[15] + jnp.where(lanes()[0:1] == 5, last, 0.0)
    for k in range(sent.shape[0]):
        sent[k] = line


def plus(a, b, scale):
    size = max(len(a), len(b))
    out = []
    for k in range(size):
        p = a[k] if k < len(a) else None
        q = scale * b[k] if k < len(b) else None
        out.append(q if p is None else p if q is None else p + q)
    return out


def image_of(a):
    raised = [None] + list(a)
    return [
        SHIFT * a[0] if k == 0 else raised[k] + SHIFT * a[k] if k < len(a) else raised[k]
        for k in range(len(a) + 1)
    ]


def inner(a, b, moment):
    by_degree = {}
    for i, p in enumerate(a):
        for j, q in enumerate(b):
            by_degree[i + j] = by_degree.get(i + j, 0.0) + p * q
    return tree([by_degree[k] * moment[k] for k in sorted(by_degree)])


def combine_kernel(
    lines, slots, near, flow, extra, inverse, cond, cell, well, factor, w0, w1, w2, solved, rest
):
    low, high = halo_tiles(near, slots, wide_tile(slots), 2)
    whole = flow_along(w2, flow, cond, low, high)
    scale_row = get_well_rows(inverse[...], 1)[0]
    means = [r * scale_row for r in well_rows(slot_rows(slots, 0, 15))]
    row, lane = cell_masks(cell[0])
    w3 = advance(means, whole, w2, extra[...], factor[0], row, lane, well_mask(well[0]))

    line = tree([lines[k] for k in range(lines.shape[0])])
    first = lanes()[0:1]
    moment = [
        jnp.broadcast_to(jnp.sum(jnp.where(first == k, line, 0.0), axis=1, keepdims=True), (1, 128))
        for k in range(6)
    ]
    one = jnp.ones((1, 128), F32)
    residual, direction, solution_field = [one], [one], []
    norm = moment[0]
    for step in range(3):
        image = image_of(direction)
        alpha = norm / inner(direction, image, moment)
        solution_field = plus(solution_field, direction, alpha)
        residual = plus(residual, image, -alpha)
        if step < 2:
            fresh = inner(residual, residual, moment)
            direction = plus(residual, direction, fresh / norm)
            norm = fresh
    solution_field = [jnp.broadcast_to(c, (8, 128)) for c in solution_field]
    residual = [jnp.broadcast_to(c, (8, 128)) for c in residual]
    for u in range(3):
        for x in range(4):
            rows = slice(8 * x, 8 * x + 8)
            basis = [w0[u, rows], w1[u, rows], w2[u, rows], w3[u][rows]]
            solved[u, rows] = tree([c * w for c, w in zip(solution_field, basis)])
            rest[u, rows] = tree([c * w for c, w in zip(residual, basis)])


def call(kernel, shapes, *args, space=pltpu.VMEM, scratch=(), mib=32):
    return pl.pallas_call(
        kernel,
        out_shape=[jax.ShapeDtypeStruct(shape, F32) for shape in shapes],
        in_specs=[pl.BlockSpec(memory_space=space)] * len(args),
        out_specs=[pl.BlockSpec(memory_space=pltpu.VMEM)] * len(shapes),
        scratch_shapes=list(scratch),
        compiler_params=pltpu.CompilerParams(vmem_limit_bytes=mib * 1024 * 1024),
    )(*args)


NEAR = 4


def near_slots(sent):
    count = lax.axis_size("gz")
    groups = [[NEAR * g + k for k in range(NEAR)] for g in range(count // NEAR)]
    return lax.all_to_all(sent, "gz", 0, 0, axis_index_groups=groups)


def copies(table):
    return jnp.broadcast_to(table[None], (NEAR,) + table.shape)


def far_slots(sent, step):
    count = lax.axis_size("gz")
    slots = count // NEAR
    order = sorted(range(slots), key=lambda group: slot_of(group, slots, step))
    groups = [[g + NEAR * k for k in order] for g in range(NEAR)]
    return lax.all_to_all(sent, "gz", 0, 0, axis_index_groups=groups)


def forward(piece, axis):
    count = lax.axis_size(axis)
    return lax.ppermute(piece, axis, [(i, i + 1) for i in range(count - 1)])


def backward(piece, axis):
    count = lax.axis_size(axis)
    return lax.ppermute(piece, axis, [(i + 1, i) for i in range(count - 1)])


def low_halos(faces):
    return [forward(faces[0], "gx"), forward(faces[2], "gy")]


def high_halos(faces):
    return [backward(faces[1], "gx"), backward(faces[3], "gy")]


def after(first, *later):
    return lax.optimization_barrier((first, *later))


def face_shapes(fields):
    return [(3 * fields, 8, 128)] * 2 + [(12 * fields, 128)] * 2


def body(right_side, block_diag, block_off, mobility, perf_cell, perf_well, perf_factor):
    block = (3, 32, 128)
    right, diag, off, mob = (
        a.reshape(block) for a in (right_side, block_diag, block_off, mobility)
    )
    perfs = (perf_cell, perf_well, perf_factor)
    groups = lax.axis_size("gz") // NEAR
    near_shape = (2, 8, 128)

    table, *faces = call(
        first_kernel, [(NEAR, 24, 128)] + face_shapes(2), right, mob, *perfs,
        space=pltpu.HBM, mib=60,
        scratch=[pltpu.VMEM(block, F32)] * 2
        + [pltpu.VMEM(a.shape, a.dtype) for a in perfs]
        + [pltpu.SemaphoreType.DMA((5,))],
    )
    sent, near = call(first_near_kernel, [(groups, 24, 128), near_shape], near_slots(table))
    sent, *faces = after(sent, *faces)
    slots = far_slots(sent, 0)
    flow, cond = call(
        first_flow_kernel, [block, (4,) + block],
        right, mob, diag, off, *low_halos(faces), *high_halos(faces),
    )
    w1, table, inverse, extra, cond_along, *faces = call(
        second_kernel,
        [block, (24, 128), (8, 128), (32, 128), (2,) + block] + face_shapes(1),
        slots, near, flow, right, mob, *perfs,
    )

    sent, near = call(near_kernel, [(groups, 17, 1, 128), near_shape], near_slots(copies(table)))
    sent, *faces = after(sent, *faces)
    slots = far_slots(sent, 1)
    flow = call(
        flow_kernel, [block], w1, diag, off, cond, *low_halos(faces), *high_halos(faces)
    )[0]
    w2, table, *faces = call(
        third_kernel, [block, (24, 128)] + face_shapes(1),
        slots, near, flow, w1, extra, inverse, cond_along, *perfs,
    )

    low = low_halos(faces)
    table = call(
        moment_kernel, [(24, 128)],
        table, right, w1, w2, extra, diag, off, cond, cond_along, *low,
    )[0]
    sent, near = call(last_near_kernel, [(groups, 20, 1, 128), near_shape], near_slots(copies(table)))
    sent, *faces = after(sent, *faces)
    slots = far_slots(sent, 2)
    high = high_halos(faces)
    flow = call(flow_kernel, [block], w2, diag, off, cond, *low, *high)[0]
    slots, flow = after(slots, flow)

    count = lax.axis_size("gx") * lax.axis_size("gy")
    sent = call(scalar_kernel, [(count, 1, 128)], slots, inverse)[0]
    order = [[(k + count // 2 + lax.axis_size("gy") // 2) % count for k in range(count)]]
    lines = lax.all_to_all(sent, ("gx", "gy"), 0, 0, axis_index_groups=order)
    solved, rest = call(
        combine_kernel, [block, block],
        lines, slots, near, flow, extra, inverse, cond_along, *perfs, right, w1, w2,
    )
    return solved.reshape(right_side.shape), rest.reshape(right_side.shape)


def solution(mesh):
    field = P(None, "gx", "gy", "gz")
    perf = P("gx", "gy", "gz")
    return jax.shard_map(
        body,
        mesh=mesh,
        in_specs=(field, field, field, field, perf, perf, perf),
        out_specs=(field, field),
        check_vma=False,
    )
```

```python
import jax
import jax.numpy as jnp
from jax import lax
from jax.experimental import pallas as pl
from jax.experimental.pallas import tpu as pltpu
from jax.sharding import PartitionSpec as P

W_COL = 640
WELL_ROWS = W_COL // 128
SHIFT = 8.0
F32 = jnp.float32
BF16 = jnp.bfloat16


def split3(a):
    first = a.astype(BF16)
    rest = a - first.astype(F32)
    second = rest.astype(BF16)
    third = (rest - second.astype(F32)).astype(BF16)
    return [first, second, third]


def sum3(a, rows):
    return a[:rows] + a[rows : 2 * rows] + a[2 * rows : 3 * rows]


def one_hot(index, rows):
    ids = lax.broadcasted_iota(jnp.int32, (rows, index.shape[1]), 0)
    return ids == index


def cell_masks(cell):
    row = one_hot(lax.shift_right_logical(cell, 7), 32).astype(F32)
    lane = one_hot(lax.bitwise_and(cell, 127), 128).astype(F32).astype(BF16)
    return row, lane


def well_mask(well):
    return one_hot(well, W_COL).astype(F32).astype(BF16)


def gather_cells(fields, row, lane):
    parts = [part for field in fields for part in split3(field)]
    picked = jnp.dot(jnp.concatenate(parts, 0), lane, preferred_element_type=F32)
    out = []
    for u in range(len(fields)):
        block = sum3(picked[96 * u : 96 * (u + 1)], 32)
        out.append(jnp.sum(block * row, axis=0, keepdims=True))
    return out


def scatter_cells(values, row, lane):
    parts = [part for value in values for part in split3(row * value)]
    placed = lax.dot_general(
        jnp.concatenate(parts, 0), lane, (((1,), (1,)), ((), ())), preferred_element_type=F32
    )
    return [sum3(placed[96 * u : 96 * (u + 1)], 32) for u in range(len(values))]


def scatter_wells(values, wells):
    count = len(values)
    stacked = jnp.concatenate(values + [jnp.zeros_like(values[0])] * (8 - count), 0)
    sums = lax.dot_general(
        jnp.concatenate(split3(stacked), 0), wells, (((1,), (1,)), ((), ())),
        preferred_element_type=F32,
    )
    sums = sum3(sums, 8)
    return [sums[u : u + 1] for u in range(count)]


def gather_wells(rows, wells):
    count = len(rows)
    stacked = jnp.concatenate(rows + [jnp.zeros_like(rows[0])] * (8 - count), 0)
    picked = sum3(jnp.dot(jnp.concatenate(split3(stacked), 0), wells, preferred_element_type=F32), 8)
    return [picked[u : u + 1] for u in range(count)]


def put_well_rows(ref, rows):
    for u, row in enumerate(rows):
        for j in range(WELL_ROWS):
            ref[u * WELL_ROWS + j : u * WELL_ROWS + j + 1, :] = row[:, 128 * j : 128 * (j + 1)]


def get_well_rows(table, count):
    out = []
    for u in range(count):
        pieces = [table[u * WELL_ROWS + j : u * WELL_ROWS + j + 1] for j in range(WELL_ROWS)]
        out.append(jnp.concatenate(pieces, 1))
    return out


def lanes():
    return lax.broadcasted_iota(jnp.int32, (8, 128), 1)


def put_faces(refs, fields):
    gx_high, gx_low, gy_high, gy_low = refs
    for k, field in enumerate(fields):
        for u in range(3):
            gx_high[3 * k + u] = field[u, 24:32]
            gx_low[3 * k + u] = field[u, 0:8]
            for x in range(4):
                at = 12 * k + 4 * u + x
                gy_high[at : at + 1] = field[u, 8 * x + 7 : 8 * x + 8]
                gy_low[at : at + 1] = field[u, 8 * x : 8 * x + 1]


def end_tile(highs, lows):
    lane = lanes()
    tile = jnp.zeros((8, 128), F32)
    for fields, turn in ((highs, 1), (lows, 0)):
        for field, start in fields:
            for u in range(3):
                for x in range(4):
                    at = start + 4 * u + x
                    value = pltpu.roll(field[u, 8 * x : 8 * x + 8], at + turn, 1)
                    tile = jnp.where(lane == at, value, tile)
    return tile


def fold(tile):
    return jnp.where(lanes()[0:4] < 64, tile[0:4], pltpu.roll(tile, 64, 1)[4:8])


def unfold(rows):
    return jnp.concatenate([rows, pltpu.roll(jnp.concatenate([rows, rows], 0), 64, 1)[0:4]], 0)


def fold_narrow(tile):
    kept = jnp.where(lanes() < 32, tile, 0.0)
    turned = [kept[0:2]] + [pltpu.roll(kept, 32 * k, 1)[2 * k : 2 * k + 2] for k in (1, 2, 3)]
    return tree(turned)


def unfold_narrow(rows):
    sub = lax.broadcasted_iota(jnp.int32, (8, 128), 0)
    spread = jnp.concatenate(rows * 4, 0)
    tile = spread
    for k in (1, 2, 3):
        tile = jnp.where(sub >= 2 * k, pltpu.roll(spread, 128 - 32 * k, 1), tile)
    return tile


def slot_rows(slots, first, last):
    return [tree([slots[k, r] for k in range(slots.shape[0])]) for r in range(first, last)]


def well_rows(rows):
    return [
        jnp.concatenate(rows[u * WELL_ROWS : (u + 1) * WELL_ROWS], 1) for u in range(3)
    ]


def narrow_tile(slots):
    return lambda k: unfold_narrow([slots[k, 15], slots[k, 16]])


def wide_tile(slots):
    return lambda k: unfold(jnp.concatenate([slots[k, r] for r in range(16, 20)], 0))


def low_views(field, k, u, x, halo, sub):
    gx_low, gy_low = halo
    value = field[u, 8 * x : 8 * x + 8]
    view_x = field[u, 8 * x - 8 : 8 * x] if x else gx_low[3 * k + u]
    at = 12 * k + 4 * u + x
    edge = jnp.broadcast_to(gy_low[at : at + 1], (8, 128))
    return [view_x, jnp.where(sub == 0, edge, pltpu.roll(value, 1, 0))]


def high_views(field, k, u, x, halo, sub):
    gx_high, gy_high = halo
    value = field[u, 8 * x : 8 * x + 8]
    view_x = field[u, 8 * x + 8 : 8 * x + 16] if x < 3 else gx_high[3 * k + u]
    at = 12 * k + 4 * u + x
    edge = jnp.broadcast_to(gy_high[at : at + 1], (8, 128))
    return [view_x, jnp.where(sub == 7, edge, pltpu.roll(value, 7, 0))]


def low_along(value, tile, at, lane):
    return jnp.where(lane == 0, pltpu.roll(tile, (128 - at) % 128, 1), pltpu.roll(value, 1, 1))


def high_along(value, tile, at, lane):
    return jnp.where(lane == 127, pltpu.roll(tile, 127 - at, 1), pltpu.roll(value, 127, 1))


def place():
    at = lax.axis_index("gz")
    return lax.div(at, NEAR), lax.rem(at, NEAR)


FIRST = (5, 3, 4)


def slot_of(group, count, step):
    return (group + count - FIRST[step] % count) % count


def near_tiles(tiles):
    _, member = place()
    low, high = tiles[0], tiles[-1]
    for k in range(1, NEAR - 1):
        low = jnp.where(member == k + 1, tiles[k], low)
        high = jnp.where(member == k - 1, tiles[k], high)
    return low, high


def halo_tiles(near, slots, read, step):
    group, member = place()
    last = slots.shape[0] - 1
    below = jnp.where(group == 0, 0.0, read(slot_of(jnp.maximum(group - 1, 0), last + 1, step)))
    above = jnp.where(
        group == last, 0.0, read(slot_of(jnp.minimum(group + 1, last), last + 1, step))
    )
    return jnp.where(member == 0, below, near[0]), jnp.where(member == NEAR - 1, above, near[1])


def block_row(field, diag, off, u, rows):
    pick = ((None, 0, 1), (0, None, 2), (1, 2, None))[u]
    total = (diag[u, rows] - SHIFT) * field[u, rows]
    for t in range(3):
        if pick[t] is not None:
            total = total + off[pick[t], rows] * field[t, rows]
    return total


def first_kernel(right_any, mobility_any, cell_any, well_any, factor_any, table, *rest):
    faces, (right, mobility, cell, well, factor, sems) = rest[:4], rest[4:]
    copies = [
        pltpu.make_async_copy(source, target, sems.at[k])
        for k, (source, target) in enumerate(
            (
                (cell_any, cell),
                (right_any, right),
                (factor_any, factor),
                (well_any, well),
                (mobility_any, mobility),
            )
        )
    ]
    for copy in copies:
        copy.start()
    copies[0].wait()
    row, lane = cell_masks(cell[0])
    copies[3].wait()
    wells = well_mask(well[0])
    copies[1].wait()
    values = gather_cells([right[u] for u in range(3)], row, lane)
    copies[2].wait()
    weight = factor[0]
    sums = scatter_wells([weight * v for v in values] + [weight], wells)
    copies[4].wait()
    ends = fold(end_tile([(right, 0), (mobility, 32)], [(right, 16), (mobility, 48)]))
    for k in range(NEAR):
        put_well_rows(table.at[k], sums)
        table[k, 4 * WELL_ROWS : 24] = ends
    put_faces(faces, [right, mobility])


def first_near_kernel(slots, sent, near):
    rows = 4 * WELL_ROWS
    total = jnp.sum(slots[...], axis=0)
    tiles = [unfold(slots[k, rows:24]) for k in range(NEAR)]
    low, high = near_tiles(tiles)
    near[0], near[1] = low, high
    lane = lanes()
    ends = fold(jnp.where(lax.bitwise_and(lane, 31) < 16, tiles[-1], tiles[0]))
    for k in range(sent.shape[0]):
        sent[k, 0:rows] = total[0:rows]
        sent[k, rows:24] = ends


def near_kernel(slots, sent, near):
    total = jnp.sum(slots[...], axis=0)
    tiles = [slots[k, 16:24] for k in range(NEAR)]
    low, high = near_tiles(tiles)
    near[0], near[1] = low, high
    ends = jnp.where(lanes() < 16, tiles[-1], tiles[0])
    ends = fold_narrow(ends)
    for k in range(sent.shape[0]):
        for r in range(15):
            sent[k, r] = total[r : r + 1]
        for r in range(2):
            sent[k, 15 + r] = ends[r : r + 1]


def face_energy(below, above):
    step = pltpu.roll(above, 112, 1) - below
    return jnp.where(lanes() < 12, pltpu.roll(above, 96, 1) * step * step, 0.0)


def whole_sum(a):
    return jnp.sum(jnp.sum(a, axis=0, keepdims=True), axis=1, keepdims=True)


def last_near_kernel(slots, sent, near):
    total = jnp.sum(slots[...], axis=0)
    tiles = [slots[k, 16:24] for k in range(NEAR)]
    low, high = near_tiles(tiles)
    near[0], near[1] = low, high
    between = whole_sum(tree([face_energy(a, b) for a, b in zip(tiles, tiles[1:])]))
    line = total[15:16] + jnp.where(lanes()[0:1] == 5, between, 0.0)
    ends = jnp.where(lanes() < 16, tiles[-1], tiles[0])
    ends = fold(ends)
    for k in range(sent.shape[0]):
        for r in range(15):
            sent[k, r] = total[r : r + 1]
        sent[k, 15] = line
        for r in range(4):
            sent[k, 16 + r] = ends[r : r + 1]


def first_flow_kernel(right, mobility, diag, off, xl, yl, xh, yh, flow, cond):
    sub = lax.broadcasted_iota(jnp.int32, (8, 128), 0)
    for u in range(3):
        for x in range(4):
            rows = slice(8 * x, 8 * x + 8)
            total = block_row(right, diag, off, u, rows)
            value, own = right[u, rows], mobility[u, rows]
            near = low_views(right, 0, u, x, (xl, yl), sub)
            near += high_views(right, 0, u, x, (xh, yh), sub)
            near_mob = low_views(mobility, 1, u, x, (xl, yl), sub)
            near_mob += high_views(mobility, 1, u, x, (xh, yh), sub)
            for d in range(4):
                weight = 2.0 * own * near_mob[d] / (own + near_mob[d])
                cond[d, u, rows] = weight
                total = total + weight * (value - near[d])
            flow[u, rows] = total


def flow_kernel(field, diag, off, cond, xl, yl, xh, yh, flow):
    sub = lax.broadcasted_iota(jnp.int32, (8, 128), 0)
    for u in range(3):
        for x in range(4):
            rows = slice(8 * x, 8 * x + 8)
            total = block_row(field, diag, off, u, rows)
            value = field[u, rows]
            near = low_views(field, 0, u, x, (xl, yl), sub)
            near += high_views(field, 0, u, x, (xh, yh), sub)
            for d in range(4):
                total = total + cond[d, u, rows] * (value - near[d])
            flow[u, rows] = total


def flow_along(field, flow, cond, low, high):
    lane = lanes()
    out = []
    for u in range(3):
        blocks = []
        for x in range(4):
            rows = slice(8 * x, 8 * x + 8)
            value = field[u, rows]
            step_low = value - low_along(value, low, 4 * u + x, lane)
            step_high = value - high_along(value, high, 16 + 4 * u + x, lane)
            total = flow[u, rows] + cond[0, u, rows] * step_low
            blocks.append(total + cond[1, u, rows] * step_high)
        out.append(jnp.concatenate(blocks, 0))
    return out


def put_cond_along(cond, mobility, low, high):
    lane = lanes()
    for u in range(3):
        for x in range(4):
            rows = slice(8 * x, 8 * x + 8)
            own = mobility[u, rows]
            near = low_along(own, low, 32 + 4 * u + x, lane)
            cond[0, u, rows] = 2.0 * own * near / (own + near)
            near = high_along(own, high, 48 + 4 * u + x, lane)
            cond[1, u, rows] = 2.0 * own * near / (own + near)


def advance(means, flow, field, extra, weight, row, lane, wells):
    picked = gather_wells(means, wells)
    pulled = scatter_cells([weight * m for m in picked], row, lane)
    return [flow[u] + extra * field[u] - pulled[u] for u in range(3)]


def second_kernel(
    slots, near, flow, right, mobility, cell, well, factor,
    field, table, inverse, extra, cond, *faces
):
    total = jnp.sum(slots[...], axis=0)
    low, high = halo_tiles(near, slots, lambda k: unfold(slots[k, 4 * WELL_ROWS : 24]), 0)
    put_cond_along(cond, mobility, low, high)
    whole = flow_along(right, flow, cond, low, high)
    scale = 1.0 / (1.0 + total[3 * WELL_ROWS : 4 * WELL_ROWS])
    inverse[...] = jnp.zeros((8, 128), F32)
    inverse[0:WELL_ROWS] = scale
    rows = get_well_rows(total[: 3 * WELL_ROWS], 3)
    scale_row = get_well_rows(scale, 1)[0]
    row, lane = cell_masks(cell[0])
    wells = well_mask(well[0])
    weight = factor[0]
    own = scatter_cells([weight], row, lane)[0]
    extra[...] = own
    fresh = advance([r * scale_row for r in rows], whole, right, own, weight, row, lane, wells)
    for u in range(3):
        field[u] = fresh[u]
    values = gather_cells(fresh, row, lane)
    put_well_rows(table, scatter_wells([weight * v for v in values], wells))
    table[15:16] = jnp.zeros((1, 128), F32)
    table[16:24] = end_tile([(field, 0)], [(field, 16)])
    put_faces(faces, [field])


def third_kernel(
    slots, near, flow, before, extra, inverse, cond, cell, well, factor, field, table, *faces
):
    low, high = halo_tiles(near, slots, narrow_tile(slots), 1)
    whole = flow_along(before, flow, cond, low, high)
    scale_row = get_well_rows(inverse[...], 1)[0]
    rows = well_rows(slot_rows(slots, 0, 15))
    row, lane = cell_masks(cell[0])
    wells = well_mask(well[0])
    weight = factor[0]
    fresh = advance([r * scale_row for r in rows], whole, before, extra[...], weight, row, lane, wells)
    for u in range(3):
        field[u] = fresh[u]
    values = gather_cells(fresh, row, lane)
    put_well_rows(table, scatter_wells([weight * v for v in values], wells))
    table[15:16] = jnp.zeros((1, 128), F32)
    table[16:24] = end_tile([(field, 0)], [(field, 16), (cond.at[0], 32)])
    put_faces(faces, [field])


def tree(terms):
    while len(terms) > 1:
        pairs = [a + b for a, b in zip(terms[::2], terms[1::2])]
        terms = pairs + ([terms[-1]] if len(terms) % 2 else [])
    return terms[0]


def moment_kernel(wells_table, w0, w1, w2, extra, diag, off, cond, cond_along, xl, yl, table):
    lane, sub = lanes(), lax.broadcasted_iota(jnp.int32, (8, 128), 0)
    sums = [[] for _ in range(6)]
    for u in range(3):
        for x in range(4):
            rows = slice(8 * x, 8 * x + 8)
            a, b, c = w0[u, rows], w1[u, rows], w2[u, rows]
            for k, (p, q) in enumerate(((a, a), (a, b), (b, b), (b, c), (c, c))):
                sums[k].append(p * q)
            energy = c * (block_row(w2, diag, off, u, rows) + extra[rows] * c)
            for d, near in enumerate(low_views(w2, 0, u, x, (xl, yl), sub)):
                energy = energy + cond[d, u, rows] * (c - near) * (c - near)
            step = jnp.where(lane == 0, 0.0, c - pltpu.roll(c, 1, 1))
            sums[5].append(energy + cond_along[0, u, rows] * step * step)
    line = jnp.zeros((1, 128), F32)
    for k in range(6):
        line = jnp.where(lane[0:1] == k, whole_sum(tree(sums[k])), line)
    table[...] = wells_table[...]
    table[15:16] = line


def scalar_kernel(slots, inverse, sent):
    rows = slot_rows(slots, 0, 16)
    pull = tree([row * row * inverse[k % WELL_ROWS : k % WELL_ROWS + 1] for k, row in enumerate(rows[:15])])
    count = slots.shape[0]
    tiles = [wide_tile(slots)(slot_of(k, count, 2)) for k in range(count)]
    between = tree([face_energy(a, b) for a, b in zip(tiles, tiles[1:])])
    last = whole_sum(between) - whole_sum(pull)
    line = rows[15] + jnp.where(lanes()[0:1] == 5, last, 0.0)
    for k in range(sent.shape[0]):
        sent[k] = line


def plus(a, b, scale):
    size = max(len(a), len(b))
    out = []
    for k in range(size):
        p = a[k] if k < len(a) else None
        q = scale * b[k] if k < len(b) else None
        out.append(q if p is None else p if q is None else p + q)
    return out


def image_of(a):
    raised = [None] + list(a)
    return [
        SHIFT * a[0] if k == 0 else raised[k] + SHIFT * a[k] if k < len(a) else raised[k]
        for k in range(len(a) + 1)
    ]


def inner(a, b, moment):
    by_degree = {}
    for i, p in enumerate(a):
        for j, q in enumerate(b):
            by_degree[i + j] = by_degree.get(i + j, 0.0) + p * q
    return tree([by_degree[k] * moment[k] for k in sorted(by_degree)])


def combine_kernel(
    lines, slots, near, flow, extra, inverse, cond, cell, well, factor, w0, w1, w2, solved, rest
):
    low, high = halo_tiles(near, slots, wide_tile(slots), 2)
    whole = flow_along(w2, flow, cond, low, high)
    scale_row = get_well_rows(inverse[...], 1)[0]
    means = [r * scale_row for r in well_rows(slot_rows(slots, 0, 15))]
    row, lane = cell_masks(cell[0])
    w3 = advance(means, whole, w2, extra[...], factor[0], row, lane, well_mask(well[0]))

    line = tree([lines[k] for k in range(lines.shape[0])])
    first = lanes()[0:1]
    moment = [
        jnp.broadcast_to(jnp.sum(jnp.where(first == k, line, 0.0), axis=1, keepdims=True), (1, 128))
        for k in range(6)
    ]
    one = jnp.ones((1, 128), F32)
    residual, direction, solution_field = [one], [one], []
    norm = moment[0]
    for step in range(3):
        image = image_of(direction)
        alpha = norm / inner(direction, image, moment)
        solution_field = plus(solution_field, direction, alpha)
        residual = plus(residual, image, -alpha)
        if step < 2:
            fresh = inner(residual, residual, moment)
            direction = plus(residual, direction, fresh / norm)
            norm = fresh
    solution_field = [jnp.broadcast_to(c, (8, 128)) for c in solution_field]
    residual = [jnp.broadcast_to(c, (8, 128)) for c in residual]
    for u in range(3):
        for x in range(4):
            rows = slice(8 * x, 8 * x + 8)
            basis = [w0[u, rows], w1[u, rows], w2[u, rows], w3[u][rows]]
            solved[u, rows] = tree([c * w for c, w in zip(solution_field, basis)])
            rest[u, rows] = tree([c * w for c, w in zip(residual, basis)])


def call(kernel, shapes, *args, space=pltpu.VMEM, scratch=(), mib=32):
    return pl.pallas_call(
        kernel,
        out_shape=[jax.ShapeDtypeStruct(shape, F32) for shape in shapes],
        in_specs=[pl.BlockSpec(memory_space=space)] * len(args),
        out_specs=[pl.BlockSpec(memory_space=pltpu.VMEM)] * len(shapes),
        scratch_shapes=list(scratch),
        compiler_params=pltpu.CompilerParams(vmem_limit_bytes=mib * 1024 * 1024),
    )(*args)


NEAR = 4


def near_slots(sent):
    count = lax.axis_size("gz")
    groups = [[NEAR * g + k for k in range(NEAR)] for g in range(count // NEAR)]
    return lax.all_to_all(sent, "gz", 0, 0, axis_index_groups=groups)


def copies(table):
    return jnp.broadcast_to(table[None], (NEAR,) + table.shape)


def far_slots(sent, step):
    count = lax.axis_size("gz")
    slots = count // NEAR
    order = sorted(range(slots), key=lambda group: slot_of(group, slots, step))
    groups = [[g + NEAR * k for k in order] for g in range(NEAR)]
    return lax.all_to_all(sent, "gz", 0, 0, axis_index_groups=groups)


def forward(piece, axis):
    count = lax.axis_size(axis)
    return lax.ppermute(piece, axis, [(i, i + 1) for i in range(count - 1)])


def backward(piece, axis):
    count = lax.axis_size(axis)
    return lax.ppermute(piece, axis, [(i + 1, i) for i in range(count - 1)])


def low_halos(faces):
    return [forward(faces[0], "gx"), forward(faces[2], "gy")]


def high_halos(faces):
    return [backward(faces[1], "gx"), backward(faces[3], "gy")]


def after(first, *later):
    return lax.optimization_barrier((first, *later))


def face_shapes(fields):
    return [(3 * fields, 8, 128)] * 2 + [(12 * fields, 128)] * 2


def body(right_side, block_diag, block_off, mobility, perf_cell, perf_well, perf_factor):
    block = (3, 32, 128)
    right, diag, off, mob = (
        a.reshape(block) for a in (right_side, block_diag, block_off, mobility)
    )
    perfs = (perf_cell, perf_well, perf_factor)
    groups = lax.axis_size("gz") // NEAR
    near_shape = (2, 8, 128)

    table, *faces = call(
        first_kernel, [(NEAR, 24, 128)] + face_shapes(2), right, mob, *perfs,
        space=pltpu.HBM, mib=60,
        scratch=[pltpu.VMEM(block, F32)] * 2
        + [pltpu.VMEM(a.shape, a.dtype) for a in perfs]
        + [pltpu.SemaphoreType.DMA((5,))],
    )
    sent, near = call(first_near_kernel, [(groups, 24, 128), near_shape], near_slots(table))
    sent, *faces = after(sent, *faces)
    slots = far_slots(sent, 0)
    flow, cond = call(
        first_flow_kernel, [block, (4,) + block],
        right, mob, diag, off, *low_halos(faces), *high_halos(faces),
    )
    w1, table, inverse, extra, cond_along, *faces = call(
        second_kernel,
        [block, (24, 128), (8, 128), (32, 128), (2,) + block] + face_shapes(1),
        slots, near, flow, right, mob, *perfs,
    )

    sent, near = call(near_kernel, [(groups, 17, 1, 128), near_shape], near_slots(copies(table)))
    sent, *faces = after(sent, *faces)
    slots = far_slots(sent, 1)
    flow = call(
        flow_kernel, [block], w1, diag, off, cond, *low_halos(faces), *high_halos(faces)
    )[0]
    w2, table, *faces = call(
        third_kernel, [block, (24, 128)] + face_shapes(1),
        slots, near, flow, w1, extra, inverse, cond_along, *perfs,
    )

    low = low_halos(faces)
    table = call(
        moment_kernel, [(24, 128)],
        table, right, w1, w2, extra, diag, off, cond, cond_along, *low,
    )[0]
    sent, near = call(last_near_kernel, [(groups, 20, 1, 128), near_shape], near_slots(copies(table)))
    sent, *faces = after(sent, *faces)
    slots = far_slots(sent, 2)
    high = high_halos(faces)
    flow = call(flow_kernel, [block], w2, diag, off, cond, *low, *high)[0]
    slots, flow = after(slots, flow)

    count = lax.axis_size("gx") * lax.axis_size("gy")
    sent = call(scalar_kernel, [(count, 1, 128)], slots, inverse)[0]
    order = [[(k + count // 2 + lax.axis_size("gy") // 2) % count for k in range(count)]]
    lines = lax.all_to_all(sent, ("gx", "gy"), 0, 0, axis_index_groups=order)
    solved, rest = call(
        combine_kernel, [block, block],
        lines, slots, near, flow, extra, inverse, cond_along, *perfs, right, w1, w2,
    )
    return solved.reshape(right_side.shape), rest.reshape(right_side.shape)


def solution(mesh):
    field = P(None, "gx", "gy", "gz")
    perf = P("gx", "gy", "gz")
    return jax.shard_map(
        body,
        mesh=mesh,
        in_specs=(field, field, field, field, perf, perf, perf),
        out_specs=(field, field),
        check_vma=False,
    )
```
